32 devices in a mesh: section: 4 (over y, x), dp: 8 (over z, core).
Axes of the slice: x: 2, y: 2, z: 4, core: 2. Of those that a mesh axis runs over, the one named last changes fastest.
Arguments:
- stream_in: bfloat16 [2, 512, 3584], P(None, 'dp'), may hold values from -6 to 6
- cotangent: bfloat16 [2, 512, 3584], P(None, 'dp'), may hold values from -6 to 6
- norm_gain: bfloat16 [4, 3584], P('section'), may hold values from 0.1 to 3.5
- weight_in: bfloat16 [4, 3584, 128], P('section', 'dp'), may hold values from -0.09375 to 0.09375
- weight_out: bfloat16 [4, 128, 3584], P('section', 'dp'), may hold values from -0.5 to 0.5
- moment_in: float32 [4, 3584, 128], P('section', 'dp'), may hold values from -3 to 3
- variance_in: float32 [4, 3584, 128], P('section', 'dp'), may hold values from 0.05 to 2
- moment_out: float32 [4, 128, 3584], P('section', 'dp'), may hold values from -3 to 3
- variance_out: float32 [4, 128, 3584], P('section', 'dp'), may hold values from 0.05 to 2
Outputs:
- weight_in_next: float32 [4, 3584, 128], P('section', 'dp')
- moment_in_next: float32 [4, 3584, 128], P('section', 'dp')
- variance_in_next: float32 [4, 3584, 128], P('section', 'dp')
- weight_out_next: float32 [4, 128, 3584], P('section', 'dp')
- moment_out_next: float32 [4, 128, 3584], P('section', 'dp')
- variance_out_next: float32 [4, 128, 3584], P('section', 'dp')
The draws below stay inside these ranges and needn't reach their ends.
All inputs are finite; a program needn't handle non-finite values.
Results may differ from the reference program's by a relative error of at most 0.02.
Values may be sent and summed in bfloat16 or wider, within the bound.
A program may use at most 64 MiB of HBM per device.

```python
import math
import jax
import jax.numpy as jnp
from jax import lax

E = 3584
R = 128
MICRO = 2
TOK_DEV = 64
SECTIONS = 4
TOKENS = 512
N_DP = 8


def draw_norm_gain(key, part):
    section_ramp = 0.5 + jnp.arange(SECTIONS, dtype=jnp.float32)[:, None] / max(SECTIONS - 1, 1)
    channel_ramp = 0.5 + jnp.arange(E, dtype=jnp.float32)[None, :] / E
    jitter = jax.random.uniform(key, (SECTIONS, E), jnp.float32, 0.7, 1.3)
    return (section_ramp * channel_ramp * jitter).astype(jnp.bfloat16)


def raised(drawn, rng, source, target, parts, factor):
    owner, partner = [(jnp.arange(drawn.shape[axis_at]) // (drawn.shape[axis_at] // parts)).reshape([-1 if axis == axis_at else 1 for axis in range(drawn.ndim)]) for axis_at in (source, target)]
    chosen = jax.random.permutation(rng, parts)[partner]
    strong = (owner == chosen) | (owner == (partner + parts // 2) % parts)
    return jnp.where(strong, factor * drawn, drawn)


def block_scale(rng, shape, cuts, low, largest):
    loudness = 1.0
    for axis_at, parts in cuts:
        heights = jax.random.uniform(jax.random.fold_in(jax.random.fold_in(rng, 6), axis_at), (parts,), jnp.float32, low / len(cuts), largest / len(cuts))
        loudness = loudness * jnp.repeat(jnp.exp(heights), shape[axis_at] // parts).reshape((-1,) + (1,) * (len(shape) - 1 - axis_at))
    return loudness


def centred(rng, shape, deviation, reach, split=(), kind=jnp.bfloat16):
    entries = deviation * jax.random.normal(rng, shape, jnp.float32)
    if split:
        entries = entries * block_scale(rng, shape, split, -0.22, 0.18)
    return jnp.clip(entries, -reach, reach).astype(kind)


def bell_draw_with(rng, dims, scale, limit, split, heavy, held_as=jnp.bfloat16):
    array = scale * jax.random.normal(rng, dims, jnp.float32)
    if split:
        array = array * block_scale(rng, dims, split, -0.22, 0.18)
    return jnp.clip(raised(array, jax.random.fold_in(rng, 3), *heavy), -limit, limit).astype(held_as)


def setup_inputs(seed: int = 0) -> dict:
    seeds = jax.random.split(jax.random.key(seed), 10)
    stream_in = bell_draw_with(seeds[0], (MICRO, TOKENS, E), 1.0, 6.0, ((1, 8),), (1, 2, 8, 2.0))
    cotangent = centred(seeds[1], (MICRO, TOKENS, E), 1.0, 6.0, ((1, 8),))
    norm_gain = draw_norm_gain(jax.random.fold_in(seeds[9], 71), 0)
    weight_in = centred(seeds[3], (SECTIONS, E, R), E ** -0.5, 0.09375, ((0, 4), (1, 8)))
    weight_out = centred(seeds[4], (SECTIONS, R, E), R ** -0.5, 0.5, ((0, 4), (1, 8)))
    moment_in = centred(seeds[5], (SECTIONS, E, R), 0.5, 3.0, ((0, 4), (1, 8)), jnp.float32)
    variance_in = jnp.clip(jnp.exp(math.log(2.0) - 3.6888794 * jax.random.uniform(seeds[6], (SECTIONS, E, R), jnp.float32) ** block_scale(seeds[6], (SECTIONS, E, R), ((0, 4), (1, 8)), -0.2, 0.2)), 0.05, 2.0)
    moment_out = centred(seeds[7], (SECTIONS, R, E), 0.5, 3.0, ((0, 4), (1, 8)), jnp.float32)
    variance_out = jnp.clip(jnp.exp(math.log(2.0) - 3.6888794 * jax.random.uniform(seeds[8], (SECTIONS, R, E), jnp.float32) ** block_scale(seeds[8], (SECTIONS, R, E), ((0, 4), (1, 8)), -0.2, 0.2)), 0.05, 2.0)
    return {"stream_in": stream_in, "cotangent": cotangent, "norm_gain": norm_gain, "weight_in": weight_in, "weight_out": weight_out, "moment_in": moment_in, "variance_in": variance_in, "moment_out": moment_out, "variance_out": variance_out}


NORM_EPS = 1e-06
BETA_ONE = 0.9
BETA_TWO = 0.95
STEP_RATE = 0.01
ADAM_EPS = 1e-08
CLIP_EPS = 1e-06

def normalize(stream, gain):
    values = stream.astype(jnp.float32)
    inv_root = lax.rsqrt(lax.optimization_barrier(jnp.mean(values * values, axis=-1, keepdims=True)) + NORM_EPS)
    unit_rows = values * inv_root
    normed = (unit_rows * gain.astype(jnp.float32)).astype(jnp.bfloat16)
    return (values, inv_root, unit_rows, normed)

def section_forward(stream, gain, in_weight, out_weight):
    values, inv_root, unit_rows, normed = normalize(stream, gain)
    pre_act = jnp.dot(normed, in_weight, preferred_element_type=jnp.float32)
    hidden = (pre_act * jax.nn.sigmoid(pre_act)).astype(jnp.bfloat16)
    return (values + jnp.dot(hidden, out_weight, preferred_element_type=jnp.float32)).astype(jnp.bfloat16)

def section_backward(stream, grad_rows, gain, in_weight, out_weight):
    values, inv_root, unit_rows, normed = normalize(stream, gain)
    pre_act = jnp.dot(normed, in_weight, preferred_element_type=jnp.float32)
    squash = jax.nn.sigmoid(pre_act)
    hidden = (pre_act * squash).astype(jnp.bfloat16)
    grad_hidden = lax.dot_general(grad_rows, out_weight, (((1,), (1,)), ((), ())), preferred_element_type=jnp.float32)
    grad_act = (grad_hidden * squash * (1.0 + pre_act * (1.0 - squash))).astype(jnp.bfloat16)
    grad_normed = lax.dot_general(grad_act, in_weight, (((1,), (1,)), ((), ())), preferred_element_type=jnp.float32) * gain.astype(jnp.float32)
    inner_mean = lax.optimization_barrier(jnp.mean(grad_normed * unit_rows, axis=-1, keepdims=True))
    grad_in = (grad_rows.astype(jnp.float32) + inv_root * (grad_normed - unit_rows * inner_mean)).astype(jnp.bfloat16)
    return (grad_in, normed, grad_act, hidden)

def grouped(left, right):
    left_width = left.shape[-1]
    right_width = right.shape[-1]
    left = left.reshape(2, MICRO // 2, N_DP, TOK_DEV, left_width).transpose(0, 2, 1, 3, 4)
    left = left.reshape(2 * N_DP, MICRO // 2 * TOK_DEV, left_width)
    right = right.reshape(2, MICRO // 2, N_DP, TOK_DEV, right_width).transpose(0, 2, 1, 3, 4)
    right = right.reshape(2 * N_DP, MICRO // 2 * TOK_DEV, right_width)

    def add_part(running, pair):
        part = lax.dot_general(pair[0], pair[1], (((0,), (0,)), ((), ())), preferred_element_type=jnp.float32)
        rounded = lax.optimization_barrier(part.astype(jnp.bfloat16))
        return (running + rounded.astype(jnp.float32), None)
    running, _ = lax.scan(add_part, jnp.zeros((left_width, right_width), jnp.float32), (left, right))
    return running

def update(weight, grad, moment, variance, factor):
    scaled = factor * grad
    moment = BETA_ONE * moment + (1.0 - BETA_ONE) * scaled
    variance = BETA_TWO * variance + (1.0 - BETA_TWO) * scaled * scaled
    weight = weight.astype(jnp.float32) - STEP_RATE * moment / (jnp.sqrt(variance) + ADAM_EPS)
    return (weight, moment, variance)

def reference(stream_in, cotangent, norm_gain, weight_in, weight_out, moment_in, variance_in, moment_out, variance_out):
    all_rows = stream_in.reshape(-1, E)
    all_grads = cotangent.reshape(-1, E)

    def forward(stream, layer_params):
        gain, in_weight, out_weight = layer_params
        return (section_forward(stream, gain, in_weight, out_weight), stream)
    _, saved_rows = lax.scan(forward, all_rows, (norm_gain, weight_in, weight_out))

    def backward(grad_rows, layer_params):
        stream, gain, in_weight, out_weight = layer_params
        grad_in, normed, grad_act, hidden = section_backward(stream, grad_rows, gain, in_weight, out_weight)
        return (grad_in, (grouped(normed, grad_act), grouped(hidden, grad_rows)))
    _, (grad_w_in, grad_w_out) = lax.scan(backward, all_grads, (saved_rows, norm_gain, weight_in, weight_out), reverse=True)
    norm_total = jnp.sum(grad_w_in * grad_w_in) + jnp.sum(grad_w_out * grad_w_out)
    count_all = 2.0 * SECTIONS * E * R
    factor = jnp.minimum(1.0, lax.rsqrt(norm_total / count_all + CLIP_EPS))
    new_in, new_moment_in, new_variance_in = update(weight_in, grad_w_in, moment_in, variance_in, factor)
    new_out, new_moment_out, new_variance_out = update(weight_out, grad_w_out, moment_out, variance_out, factor)
    return (new_in, new_moment_in, new_variance_in, new_out, new_moment_out, new_variance_out)
```

```python
import functools

import jax
import jax.numpy as jnp
from jax import lax
from jax.experimental import pallas as pl
from jax.experimental.pallas import tpu as pltpu
from jax.sharding import PartitionSpec as P

E = 3584
R = 128


NORM_EPS = 1e-06
BETA_ONE = 0.9
BETA_TWO = 0.95
STEP_RATE = 0.01
ADAM_EPS = 1e-08
CLIP_EPS = 1e-06


def from_behind(x, axis, by):
    count = lax.axis_size(axis)
    pairs = [(i, i + by) for i in range(count) if 0 <= i + by < count]
    return lax.ppermute(x, axis, pairs)


def normalize(stream, gain):
    values = stream.astype(jnp.float32)
    inv_root = lax.rsqrt(jnp.mean(values * values, axis=-1, keepdims=True) + NORM_EPS)
    unit_rows = values * inv_root
    normed = (unit_rows * gain.astype(jnp.float32)).astype(jnp.bfloat16)
    return (values, inv_root, unit_rows, normed)


def section_forward(stream, gain, in_weight, out_weight):
    values, inv_root, unit_rows, normed = normalize(stream, gain)
    pre_act = jnp.dot(normed, in_weight, preferred_element_type=jnp.float32)
    hidden = (pre_act * jax.nn.sigmoid(pre_act)).astype(jnp.bfloat16)
    return (values + jnp.dot(hidden, out_weight, preferred_element_type=jnp.float32)).astype(
        jnp.bfloat16
    )


def section_backward(stream, grad_rows, gain, in_weight, out_weight):
    values, inv_root, unit_rows, normed = normalize(stream, gain)
    pre_act = jnp.dot(normed, in_weight, preferred_element_type=jnp.float32)
    squash = jax.nn.sigmoid(pre_act)
    hidden = (pre_act * squash).astype(jnp.bfloat16)
    grad_hidden = lax.dot_general(
        grad_rows, out_weight, (((1,), (1,)), ((), ())), preferred_element_type=jnp.float32
    )
    grad_act = (grad_hidden * squash * (1.0 + pre_act * (1.0 - squash))).astype(jnp.bfloat16)
    grad_normed = lax.dot_general(
        grad_act, in_weight, (((1,), (1,)), ((), ())), preferred_element_type=jnp.float32
    ) * gain.astype(jnp.float32)
    inner_mean = jnp.mean(grad_normed * unit_rows, axis=-1, keepdims=True)
    grad_in = (
        grad_rows.astype(jnp.float32) + inv_root * (grad_normed - unit_rows * inner_mean)
    ).astype(jnp.bfloat16)
    return (grad_in, normed, grad_act, hidden)


def contract_rows(left, right):
    return lax.dot_general(
        left, right, (((0,), (0,)), ((), ())), preferred_element_type=jnp.float32
    )


def forward_tick(step_tick, position, is_first, incoming, saved_rows, inputs, weights):
    batch_count = inputs.shape[0]
    chain_index = step_tick - position
    active = jnp.logical_and(chain_index >= 0, chain_index < batch_count)
    batch_slot = jnp.clip(chain_index, 0, batch_count - 1)
    stream = jnp.where(is_first, lax.dynamic_index_in_dim(inputs, batch_slot, 0, False), incoming)
    kept_row = jnp.where(active, stream, lax.dynamic_index_in_dim(saved_rows, batch_slot, 0, False))
    saved_rows = lax.dynamic_update_index_in_dim(saved_rows, kept_row, batch_slot, 0)
    section_out = lax.cond(
        active, lambda rows_in: section_forward(rows_in, *weights), jnp.zeros_like, stream
    )
    return (section_out, saved_rows)


def backward_tick(
    step_tick, position, is_last, incoming, saved_rows, targets, weights, grad_sums, groups
):
    batch_count = targets.shape[0]
    chain_index = step_tick - position
    active = jnp.logical_and(chain_index >= 0, chain_index < batch_count)
    batch_slot = jnp.clip(chain_index, 0, batch_count - 1)
    grad_rows = jnp.where(
        is_last, lax.dynamic_index_in_dim(targets, batch_slot, 0, False), incoming
    )
    stream = lax.dynamic_index_in_dim(saved_rows, batch_slot, 0, False)
    half_group = batch_slot * groups // batch_count

    def run_section(operands):
        rows_in, grad_now, sums_now = operands
        grad_in, normed, grad_act, hidden = section_backward(rows_in, grad_now, *weights)
        sum_in, sum_out = sums_now
        sum_in = lax.dynamic_update_index_in_dim(
            sum_in,
            lax.dynamic_index_in_dim(sum_in, half_group, 0, False)
            + contract_rows(normed, grad_act),
            half_group,
            0,
        )
        sum_out = lax.dynamic_update_index_in_dim(
            sum_out,
            lax.dynamic_index_in_dim(sum_out, half_group, 0, False)
            + contract_rows(hidden, grad_now),
            half_group,
            0,
        )
        return (grad_in, (sum_in, sum_out))

    def skip_section(operands):
        return (jnp.zeros_like(operands[1]), operands[2])

    return lax.cond(active, run_section, skip_section, (stream, grad_rows, grad_sums))


def update(weight, grad, moment, variance, factor):
    scaled = factor * grad
    moment = BETA_ONE * moment + (1.0 - BETA_ONE) * scaled
    variance = BETA_TWO * variance + (1.0 - BETA_TWO) * scaled * scaled
    weight = weight.astype(jnp.float32) - STEP_RATE * moment / (jnp.sqrt(variance) + ADAM_EPS)
    return (weight[None], moment[None], variance[None])


def shards(
    stream_in,
    cotangent,
    norm_gain,
    weight_in,
    weight_out,
    moment_in,
    variance_in,
    moment_out,
    variance_out,
):
    section_count = lax.axis_size("section")
    section_place = lax.axis_index("section")
    micro_count = stream_in.shape[0]
    in_slice = weight_in[0]
    out_slice = weight_out[0]
    full_in_shape = (in_slice.shape[0] * lax.axis_size("dp"), in_slice.shape[1])
    full_out_shape = (out_slice.shape[0] * lax.axis_size("dp"), out_slice.shape[1])
    empty_stream = jnp.zeros(stream_in.shape[1:], jnp.bfloat16)
    is_first = section_place == 0
    is_last = section_place == section_count - 1
    whole_in, whole_out = (
        lax.all_gather(in_slice, "dp", axis=0, tiled=True),
        lax.all_gather(out_slice, "dp", axis=0, tiled=True),
    )
    own_layer = (norm_gain[0], whole_in, whole_out)
    tick_count = micro_count + section_count - 1

    def run_forward(step_tick, loop_state):
        incoming, saved_rows = loop_state
        section_out, saved_rows = forward_tick(
            step_tick, section_place, is_first, incoming, saved_rows, stream_in, own_layer
        )
        return (from_behind(section_out, "section", 1), saved_rows)

    _, saved_rows = lax.fori_loop(
        0, tick_count, run_forward, (empty_stream, jnp.zeros_like(stream_in))
    )
    start_sums = (
        jnp.zeros((2,) + full_in_shape, jnp.float32),
        jnp.zeros((2,) + full_out_shape, jnp.float32),
    )

    def run_backward(step_tick, loop_state):
        incoming, grad_sums = loop_state
        grad_in, grad_sums = backward_tick(
            step_tick,
            section_count - 1 - section_place,
            is_last,
            incoming,
            saved_rows,
            cotangent,
            own_layer,
            grad_sums,
            2,
        )
        return (from_behind(grad_in, "section", -1), grad_sums)

    _, (stacked_in, stacked_out) = lax.fori_loop(
        0, tick_count, run_backward, (empty_stream, start_sums)
    )
    reduced_in, reduced_out = (
        lax.psum_scatter(
            stacked_in.astype(jnp.bfloat16), "dp", scatter_dimension=1, tiled=True
        ).astype(jnp.float32),
        lax.psum_scatter(
            stacked_out.astype(jnp.bfloat16), "dp", scatter_dimension=1, tiled=True
        ).astype(jnp.float32),
    )
    grad_w_in = reduced_in[0] + reduced_in[1]
    grad_w_out = reduced_out[0] + reduced_out[1]
    local_sum = jnp.sum(grad_w_in * grad_w_in) + jnp.sum(grad_w_out * grad_w_out)
    norm_total = lax.psum(local_sum, ("section", "dp"))
    count_all = 2.0 * E * R * section_count
    factor = jnp.minimum(1.0, lax.rsqrt(norm_total / count_all + CLIP_EPS))
    new_in, new_moment_in, new_variance_in = update(
        in_slice, grad_w_in, moment_in[0], variance_in[0], factor
    )
    new_out, new_moment_out, new_variance_out = update(
        out_slice, grad_w_out, moment_out[0], variance_out[0], factor
    )
    return (new_in, new_moment_in, new_variance_in, new_out, new_moment_out, new_variance_out)


MESH = pl.DeviceIdType.MESH
CORES = 2


def dot(left, right, left_dim, right_dim):
    return lax.dot_general(
        left, right, (((left_dim,), (right_dim,)), ((), ())), preferred_element_type=jnp.float32
    )


def step_kernel(
    sections,
    planes,
    stream_ref,
    cotangent_ref,
    piece_ref,
    gain_ref,
    grad_ref,
    factor_ref,
    weights,
    parts,
    from_core,
    chip_sums,
    from_planes,
    totals,
    owned,
    streams,
    pre_acts,
    roots,
    hiddens,
    sent,
    received,
    squares,
    squares_dp,
    squares_section,
    piece_send,
    piece_recv,
    rail_send,
    core_send,
    weight_recv,
    swap_send,
    swap_recv,
    part_send,
    part_recv,
    sum_send,
    sum_recv,
    total_send,
    total_recv,
    dp_send,
    dp_recv,
    section_send,
    section_recv,
):
    me_s = lax.axis_index("section")
    me_d = lax.axis_index("dp")
    plane = me_d // CORES
    core = lax.rem(me_d, CORES)
    other = 1 - core
    dp_count = planes * CORES
    tokens, width = stream_ref.shape
    channels = width * sections
    rank = piece_ref.shape[2]
    tiles = width // 128
    in_rows = gain_ref.shape[1]
    out_rows = rank // dp_count

    def section_peer(offset):
        return (lax.rem(me_s + offset, sections), me_d)

    def dp_peer(offset):
        return (me_s, lax.rem(me_d + offset, dp_count))

    def plane_peer(offset):
        return (me_s, lax.rem(plane + offset, planes) * CORES + core)

    partner = (me_s, plane * CORES + other)

    def remote(source, target, send_sem, recv_sem, device):
        copy = pltpu.make_async_remote_copy(
            src_ref=source,
            dst_ref=target,
            send_sem=send_sem,
            recv_sem=recv_sem,
            device_id=device,
            device_id_type=MESH,
        )
        copy.start()
        started.append(copy)
        return copy

    def landed(target, sem):
        pltpu.make_async_copy(target, target, sem).wait()

    started = []
    barrier = pltpu.get_barrier_semaphore()
    for offset in range(1, sections):
        pl.semaphore_signal(barrier, inc=1, device_id=section_peer(offset), device_id_type=MESH)
    for offset in range(1, dp_count):
        pl.semaphore_signal(barrier, inc=1, device_id=dp_peer(offset), device_id_type=MESH)
    pl.semaphore_wait(barrier, sections + dp_count - 2)

    for offset in range(1, sections):
        target = section_peer(offset)
        remote(
            piece_ref.at[target[0]],
            weights.at[me_s, plane, core],
            piece_send.at[offset - 1],
            piece_recv.at[me_s],
            target,
        )
    pltpu.make_async_copy(
        piece_ref.at[me_s], weights.at[me_s, plane, core], piece_recv.at[me_s]
    ).start()
    for k in range(sections):
        landed(weights.at[k, plane, core], piece_recv.at[k])
        piece = weights.at[k, plane, core]
        for offset in range(1, planes):
            remote(
                piece,
                piece,
                rail_send.at[k, offset - 1],
                weight_recv.at[k, plane, core],
                plane_peer(offset),
            )
        remote(piece, piece, core_send.at[k, 0], weight_recv.at[k, plane, core], partner)

    def pass_on(k):
        for offset in range(1, planes):
            source = lax.rem(plane + offset, planes)
            piece = weights.at[k, source, core]
            landed(piece, weight_recv.at[k, source, core])
            remote(
                piece, piece, core_send.at[k, offset], weight_recv.at[k, source, core], partner
            )

    def arrive(k):
        for source in range(planes):
            landed(weights.at[k, source, other], weight_recv.at[k, source, other])

    def weight_in(k):
        return weights[k, :, :, :in_rows, :].reshape(width, rank)

    def weight_out(k):
        columns = [
            weights[k, :, :, in_rows + out_rows * t : in_rows + out_rows * (t + 1), :].reshape(
                rank, 128
            )
            for t in range(tiles)
        ]
        return jnp.concatenate(columns, axis=1)

    def swap(slot, rows):
        return [
            remote(
                sent.at[slot, pl.ds(0, rows)],
                received.at[slot, offset - 1, pl.ds(0, rows)],
                swap_send.at[slot, offset - 1],
                swap_recv.at[slot, offset - 1],
                section_peer(offset),
            )
            for offset in range(1, sections)
        ]

    def spread(column):
        return jnp.transpose(jnp.broadcast_to(column, (tokens, tokens)))[:8]

    streams[0] = stream_ref[...]
    pass_on(0)
    grad_partial = None
    for k in range(sections):
        last = k == sections - 1
        arrive(k)
        values = streams[k]
        wide = values.astype(jnp.float32)
        partial = dot(values, weight_in(k), 1, 0)
        square = spread(jnp.sum(wide * wide, axis=1, keepdims=True))
        square_hi = square.astype(jnp.bfloat16).astype(jnp.float32)
        sent[k, :tokens] = partial.astype(jnp.bfloat16)
        sent[k, tokens : tokens + 16] = jnp.concatenate(
            [square_hi, square - square_hi], axis=0
        ).astype(jnp.bfloat16)
        rows = tokens + 16
        if last:
            grad_partial = dot(cotangent_ref[...], weight_out(k), 1, 1)
            sent[k, rows : rows + tokens] = grad_partial.astype(jnp.bfloat16)
            rows = rows + tokens
        copies = swap(k, rows)
        if not last:
            pass_on(k + 1)
        for offset, copy in enumerate(copies):
            copy.wait_recv()
            arrived = received[k, offset, : tokens + 16].astype(jnp.float32)
            partial = partial + arrived[:tokens]
            square = square + arrived[tokens : tokens + 8] + arrived[tokens + 8 : tokens + 16]
            if last:
                grad_partial = grad_partial + received[
                    k, offset, tokens + 16 : rows
                ].astype(jnp.float32)
        mean = jnp.transpose(jnp.broadcast_to(square[:1], (tokens, tokens))) / channels
        root = lax.rsqrt(mean + NORM_EPS)
        pre_act = partial * root[:, :rank]
        hidden = (pre_act * jax.nn.sigmoid(pre_act)).astype(jnp.bfloat16)
        pre_acts[k] = pre_act
        roots[k] = root
        hiddens[k] = hidden
        if not last:
            streams[k + 1] = (wide + dot(hidden, weight_out(k), 1, 0)).astype(jnp.bfloat16)

    def send_chip_sums(k):
        landed(from_core.at[k], part_recv.at[k])
        chip_sums[k] = (
            parts[k, :, core].astype(jnp.float32) + from_core[k].astype(jnp.float32)
        ).astype(jnp.bfloat16)
        for offset in range(1, planes):
            target = plane_peer(offset)
            remote(
                chip_sums.at[k, lax.rem(plane + offset, planes)],
                from_planes.at[k, offset - 1],
                sum_send.at[k, offset - 1],
                sum_recv.at[k, offset - 1],
                target,
            )

    grad = cotangent_ref[...].astype(jnp.float32)
    for k in reversed(range(sections)):
        slot = 2 * sections - 2 - k
        pre_act = pre_acts[k]
        root = roots[k]
        squash = jax.nn.sigmoid(pre_act)
        grad_act = grad_partial * squash * (1.0 + pre_act * (1.0 - squash))
        act = grad_act.astype(jnp.bfloat16)
        grad_rounded = grad.astype(jnp.bfloat16)
        copies = []
        if k > 0:
            column = root[:, :1]
            inner_mean = jnp.sum(grad_act * pre_act, axis=1, keepdims=True) / channels
            grad_normed = dot(act, weight_in(k), 1, 1)
            grad = grad + column * (
                grad_normed - streams[k].astype(jnp.float32) * (column * inner_mean)
            )
            grad_partial = dot(grad.astype(jnp.bfloat16), weight_out(k - 1), 1, 1)
            sent[slot + 1, :tokens] = grad_partial.astype(jnp.bfloat16)
            copies = swap(slot + 1, tokens)
        scaled = (grad_act * root[:, :rank]).astype(jnp.bfloat16)
        part_in = dot(streams[k], scaled, 0, 0).astype(jnp.bfloat16)
        parts[k, :, :, :in_rows, :] = part_in.reshape(planes, CORES, in_rows, rank)
        part_out = dot(hiddens[k], grad_rounded, 0, 0).astype(jnp.bfloat16)
        for t in range(tiles):
            parts[k, :, :, in_rows + out_rows * t : in_rows + out_rows * (t + 1), :] = part_out[
                :, 128 * t : 128 * (t + 1)
            ].reshape(planes, CORES, out_rows, 128)
        remote(parts.at[k, :, other], from_core.at[k], part_send.at[k], part_recv.at[k], partner)
        if k < sections - 1:
            send_chip_sums(k + 1)
        for offset, copy in enumerate(copies):
            copy.wait_recv()
            grad_partial = grad_partial + received[slot + 1, offset, :tokens].astype(jnp.float32)
    send_chip_sums(0)

    for k in reversed(range(sections)):
        total = chip_sums[k, plane].astype(jnp.float32)
        for offset in range(1, planes):
            landed(from_planes.at[k, offset - 1], sum_recv.at[k, offset - 1])
            total = total + from_planes[k, offset - 1].astype(jnp.float32)
        totals[k] = total.astype(jnp.bfloat16)

        @pl.when(me_s != k)
        def _():
            pltpu.make_async_remote_copy(
                src_ref=totals.at[k],
                dst_ref=owned.at[me_s],
                send_sem=total_send.at[k],
                recv_sem=total_recv.at[me_s],
                device_id=(k, me_d),
                device_id_type=MESH,
            ).start()

        @pl.when(me_s == k)
        def _():
            pltpu.make_async_copy(totals.at[k], owned.at[me_s], total_recv.at[me_s]).start()

    square = jnp.zeros((8, 128), jnp.float32)
    for s in range(sections):
        landed(owned.at[s], total_recv.at[s])
        piece = owned[s].astype(jnp.float32)
        in_part = piece[:in_rows] * gain_ref[s]
        out_part = piece[in_rows:]
        grad_ref[s, :in_rows] = in_part
        grad_ref[s, in_rows:] = out_part
        square = square + jnp.sum((in_part * in_part).reshape(-1, 8, 128), axis=0)
        square = square + jnp.sum((out_part * out_part).reshape(-1, 8, 128), axis=0)
    squares[0] = square
    copies = [
        remote(
            squares.at[0],
            squares_dp.at[offset - 1],
            dp_send.at[offset - 1],
            dp_recv.at[offset - 1],
            dp_peer(offset),
        )
        for offset in range(1, dp_count)
    ]
    for offset, copy in enumerate(copies):
        copy.wait_recv()
        square = square + squares_dp[offset]
    squares[1] = square
    copies = [
        remote(
            squares.at[1],
            squares_section.at[offset - 1],
            section_send.at[offset - 1],
            section_recv.at[offset - 1],
            section_peer(offset),
        )
        for offset in range(1, sections)
    ]
    for offset, copy in enumerate(copies):
        copy.wait_recv()
        square = square + squares_section[offset]
    count_all = 2.0 * channels * rank * sections
    norm_total = jnp.sum(square, keepdims=True)
    factor = jnp.minimum(1.0, lax.rsqrt(norm_total / count_all + CLIP_EPS))
    factor_ref[...] = jnp.broadcast_to(factor, factor_ref.shape)

    for copy in started:
        copy.wait_send()
    for k in range(sections):

        @pl.when(me_s != k)
        def _():
            pltpu.make_async_copy(totals.at[k], totals.at[k], total_send.at[k]).wait()


def fast_shards(
    stream_in,
    cotangent,
    norm_gain,
    weight_in,
    weight_out,
    moment_in,
    variance_in,
    moment_out,
    variance_out,
):
    sections = lax.axis_size("section")
    dp_count = lax.axis_size("dp")
    planes = dp_count // CORES
    place = lax.axis_index("section")
    row = lax.axis_index("dp")
    channels = stream_in.shape[-1]
    tokens = stream_in.shape[0] * stream_in.shape[1]
    shard_rows, rank = weight_in.shape[1:]
    if tokens != rank:
        return shards(
            stream_in,
            cotangent,
            norm_gain,
            weight_in,
            weight_out,
            moment_in,
            variance_in,
            moment_out,
            variance_out,
        )
    out_rows = weight_out.shape[1]
    in_rows = shard_rows // sections
    width = channels // sections
    tiles = width // 128
    piece_rows = in_rows + out_rows * tiles

    def own_channels(rows):
        rows = rows.reshape(tokens, dp_count, sections, in_rows)
        return lax.dynamic_index_in_dim(rows, place, 2, False).reshape(tokens, width)

    gain = lax.dynamic_slice_in_dim(norm_gain[0], row * shard_rows, shard_rows).astype(jnp.float32)
    gained = (weight_in[0].astype(jnp.float32) * gain[:, None]).astype(jnp.bfloat16)
    out_cut = weight_out[0].reshape(out_rows, dp_count, sections, in_rows)
    out_cut = out_cut.transpose(2, 0, 1, 3).reshape(sections, out_rows, tiles, 128)
    out_cut = out_cut.transpose(0, 2, 1, 3).reshape(sections, tiles * out_rows, 128)
    pieces = jnp.concatenate([gained.reshape(sections, in_rows, rank), out_cut], axis=1)

    narrow, full = jnp.bfloat16, jnp.float32
    slots = 2 * sections - 1
    dma = pltpu.SemaphoreType.DMA
    vmem = pl.BlockSpec(memory_space=pltpu.VMEM)
    grads, factor = pl.pallas_call(
        functools.partial(step_kernel, sections, planes),
        out_shape=(
            jax.ShapeDtypeStruct((sections, piece_rows, 128), full),
            jax.ShapeDtypeStruct((8, 128), full),
        ),
        in_specs=[vmem] * 4,
        out_specs=(vmem, vmem),
        scratch_shapes=[
            pltpu.VMEM((sections, planes, CORES, piece_rows, 128), narrow),
            pltpu.VMEM((sections, planes, CORES, piece_rows, 128), narrow),
            pltpu.VMEM((sections, planes, piece_rows, 128), narrow),
            pltpu.VMEM((sections, planes, piece_rows, 128), narrow),
            pltpu.VMEM((sections, planes - 1, piece_rows, 128), narrow),
            pltpu.VMEM((sections, piece_rows, 128), narrow),
            pltpu.VMEM((sections, piece_rows, 128), narrow),
            pltpu.VMEM((sections, tokens, width), narrow),
            pltpu.VMEM((sections, tokens, rank), full),
            pltpu.VMEM((sections, tokens, tokens), full),
            pltpu.VMEM((sections, tokens, rank), narrow),
            pltpu.VMEM((slots, 2 * tokens + 16, rank), narrow),
            pltpu.VMEM((slots, sections - 1, 2 * tokens + 16, rank), narrow),
            pltpu.VMEM((2, 8, 128), full),
            pltpu.VMEM((dp_count - 1, 8, 128), full),
            pltpu.VMEM((sections - 1, 8, 128), full),
            dma((sections - 1,)),
            dma((sections,)),
            dma((sections, planes - 1)),
            dma((sections, planes)),
            dma((sections, planes, CORES)),
            dma((slots, sections - 1)),
            dma((slots, sections - 1)),
            dma((sections,)),
            dma((sections,)),
            dma((sections, planes - 1)),
            dma((sections, planes - 1)),
            dma((sections,)),
            dma((sections,)),
            dma((dp_count - 1,)),
            dma((dp_count - 1,)),
            dma((sections - 1,)),
            dma((sections - 1,)),
        ],
        compiler_params=pltpu.CompilerParams(
            collective_id=0, has_side_effects=True, vmem_limit_bytes=48 * 1024 * 1024
        ),
    )(
        own_channels(stream_in),
        own_channels(cotangent),
        pieces,
        gain.reshape(sections, in_rows, 1),
    )
    factor = factor[0, 0]
    grad_w_in = grads[:, :in_rows].reshape(shard_rows, rank)
    grad_w_out = grads[:, in_rows:].reshape(sections, tiles, out_rows, 128).transpose(0, 2, 1, 3)
    grad_w_out = grad_w_out.reshape(sections, out_rows, dp_count, in_rows).transpose(1, 2, 0, 3)
    grad_w_out = grad_w_out.reshape(out_rows, channels)
    new_in, new_moment_in, new_variance_in = update(
        weight_in[0], grad_w_in, moment_in[0], variance_in[0], factor
    )
    new_out, new_moment_out, new_variance_out = update(
        weight_out[0], grad_w_out, moment_out[0], variance_out[0], factor
    )
    return (new_in, new_moment_in, new_variance_in, new_out, new_moment_out, new_variance_out)


def aligned(sections, dp_count):
    width, in_rows, out_rows = E // sections, E // (sections * dp_count), R // dp_count
    return (
        sections > 1
        and dp_count % CORES == 0
        and dp_count > CORES
        and width % 128 == 0
        and in_rows % 16 == 0
        and out_rows % 16 == 0
        and R == 128
    )


def solution(mesh):
    fast = aligned(mesh.shape["section"], mesh.shape["dp"])
    return jax.shard_map(
        fast_shards if fast else shards,
        mesh=mesh,
        in_specs=(
            P(None, "dp", None),
            P(None, "dp", None),
            P("section", None),
            P("section", "dp", None),
            P("section", "dp", None),
            P("section", "dp", None),
            P("section", "dp", None),
            P("section", "dp", None),
            P("section", "dp", None),
        ),
        out_specs=(
            P("section", "dp", None),
            P("section", "dp", None),
            P("section", "dp", None),
            P("section", "dp", None),
            P("section", "dp", None),
            P("section", "dp", None),
        ),
        check_vma=False,
    )
```

```python
import functools

import jax
import jax.numpy as jnp
from jax import lax
from jax.experimental import pallas as pl
from jax.experimental.pallas import tpu as pltpu
from jax.sharding import PartitionSpec as P

E = 3584
R = 128


NORM_EPS = 1e-06
BETA_ONE = 0.9
BETA_TWO = 0.95
STEP_RATE = 0.01
ADAM_EPS = 1e-08
CLIP_EPS = 1e-06


def from_behind(x, axis, by):
    count = lax.axis_size(axis)
    pairs = [(i, i + by) for i in range(count) if 0 <= i + by < count]
    return lax.ppermute(x, axis, pairs)


def normalize(stream, gain):
    values = stream.astype(jnp.float32)
    inv_root = lax.rsqrt(jnp.mean(values * values, axis=-1, keepdims=True) + NORM_EPS)
    unit_rows = values * inv_root
    normed = (unit_rows * gain.astype(jnp.float32)).astype(jnp.bfloat16)
    return (values, inv_root, unit_rows, normed)


def section_forward(stream, gain, in_weight, out_weight):
    values, inv_root, unit_rows, normed = normalize(stream, gain)
    pre_act = jnp.dot(normed, in_weight, preferred_element_type=jnp.float32)
    hidden = (pre_act * jax.nn.sigmoid(pre_act)).astype(jnp.bfloat16)
    return (values + jnp.dot(hidden, out_weight, preferred_element_type=jnp.float32)).astype(
        jnp.bfloat16
    )


def section_backward(stream, grad_rows, gain, in_weight, out_weight):
    values, inv_root, unit_rows, normed = normalize(stream, gain)
    pre_act = jnp.dot(normed, in_weight, preferred_element_type=jnp.float32)
    squash = jax.nn.sigmoid(pre_act)
    hidden = (pre_act * squash).astype(jnp.bfloat16)
    grad_hidden = lax.dot_general(
        grad_rows, out_weight, (((1,), (1,)), ((), ())), preferred_element_type=jnp.float32
    )
    grad_act = (grad_hidden * squash * (1.0 + pre_act * (1.0 - squash))).astype(jnp.bfloat16)
    grad_normed = lax.dot_general(
        grad_act, in_weight, (((1,), (1,)), ((), ())), preferred_element_type=jnp.float32
    ) * gain.astype(jnp.float32)
    inner_mean = jnp.mean(grad_normed * unit_rows, axis=-1, keepdims=True)
    grad_in = (
        grad_rows.astype(jnp.float32) + inv_root * (grad_normed - unit_rows * inner_mean)
    ).astype(jnp.bfloat16)
    return (grad_in, normed, grad_act, hidden)


def contract_rows(left, right):
    return lax.dot_general(
        left, right, (((0,), (0,)), ((), ())), preferred_element_type=jnp.float32
    )


def forward_tick(step_tick, position, is_first, incoming, saved_rows, inputs, weights):
    batch_count = inputs.shape[0]
    chain_index = step_tick - position
    active = jnp.logical_and(chain_index >= 0, chain_index < batch_count)
    batch_slot = jnp.clip(chain_index, 0, batch_count - 1)
    stream = jnp.where(is_first, lax.dynamic_index_in_dim(inputs, batch_slot, 0, False), incoming)
    kept_row = jnp.where(active, stream, lax.dynamic_index_in_dim(saved_rows, batch_slot, 0, False))
    saved_rows = lax.dynamic_update_index_in_dim(saved_rows, kept_row, batch_slot, 0)
    section_out = lax.cond(
        active, lambda rows_in: section_forward(rows_in, *weights), jnp.zeros_like, stream
    )
    return (section_out, saved_rows)


def backward_tick(
    step_tick, position, is_last, incoming, saved_rows, targets, weights, grad_sums, groups
):
    batch_count = targets.shape[0]
    chain_index = step_tick - position
    active = jnp.logical_and(chain_index >= 0, chain_index < batch_count)
    batch_slot = jnp.clip(chain_index, 0, batch_count - 1)
    grad_rows = jnp.where(
        is_last, lax.dynamic_index_in_dim(targets, batch_slot, 0, False), incoming
    )
    stream = lax.dynamic_index_in_dim(saved_rows, batch_slot, 0, False)
    half_group = batch_slot * groups // batch_count

    def run_section(operands):
        rows_in, grad_now, sums_now = operands
        grad_in, normed, grad_act, hidden = section_backward(rows_in, grad_now, *weights)
        sum_in, sum_out = sums_now
        sum_in = lax.dynamic_update_index_in_dim(
            sum_in,
            lax.dynamic_index_in_dim(sum_in, half_group, 0, False)
            + contract_rows(normed, grad_act),
            half_group,
            0,
        )
        sum_out = lax.dynamic_update_index_in_dim(
            sum_out,
            lax.dynamic_index_in_dim(sum_out, half_group, 0, False)
            + contract_rows(hidden, grad_now),
            half_group,
            0,
        )
        return (grad_in, (sum_in, sum_out))

    def skip_section(operands):
        return (jnp.zeros_like(operands[1]), operands[2])

    return lax.cond(active, run_section, skip_section, (stream, grad_rows, grad_sums))


def update(weight, grad, moment, variance, factor):
    scaled = factor * grad
    moment = BETA_ONE * moment + (1.0 - BETA_ONE) * scaled
    variance = BETA_TWO * variance + (1.0 - BETA_TWO) * scaled * scaled
    weight = weight.astype(jnp.float32) - STEP_RATE * moment / (jnp.sqrt(variance) + ADAM_EPS)
    return (weight[None], moment[None], variance[None])


def shards(
    stream_in,
    cotangent,
    norm_gain,
    weight_in,
    weight_out,
    moment_in,
    variance_in,
    moment_out,
    variance_out,
):
    section_count = lax.axis_size("section")
    section_place = lax.axis_index("section")
    micro_count = stream_in.shape[0]
    in_slice = weight_in[0]
    out_slice = weight_out[0]
    full_in_shape = (in_slice.shape[0] * lax.axis_size("dp"), in_slice.shape[1])
    full_out_shape = (out_slice.shape[0] * lax.axis_size("dp"), out_slice.shape[1])
    empty_stream = jnp.zeros(stream_in.shape[1:], jnp.bfloat16)
    is_first = section_place == 0
    is_last = section_place == section_count - 1
    whole_in, whole_out = (
        lax.all_gather(in_slice, "dp", axis=0, tiled=True),
        lax.all_gather(out_slice, "dp", axis=0, tiled=True),
    )
    own_layer = (norm_gain[0], whole_in, whole_out)
    tick_count = micro_count + section_count - 1

    def run_forward(step_tick, loop_state):
        incoming, saved_rows = loop_state
        section_out, saved_rows = forward_tick(
            step_tick, section_place, is_first, incoming, saved_rows, stream_in, own_layer
        )
        return (from_behind(section_out, "section", 1), saved_rows)

    _, saved_rows = lax.fori_loop(
        0, tick_count, run_forward, (empty_stream, jnp.zeros_like(stream_in))
    )
    start_sums = (
        jnp.zeros((2,) + full_in_shape, jnp.float32),
        jnp.zeros((2,) + full_out_shape, jnp.float32),
    )

    def run_backward(step_tick, loop_state):
        incoming, grad_sums = loop_state
        grad_in, grad_sums = backward_tick(
            step_tick,
            section_count - 1 - section_place,
            is_last,
            incoming,
            saved_rows,
            cotangent,
            own_layer,
            grad_sums,
            2,
        )
        return (from_behind(grad_in, "section", -1), grad_sums)

    _, (stacked_in, stacked_out) = lax.fori_loop(
        0, tick_count, run_backward, (empty_stream, start_sums)
    )
    reduced_in, reduced_out = (
        lax.psum_scatter(
            stacked_in.astype(jnp.bfloat16), "dp", scatter_dimension=1, tiled=True
        ).astype(jnp.float32),
        lax.psum_scatter(
            stacked_out.astype(jnp.bfloat16), "dp", scatter_dimension=1, tiled=True
        ).astype(jnp.float32),
    )
    grad_w_in = reduced_in[0] + reduced_in[1]
    grad_w_out = reduced_out[0] + reduced_out[1]
    local_sum = jnp.sum(grad_w_in * grad_w_in) + jnp.sum(grad_w_out * grad_w_out)
    norm_total = lax.psum(local_sum, ("section", "dp"))
    count_all = 2.0 * E * R * section_count
    factor = jnp.minimum(1.0, lax.rsqrt(norm_total / count_all + CLIP_EPS))
    new_in, new_moment_in, new_variance_in = update(
        in_slice, grad_w_in, moment_in[0], variance_in[0], factor
    )
    new_out, new_moment_out, new_variance_out = update(
        out_slice, grad_w_out, moment_out[0], variance_out[0], factor
    )
    return (new_in, new_moment_in, new_variance_in, new_out, new_moment_out, new_variance_out)


MESH = pl.DeviceIdType.MESH
CORES = 2


def dot(left, right, left_dim, right_dim):
    return lax.dot_general(
        left, right, (((left_dim,), (right_dim,)), ((), ())), preferred_element_type=jnp.float32
    )


def step_kernel(
    sections,
    planes,
    stream_ref,
    cotangent_any,
    gain_ref,
    weight_in_ref,
    weight_out_ref,
    grad_in_ref,
    grad_out_ref,
    factor_ref,
    rows_ref,
    cotangent_ref,
    piece_ref,
    gain_rows,
    weights,
    parts,
    from_core,
    chip_sums,
    from_planes,
    totals,
    owned,
    streams,
    pre_acts,
    roots,
    hiddens,
    sent,
    received,
    squares,
    squares_dp,
    squares_section,
    row_sems,
    piece_send,
    piece_recv,
    rail_send,
    core_send,
    weight_recv,
    swap_send,
    swap_recv,
    part_send,
    part_recv,
    sum_send,
    sum_recv,
    total_send,
    total_recv,
    dp_send,
    dp_recv,
    section_send,
    section_recv,
):
    me_s = lax.axis_index("section")
    me_d = lax.axis_index("dp")
    plane = me_d // CORES
    core = lax.rem(me_d, CORES)
    other = 1 - core
    dp_count = planes * CORES
    tokens, width = cotangent_ref.shape
    channels = width * sections
    shard_rows, rank = weight_in_ref.shape
    tiles = width // 128
    in_rows = shard_rows // sections
    out_rows = weight_out_ref.shape[0]

    def section_peer(offset):
        return (lax.rem(me_s + offset, sections), me_d)

    def dp_peer(offset):
        return (me_s, lax.rem(me_d + offset, dp_count))

    def plane_peer(offset):
        return (me_s, lax.rem(plane + offset, planes) * CORES + core)

    partner = (me_s, plane * CORES + other)

    def remote(source, target, send_sem, recv_sem, device):
        copy = pltpu.make_async_remote_copy(
            src_ref=source,
            dst_ref=target,
            send_sem=send_sem,
            recv_sem=recv_sem,
            device_id=device,
            device_id_type=MESH,
        )
        copy.start()
        started.append(copy)
        return copy

    def landed(target, sem):
        pltpu.make_async_copy(target, target, sem).wait()

    started = []
    row_copies = [
        pltpu.make_async_copy(source, rows_ref.at[i], row_sems.at[i])
        for i, source in enumerate((stream_ref, cotangent_any))
    ]
    for copy in row_copies:
        copy.start()
    barrier = pltpu.get_barrier_semaphore()
    for offset in range(1, sections):
        pl.semaphore_signal(barrier, inc=1, device_id=section_peer(offset), device_id_type=MESH)
    for offset in range(1, dp_count):
        pl.semaphore_signal(barrier, inc=1, device_id=dp_peer(offset), device_id_type=MESH)

    gain_tiles = gain_ref.shape[0]
    gains = jnp.concatenate(
        [gain_ref[...].astype(jnp.float32), jnp.zeros((128 - gain_tiles, 128), jnp.float32)], axis=0
    )
    gains = jnp.transpose(gains)
    lanes = lax.broadcasted_iota(jnp.int32, (128, 128), 1)
    for b in range(shard_rows // 64):
        half = me_d * (shard_rows // 64) + b
        column = jnp.sum(jnp.where(lanes == half // 2, gains, 0.0), axis=1, keepdims=True)
        odd = jnp.full((64, 1), lax.rem(half, 2), jnp.int32) == 1
        gain_rows[64 * b : 64 * (b + 1)] = jnp.broadcast_to(
            jnp.where(odd, column[64:], column[:64]), (64, 128)
        )

    def own_channels(rows, s):
        cuts = [
            rows[:, shard_rows * d + in_rows * s : shard_rows * d + in_rows * (s + 1)]
            for d in range(dp_count)
        ]
        return jnp.concatenate(cuts, axis=1)

    shard_out = weight_out_ref[...].astype(jnp.float32)
    for s in range(sections):
        own = slice(in_rows * s, in_rows * (s + 1))
        piece_ref[s, :in_rows] = (
            weight_in_ref[own].astype(jnp.float32) * gain_rows[own]
        ).astype(jnp.bfloat16)
        cut = own_channels(shard_out, s).astype(jnp.bfloat16)
        for t in range(tiles):
            piece_ref[s, in_rows + out_rows * t : in_rows + out_rows * (t + 1)] = cut[
                :, 128 * t : 128 * (t + 1)
            ]
    pl.semaphore_wait(barrier, sections + dp_count - 2)

    for offset in range(1, sections):
        target = section_peer(offset)
        remote(
            piece_ref.at[target[0]],
            weights.at[me_s, plane, core],
            piece_send.at[offset - 1],
            piece_recv.at[me_s],
            target,
        )
    pltpu.make_async_copy(
        piece_ref.at[me_s], weights.at[me_s, plane, core], piece_recv.at[me_s]
    ).start()
    for k in range(sections):
        landed(weights.at[k, plane, core], piece_recv.at[k])
        piece = weights.at[k, plane, core]
        for offset in range(1, planes):
            remote(
                piece,
                piece,
                rail_send.at[k, offset - 1],
                weight_recv.at[k, plane, core],
                plane_peer(offset),
            )
        remote(piece, piece, core_send.at[k, 0], weight_recv.at[k, plane, core], partner)

    def pass_on(k):
        for offset in range(1, planes):
            source = lax.rem(plane + offset, planes)
            piece = weights.at[k, source, core]
            landed(piece, weight_recv.at[k, source, core])
            remote(
                piece, piece, core_send.at[k, offset], weight_recv.at[k, source, core], partner
            )

    def arrive(k):
        for source in range(planes):
            landed(weights.at[k, source, other], weight_recv.at[k, source, other])

    def weight_in(k):
        return weights[k, :, :, :in_rows, :].reshape(width, rank)

    def weight_out(k):
        columns = [
            weights[k, :, :, in_rows + out_rows * t : in_rows + out_rows * (t + 1), :].reshape(
                rank, 128
            )
            for t in range(tiles)
        ]
        return jnp.concatenate(columns, axis=1)

    def swap(slot, rows):
        return [
            remote(
                sent.at[slot, pl.ds(0, rows)],
                received.at[slot, offset - 1, pl.ds(0, rows)],
                swap_send.at[slot, offset - 1],
                swap_recv.at[slot, offset - 1],
                section_peer(offset),
            )
            for offset in range(1, sections)
        ]

    def spread(column):
        return jnp.transpose(jnp.broadcast_to(column, (tokens, tokens)))[:8]

    for copy in row_copies:
        copy.wait()
    for s in range(sections):

        @pl.when(me_s == s)
        def _():
            streams[0] = own_channels(rows_ref[0].astype(jnp.float32), s).astype(jnp.bfloat16)
            cotangent_ref[...] = own_channels(rows_ref[1].astype(jnp.float32), s).astype(
                jnp.bfloat16
            )

    pass_on(0)
    grad_partial = None
    for k in range(sections):
        last = k == sections - 1
        arrive(k)
        values = streams[k]
        wide = values.astype(jnp.float32)
        partial = dot(values, weight_in(k), 1, 0)
        square = spread(jnp.sum(wide * wide, axis=1, keepdims=True))
        square_hi = square.astype(jnp.bfloat16).astype(jnp.float32)
        sent[k, :tokens] = partial.astype(jnp.bfloat16)
        sent[k, tokens : tokens + 16] = jnp.concatenate(
            [square_hi, square - square_hi], axis=0
        ).astype(jnp.bfloat16)
        rows = tokens + 16
        if last:
            grad_partial = dot(cotangent_ref[...], weight_out(k), 1, 1)
            sent[k, rows : rows + tokens] = grad_partial.astype(jnp.bfloat16)
            rows = rows + tokens
        copies = swap(k, rows)
        if not last:
            pass_on(k + 1)
        for offset, copy in enumerate(copies):
            copy.wait_recv()
            arrived = received[k, offset, : tokens + 16].astype(jnp.float32)
            partial = partial + arrived[:tokens]
            square = square + arrived[tokens : tokens + 8] + arrived[tokens + 8 : tokens + 16]
            if last:
                grad_partial = grad_partial + received[
                    k, offset, tokens + 16 : rows
                ].astype(jnp.float32)
        mean = jnp.transpose(jnp.broadcast_to(square[:1], (tokens, tokens))) / channels
        root = lax.rsqrt(mean + NORM_EPS)
        pre_act = partial * root[:, :rank]
        hidden = (pre_act * jax.nn.sigmoid(pre_act)).astype(jnp.bfloat16)
        pre_acts[k] = pre_act
        roots[k] = root
        hiddens[k] = hidden
        if not last:
            streams[k + 1] = (wide + dot(hidden, weight_out(k), 1, 0)).astype(jnp.bfloat16)

    def send_chip_sums(k):
        landed(from_core.at[k], part_recv.at[k])
        chip_sums[k] = (
            parts[k, :, core].astype(jnp.float32) + from_core[k].astype(jnp.float32)
        ).astype(jnp.bfloat16)
        for offset in range(1, planes):
            target = plane_peer(offset)
            remote(
                chip_sums.at[k, lax.rem(plane + offset, planes)],
                from_planes.at[k, offset - 1],
                sum_send.at[k, offset - 1],
                sum_recv.at[k, offset - 1],
                target,
            )

    grad = cotangent_ref[...].astype(jnp.float32)
    for k in reversed(range(sections)):
        slot = 2 * sections - 2 - k
        pre_act = pre_acts[k]
        root = roots[k]
        squash = jax.nn.sigmoid(pre_act)
        grad_act = grad_partial * squash * (1.0 + pre_act * (1.0 - squash))
        act = grad_act.astype(jnp.bfloat16)
        grad_rounded = grad.astype(jnp.bfloat16)
        copies = []
        if k > 0:
            column = root[:, :1]
            inner_mean = jnp.sum(grad_act * pre_act, axis=1, keepdims=True) / channels
            grad_normed = dot(act, weight_in(k), 1, 1)
            grad = grad + column * (
                grad_normed - streams[k].astype(jnp.float32) * (column * inner_mean)
            )
            grad_partial = dot(grad.astype(jnp.bfloat16), weight_out(k - 1), 1, 1)
            sent[slot + 1, :tokens] = grad_partial.astype(jnp.bfloat16)
            copies = swap(slot + 1, tokens)
        scaled = (grad_act * root[:, :rank]).astype(jnp.bfloat16)
        part_in = dot(streams[k], scaled, 0, 0).astype(jnp.bfloat16)
        parts[k, :, :, :in_rows, :] = part_in.reshape(planes, CORES, in_rows, rank)
        part_out = dot(hiddens[k], grad_rounded, 0, 0).astype(jnp.bfloat16)
        for t in range(tiles):
            parts[k, :, :, in_rows + out_rows * t : in_rows + out_rows * (t + 1), :] = part_out[
                :, 128 * t : 128 * (t + 1)
            ].reshape(planes, CORES, out_rows, 128)
        remote(parts.at[k, :, other], from_core.at[k], part_send.at[k], part_recv.at[k], partner)
        if k < sections - 1:
            send_chip_sums(k + 1)
        for offset, copy in enumerate(copies):
            copy.wait_recv()
            grad_partial = grad_partial + received[slot + 1, offset, :tokens].astype(jnp.float32)
    send_chip_sums(0)

    for k in reversed(range(sections)):
        total = chip_sums[k, plane].astype(jnp.float32)
        for offset in range(1, planes):
            landed(from_planes.at[k, offset - 1], sum_recv.at[k, offset - 1])
            total = total + from_planes[k, offset - 1].astype(jnp.float32)
        totals[k] = total.astype(jnp.bfloat16)

        @pl.when(me_s != k)
        def _():
            pltpu.make_async_remote_copy(
                src_ref=totals.at[k],
                dst_ref=owned.at[me_s],
                send_sem=total_send.at[k],
                recv_sem=total_recv.at[me_s],
                device_id=(k, me_d),
                device_id_type=MESH,
            ).start()

        @pl.when(me_s == k)
        def _():
            pltpu.make_async_copy(totals.at[k], owned.at[me_s], total_recv.at[me_s]).start()

    square = jnp.zeros((8, 128), jnp.float32)
    out_parts = []
    for s in range(sections):
        landed(owned.at[s], total_recv.at[s])
        piece = owned[s].astype(jnp.float32)
        own = slice(in_rows * s, in_rows * (s + 1))
        in_part = piece[:in_rows] * gain_rows[own]
        out_part = piece[in_rows:]
        grad_in_ref[own] = in_part
        out_parts.append(
            jnp.concatenate(
                [out_part[out_rows * t : out_rows * (t + 1)] for t in range(tiles)], axis=1
            )
        )
        square = square + jnp.sum((in_part * in_part).reshape(-1, 8, 128), axis=0)
        square = square + jnp.sum((out_part * out_part).reshape(-1, 8, 128), axis=0)
    squares[0] = square
    copies = [
        remote(
            squares.at[0],
            squares_dp.at[offset - 1],
            dp_send.at[offset - 1],
            dp_recv.at[offset - 1],
            dp_peer(offset),
        )
        for offset in range(1, dp_count)
    ]
    grad_out_ref[...] = jnp.concatenate(
        [
            out_parts[s][:, in_rows * d : in_rows * (d + 1)]
            for d in range(dp_count)
            for s in range(sections)
        ],
        axis=1,
    )
    for offset, copy in enumerate(copies):
        copy.wait_recv()
        square = square + squares_dp[offset]
    squares[1] = square
    copies = [
        remote(
            squares.at[1],
            squares_section.at[offset - 1],
            section_send.at[offset - 1],
            section_recv.at[offset - 1],
            section_peer(offset),
        )
        for offset in range(1, sections)
    ]
    for offset, copy in enumerate(copies):
        copy.wait_recv()
        square = square + squares_section[offset]
    count_all = 2.0 * channels * rank * sections
    norm_total = jnp.sum(square, keepdims=True)
    factor = jnp.minimum(1.0, lax.rsqrt(norm_total / count_all + CLIP_EPS))
    factor_ref[...] = jnp.broadcast_to(factor, factor_ref.shape)

    for copy in started:
        copy.wait_send()
    for k in range(sections):

        @pl.when(me_s != k)
        def _():
            pltpu.make_async_copy(totals.at[k], totals.at[k], total_send.at[k]).wait()


def adam_kernel(factor_ref, *refs):
    factor = factor_ref[:1, :1]
    for place in (0, 1):
        weight, grad, moment, variance = (ref for ref in refs[4 * place : 4 * place + 4])
        results = update(weight[0], grad[...], moment[0], variance[0], factor)
        for ref, result in zip(refs[8 + 3 * place : 11 + 3 * place], results):
            ref[...] = result


def fast_shards(
    stream_in,
    cotangent,
    norm_gain,
    weight_in,
    weight_out,
    moment_in,
    variance_in,
    moment_out,
    variance_out,
):
    sections = lax.axis_size("section")
    dp_count = lax.axis_size("dp")
    planes = dp_count // CORES
    channels = stream_in.shape[-1]
    tokens = stream_in.shape[0] * stream_in.shape[1]
    shard_rows, rank = weight_in.shape[1:]
    if tokens != rank:
        return shards(
            stream_in,
            cotangent,
            norm_gain,
            weight_in,
            weight_out,
            moment_in,
            variance_in,
            moment_out,
            variance_out,
        )
    out_rows = weight_out.shape[1]
    in_rows = shard_rows // sections
    width = channels // sections
    tiles = width // 128
    piece_rows = in_rows + out_rows * tiles

    narrow, full = jnp.bfloat16, jnp.float32
    slots = 2 * sections - 1
    dma = pltpu.SemaphoreType.DMA
    vmem = pl.BlockSpec(memory_space=pltpu.VMEM)
    grad_w_in, grad_w_out, factor = pl.pallas_call(
        functools.partial(step_kernel, sections, planes),
        out_shape=(
            jax.ShapeDtypeStruct((shard_rows, rank), full),
            jax.ShapeDtypeStruct((out_rows, channels), full),
            jax.ShapeDtypeStruct((8, 128), full),
        ),
        in_specs=[pl.BlockSpec(memory_space=pl.ANY)] * 2 + [vmem] * 3,
        out_specs=(vmem, vmem, vmem),
        scratch_shapes=[
            pltpu.VMEM((2, tokens, channels), narrow),
            pltpu.VMEM((tokens, width), narrow),
            pltpu.VMEM((sections, piece_rows, 128), narrow),
            pltpu.VMEM((shard_rows, 128), full),
            pltpu.VMEM((sections, planes, CORES, piece_rows, 128), narrow),
            pltpu.VMEM((sections, planes, CORES, piece_rows, 128), narrow),
            pltpu.VMEM((sections, planes, piece_rows, 128), narrow),
            pltpu.VMEM((sections, planes, piece_rows, 128), narrow),
            pltpu.VMEM((sections, planes - 1, piece_rows, 128), narrow),
            pltpu.VMEM((sections, piece_rows, 128), narrow),
            pltpu.VMEM((sections, piece_rows, 128), narrow),
            pltpu.VMEM((sections, tokens, width), narrow),
            pltpu.VMEM((sections, tokens, rank), full),
            pltpu.VMEM((sections, tokens, tokens), full),
            pltpu.VMEM((sections, tokens, rank), narrow),
            pltpu.VMEM((slots, 2 * tokens + 16, rank), narrow),
            pltpu.VMEM((slots, sections - 1, 2 * tokens + 16, rank), narrow),
            pltpu.VMEM((2, 8, 128), full),
            pltpu.VMEM((dp_count - 1, 8, 128), full),
            pltpu.VMEM((sections - 1, 8, 128), full),
            dma((2,)),
            dma((sections - 1,)),
            dma((sections,)),
            dma((sections, planes - 1)),
            dma((sections, planes)),
            dma((sections, planes, CORES)),
            dma((slots, sections - 1)),
            dma((slots, sections - 1)),
            dma((sections,)),
            dma((sections,)),
            dma((sections, planes - 1)),
            dma((sections, planes - 1)),
            dma((sections,)),
            dma((sections,)),
            dma((dp_count - 1,)),
            dma((dp_count - 1,)),
            dma((sections - 1,)),
            dma((sections - 1,)),
        ],
        compiler_params=pltpu.CompilerParams(
            collective_id=0, has_side_effects=True, vmem_limit_bytes=48 * 1024 * 1024
        ),
    )(
        stream_in.reshape(tokens, channels),
        cotangent.reshape(tokens, channels),
        norm_gain.reshape(channels // 128, 128),
        weight_in[0],
        weight_out[0],
    )
    in_shape = jax.ShapeDtypeStruct(moment_in.shape, full)
    out_shape = jax.ShapeDtypeStruct(moment_out.shape, full)
    return pl.pallas_call(
        adam_kernel,
        out_shape=(in_shape,) * 3 + (out_shape,) * 3,
        in_specs=[vmem] * 9,
        out_specs=(vmem,) * 6,
        compiler_params=pltpu.CompilerParams(vmem_limit_bytes=16 * 1024 * 1024),
    )(
        factor,
        weight_in,
        grad_w_in,
        moment_in,
        variance_in,
        weight_out,
        grad_w_out,
        moment_out,
        variance_out,
    )


def aligned(sections, dp_count):
    width, in_rows, out_rows = E // sections, E // (sections * dp_count), R // dp_count
    return (
        sections > 1
        and dp_count % CORES == 0
        and dp_count > CORES
        and width % 128 == 0
        and in_rows % 16 == 0
        and out_rows % 16 == 0
        and R == 128
        and E <= 128 * 128
        and E % (64 * dp_count) == 0
    )


def solution(mesh):
    fast = aligned(mesh.shape["section"], mesh.shape["dp"])
    return jax.shard_map(
        fast_shards if fast else shards,
        mesh=mesh,
        in_specs=(
            P(None, "dp", None),
            P(None, "dp", None),
            P("section", None),
            P("section", "dp", None),
            P("section", "dp", None),
            P("section", "dp", None),
            P("section", "dp", None),
            P("section", "dp", None),
            P("section", "dp", None),
        ),
        out_specs=(
            P("section", "dp", None),
            P("section", "dp", None),
            P("section", "dp", None),
            P("section", "dp", None),
            P("section", "dp", None),
            P("section", "dp", None),
        ),
        check_vma=False,
    )
```

```python
import functools

import jax
import jax.numpy as jnp
from jax import lax
from jax.experimental import pallas as pl
from jax.experimental.pallas import tpu as pltpu
from jax.sharding import PartitionSpec as P

E = 3584
R = 128


NORM_EPS = 1e-06
BETA_ONE = 0.9
BETA_TWO = 0.95
STEP_RATE = 0.01
ADAM_EPS = 1e-08
CLIP_EPS = 1e-06


def from_behind(x, axis, by):
    count = lax.axis_size(axis)
    pairs = [(i, i + by) for i in range(count) if 0 <= i + by < count]
    return lax.ppermute(x, axis, pairs)


def normalize(stream, gain):
    values = stream.astype(jnp.float32)
    inv_root = lax.rsqrt(jnp.mean(values * values, axis=-1, keepdims=True) + NORM_EPS)
    unit_rows = values * inv_root
    normed = (unit_rows * gain.astype(jnp.float32)).astype(jnp.bfloat16)
    return (values, inv_root, unit_rows, normed)


def section_forward(stream, gain, in_weight, out_weight):
    values, inv_root, unit_rows, normed = normalize(stream, gain)
    pre_act = jnp.dot(normed, in_weight, preferred_element_type=jnp.float32)
    hidden = (pre_act * jax.nn.sigmoid(pre_act)).astype(jnp.bfloat16)
    return (values + jnp.dot(hidden, out_weight, preferred_element_type=jnp.float32)).astype(
        jnp.bfloat16
    )


def section_backward(stream, grad_rows, gain, in_weight, out_weight):
    values, inv_root, unit_rows, normed = normalize(stream, gain)
    pre_act = jnp.dot(normed, in_weight, preferred_element_type=jnp.float32)
    squash = jax.nn.sigmoid(pre_act)
    hidden = (pre_act * squash).astype(jnp.bfloat16)
    grad_hidden = lax.dot_general(
        grad_rows, out_weight, (((1,), (1,)), ((), ())), preferred_element_type=jnp.float32
    )
    grad_act = (grad_hidden * squash * (1.0 + pre_act * (1.0 - squash))).astype(jnp.bfloat16)
    grad_normed = lax.dot_general(
        grad_act, in_weight, (((1,), (1,)), ((), ())), preferred_element_type=jnp.float32
    ) * gain.astype(jnp.float32)
    inner_mean = jnp.mean(grad_normed * unit_rows, axis=-1, keepdims=True)
    grad_in = (
        grad_rows.astype(jnp.float32) + inv_root * (grad_normed - unit_rows * inner_mean)
    ).astype(jnp.bfloat16)
    return (grad_in, normed, grad_act, hidden)


def contract_rows(left, right):
    return lax.dot_general(
        left, right, (((0,), (0,)), ((), ())), preferred_element_type=jnp.float32
    )


def forward_tick(step_tick, position, is_first, incoming, saved_rows, inputs, weights):
    batch_count = inputs.shape[0]
    chain_index = step_tick - position
    active = jnp.logical_and(chain_index >= 0, chain_index < batch_count)
    batch_slot = jnp.clip(chain_index, 0, batch_count - 1)
    stream = jnp.where(is_first, lax.dynamic_index_in_dim(inputs, batch_slot, 0, False), incoming)
    kept_row = jnp.where(active, stream, lax.dynamic_index_in_dim(saved_rows, batch_slot, 0, False))
    saved_rows = lax.dynamic_update_index_in_dim(saved_rows, kept_row, batch_slot, 0)
    section_out = lax.cond(
        active, lambda rows_in: section_forward(rows_in, *weights), jnp.zeros_like, stream
    )
    return (section_out, saved_rows)


def backward_tick(
    step_tick, position, is_last, incoming, saved_rows, targets, weights, grad_sums, groups
):
    batch_count = targets.shape[0]
    chain_index = step_tick - position
    active = jnp.logical_and(chain_index >= 0, chain_index < batch_count)
    batch_slot = jnp.clip(chain_index, 0, batch_count - 1)
    grad_rows = jnp.where(
        is_last, lax.dynamic_index_in_dim(targets, batch_slot, 0, False), incoming
    )
    stream = lax.dynamic_index_in_dim(saved_rows, batch_slot, 0, False)
    half_group = batch_slot * groups // batch_count

    def run_section(operands):
        rows_in, grad_now, sums_now = operands
        grad_in, normed, grad_act, hidden = section_backward(rows_in, grad_now, *weights)
        sum_in, sum_out = sums_now
        sum_in = lax.dynamic_update_index_in_dim(
            sum_in,
            lax.dynamic_index_in_dim(sum_in, half_group, 0, False)
            + contract_rows(normed, grad_act),
            half_group,
            0,
        )
        sum_out = lax.dynamic_update_index_in_dim(
            sum_out,
            lax.dynamic_index_in_dim(sum_out, half_group, 0, False)
            + contract_rows(hidden, grad_now),
            half_group,
            0,
        )
        return (grad_in, (sum_in, sum_out))

    def skip_section(operands):
        return (jnp.zeros_like(operands[1]), operands[2])

    return lax.cond(active, run_section, skip_section, (stream, grad_rows, grad_sums))


def update(weight, grad, moment, variance, factor):
    scaled = factor * grad
    moment = BETA_ONE * moment + (1.0 - BETA_ONE) * scaled
    variance = BETA_TWO * variance + (1.0 - BETA_TWO) * scaled * scaled
    weight = weight.astype(jnp.float32) - STEP_RATE * moment / (jnp.sqrt(variance) + ADAM_EPS)
    return (weight[None], moment[None], variance[None])


def shards(
    stream_in,
    cotangent,
    norm_gain,
    weight_in,
    weight_out,
    moment_in,
    variance_in,
    moment_out,
    variance_out,
):
    section_count = lax.axis_size("section")
    section_place = lax.axis_index("section")
    micro_count = stream_in.shape[0]
    in_slice = weight_in[0]
    out_slice = weight_out[0]
    full_in_shape = (in_slice.shape[0] * lax.axis_size("dp"), in_slice.shape[1])
    full_out_shape = (out_slice.shape[0] * lax.axis_size("dp"), out_slice.shape[1])
    empty_stream = jnp.zeros(stream_in.shape[1:], jnp.bfloat16)
    is_first = section_place == 0
    is_last = section_place == section_count - 1
    whole_in, whole_out = (
        lax.all_gather(in_slice, "dp", axis=0, tiled=True),
        lax.all_gather(out_slice, "dp", axis=0, tiled=True),
    )
    own_layer = (norm_gain[0], whole_in, whole_out)
    tick_count = micro_count + section_count - 1

    def run_forward(step_tick, loop_state):
        incoming, saved_rows = loop_state
        section_out, saved_rows = forward_tick(
            step_tick, section_place, is_first, incoming, saved_rows, stream_in, own_layer
        )
        return (from_behind(section_out, "section", 1), saved_rows)

    _, saved_rows = lax.fori_loop(
        0, tick_count, run_forward, (empty_stream, jnp.zeros_like(stream_in))
    )
    start_sums = (
        jnp.zeros((2,) + full_in_shape, jnp.float32),
        jnp.zeros((2,) + full_out_shape, jnp.float32),
    )

    def run_backward(step_tick, loop_state):
        incoming, grad_sums = loop_state
        grad_in, grad_sums = backward_tick(
            step_tick,
            section_count - 1 - section_place,
            is_last,
            incoming,
            saved_rows,
            cotangent,
            own_layer,
            grad_sums,
            2,
        )
        return (from_behind(grad_in, "section", -1), grad_sums)

    _, (stacked_in, stacked_out) = lax.fori_loop(
        0, tick_count, run_backward, (empty_stream, start_sums)
    )
    reduced_in, reduced_out = (
        lax.psum_scatter(
            stacked_in.astype(jnp.bfloat16), "dp", scatter_dimension=1, tiled=True
        ).astype(jnp.float32),
        lax.psum_scatter(
            stacked_out.astype(jnp.bfloat16), "dp", scatter_dimension=1, tiled=True
        ).astype(jnp.float32),
    )
    grad_w_in = reduced_in[0] + reduced_in[1]
    grad_w_out = reduced_out[0] + reduced_out[1]
    local_sum = jnp.sum(grad_w_in * grad_w_in) + jnp.sum(grad_w_out * grad_w_out)
    norm_total = lax.psum(local_sum, ("section", "dp"))
    count_all = 2.0 * E * R * section_count
    factor = jnp.minimum(1.0, lax.rsqrt(norm_total / count_all + CLIP_EPS))
    new_in, new_moment_in, new_variance_in = update(
        in_slice, grad_w_in, moment_in[0], variance_in[0], factor
    )
    new_out, new_moment_out, new_variance_out = update(
        out_slice, grad_w_out, moment_out[0], variance_out[0], factor
    )
    return (new_in, new_moment_in, new_variance_in, new_out, new_moment_out, new_variance_out)


MESH = pl.DeviceIdType.MESH
CORES = 2


def dot(left, right, left_dim, right_dim):
    return lax.dot_general(
        left, right, (((left_dim,), (right_dim,)), ((), ())), preferred_element_type=jnp.float32
    )


def step_kernel(
    sections,
    planes,
    stream_any,
    cotangent_any,
    gain_any,
    weight_in_any,
    weight_out_any,
    grad_in_ref,
    grad_out_ref,
    factor_ref,
    rows_ref,
    gain_ref,
    weight_in_ref,
    weight_out_ref,
    cotangent_ref,
    piece_ref,
    gain_rows,
    weights,
    parts,
    from_core,
    chip_sums,
    from_planes,
    totals,
    owned,
    streams,
    pre_acts,
    roots,
    hiddens,
    sent,
    received,
    squares,
    squares_dp,
    squares_section,
    load_sems,
    piece_send,
    piece_recv,
    rail_send,
    relay_send,
    core_send,
    weight_recv,
    swap_send,
    swap_recv,
    part_send,
    part_recv,
    sum_send,
    sum_recv,
    total_send,
    total_recv,
    dp_send,
    dp_recv,
    section_send,
    section_recv,
):
    me_s = lax.axis_index("section")
    me_d = lax.axis_index("dp")
    plane = me_d // CORES
    core = lax.rem(me_d, CORES)
    other = 1 - core
    dp_count = planes * CORES
    tokens, width = cotangent_ref.shape
    channels = width * sections
    shard_rows, rank = weight_in_ref.shape
    tiles = width // 128
    in_rows = shard_rows // sections
    out_rows = weight_out_ref.shape[0]

    def section_peer(offset):
        return (lax.rem(me_s + offset, sections), me_d)

    def dp_peer(offset):
        return (me_s, lax.rem(me_d + offset, dp_count))

    def plane_peer(offset):
        return (me_s, lax.rem(plane + offset, planes) * CORES + core)

    partner = (me_s, plane * CORES + other)

    def send(source, target, send_sem, recv_sem, device):
        copy = pltpu.make_async_remote_copy(
            src_ref=source,
            dst_ref=target,
            send_sem=send_sem,
            recv_sem=recv_sem,
            device_id=device,
            device_id_type=MESH,
        )
        copy.start()
        return copy

    def remote(*copy):
        started.append(send(*copy))
        return started[-1]

    def landed(target, sem):
        pltpu.make_async_copy(target, target, sem).wait()

    started = []
    loads = [
        pltpu.make_async_copy(source, target, load_sems.at[i])
        for i, (source, target) in enumerate(
            (
                (gain_any, gain_ref),
                (weight_out_any, weight_out_ref),
                (weight_in_any, weight_in_ref),
                (stream_any, rows_ref.at[0]),
                (cotangent_any, rows_ref.at[1]),
            )
        )
    ]
    for copy in loads:
        copy.start()
    barrier = pltpu.get_barrier_semaphore()
    for offset in range(1, sections):
        pl.semaphore_signal(barrier, inc=1, device_id=section_peer(offset), device_id_type=MESH)
    for offset in range(1, dp_count):
        pl.semaphore_signal(barrier, inc=1, device_id=dp_peer(offset), device_id_type=MESH)

    loads[0].wait()
    gain_row = gain_ref[...].astype(jnp.float32)
    gain_tiles = channels // 128
    gains = [gain_row[:, 128 * t : 128 * (t + 1)] for t in range(gain_tiles)]
    gains = jnp.concatenate(gains + [jnp.zeros((128 - gain_tiles, 128), jnp.float32)], axis=0)
    gains = jnp.transpose(gains)
    lanes = lax.broadcasted_iota(jnp.int32, (128, 128), 1)
    for b in range(shard_rows // 64):
        half = me_d * (shard_rows // 64) + b
        column = jnp.sum(jnp.where(lanes == half // 2, gains, 0.0), axis=1, keepdims=True)
        odd = jnp.full((64, 1), lax.rem(half, 2), jnp.int32) == 1
        gain_rows[64 * b : 64 * (b + 1)] = jnp.broadcast_to(
            jnp.where(odd, column[64:], column[:64]), (64, 128)
        )

    def own_channels(rows, s):
        cuts = [
            rows[:, shard_rows * d + in_rows * s : shard_rows * d + in_rows * (s + 1)]
            for d in range(dp_count)
        ]
        return jnp.concatenate(cuts, axis=1)

    loads[1].wait()
    loads[2].wait()
    shard_out = weight_out_ref[...].astype(jnp.float32)
    for s in range(sections):
        own = slice(in_rows * s, in_rows * (s + 1))
        piece_ref[s, :in_rows] = (
            weight_in_ref[own].astype(jnp.float32) * gain_rows[own]
        ).astype(jnp.bfloat16)
        cut = own_channels(shard_out, s).astype(jnp.bfloat16)
        for t in range(tiles):
            piece_ref[s, in_rows + out_rows * t : in_rows + out_rows * (t + 1)] = cut[
                :, 128 * t : 128 * (t + 1)
            ]
    pl.semaphore_wait(barrier, sections + dp_count - 2)

    for offset in range(1, sections):
        target = section_peer(offset)
        remote(
            piece_ref.at[target[0]],
            weights.at[me_s, plane, core],
            piece_send.at[offset - 1],
            piece_recv.at[me_s],
            target,
        )
    pltpu.make_async_copy(
        piece_ref.at[me_s], weights.at[me_s, plane, core], piece_recv.at[me_s]
    ).start()
    far = planes - 1
    for place in range(sections):
        k = me_s if place == 0 else jnp.where(place - 1 < me_s, place - 1, place)
        landed(weights.at[k, plane, core], piece_recv.at[k])
        piece = weights.at[k, plane, core]
        for offset in range(1, planes):
            target = lax.rem(plane + offset, planes)

            @pl.when((target - plane != far) & (plane - target != far))
            def _():
                send(
                    piece,
                    piece,
                    rail_send.at[k, offset - 1],
                    weight_recv.at[k, plane, core],
                    (me_s, target * CORES + core),
                )

        remote(piece, piece, core_send.at[k, 0], weight_recv.at[k, plane, core], partner)

    def pass_on(k):
        for offset in range(1, planes):
            source = lax.rem(plane + offset, planes)
            piece = weights.at[k, source, core]
            landed(piece, weight_recv.at[k, source, core])

            @pl.when((source == 0) & (plane == far - 1))
            def _():
                send(
                    piece,
                    piece,
                    relay_send.at[k, 0],
                    weight_recv.at[k, source, core],
                    (me_s, far * CORES + core),
                )

            @pl.when((source == far) & (plane == 1))
            def _():
                send(
                    piece, piece, relay_send.at[k, 1], weight_recv.at[k, source, core], (me_s, core)
                )

            remote(
                piece, piece, core_send.at[k, offset], weight_recv.at[k, source, core], partner
            )

    def arrive(k):
        for source in range(planes):
            landed(weights.at[k, source, other], weight_recv.at[k, source, other])

    def weight_in(k):
        return weights[k, :, :, :in_rows, :].reshape(width, rank)

    def weight_out(k):
        columns = [
            weights[k, :, :, in_rows + out_rows * t : in_rows + out_rows * (t + 1), :].reshape(
                rank, 128
            )
            for t in range(tiles)
        ]
        return jnp.concatenate(columns, axis=1)

    def swap(slot, rows):
        return [
            remote(
                sent.at[slot, pl.ds(0, rows)],
                received.at[slot, offset - 1, pl.ds(0, rows)],
                swap_send.at[slot, offset - 1],
                swap_recv.at[slot, offset - 1],
                section_peer(offset),
            )
            for offset in range(1, sections)
        ]

    def spread(column):
        return jnp.transpose(jnp.broadcast_to(column, (tokens, tokens)))[:8]

    loads[3].wait()
    loads[4].wait()
    for s in range(sections):

        @pl.when(me_s == s)
        def _():
            streams[0] = own_channels(rows_ref[0].astype(jnp.float32), s).astype(jnp.bfloat16)
            cotangent_ref[...] = own_channels(rows_ref[1].astype(jnp.float32), s).astype(
                jnp.bfloat16
            )

    pass_on(0)
    grad_partial = None
    for k in range(sections):
        last = k == sections - 1
        arrive(k)
        values = streams[k]
        wide = values.astype(jnp.float32)
        partial = dot(values, weight_in(k), 1, 0)
        square = spread(jnp.sum(wide * wide, axis=1, keepdims=True))
        square_hi = square.astype(jnp.bfloat16).astype(jnp.float32)
        sent[k, :tokens] = partial.astype(jnp.bfloat16)
        sent[k, tokens : tokens + 16] = jnp.concatenate(
            [square_hi, square - square_hi], axis=0
        ).astype(jnp.bfloat16)
        rows = tokens + 16
        if last:
            grad_partial = dot(cotangent_ref[...], weight_out(k), 1, 1)
            sent[k, rows : rows + tokens] = grad_partial.astype(jnp.bfloat16)
            rows = rows + tokens
        copies = swap(k, rows)
        if not last:
            pass_on(k + 1)
        for offset, copy in enumerate(copies):
            copy.wait_recv()
            arrived = received[k, offset, : tokens + 16].astype(jnp.float32)
            partial = partial + arrived[:tokens]
            square = square + arrived[tokens : tokens + 8] + arrived[tokens + 8 : tokens + 16]
            if last:
                grad_partial = grad_partial + received[
                    k, offset, tokens + 16 : rows
                ].astype(jnp.float32)
        mean = jnp.transpose(jnp.broadcast_to(square[:1], (tokens, tokens))) / channels
        root = lax.rsqrt(mean + NORM_EPS)
        pre_act = partial * root[:, :rank]
        hidden = (pre_act * jax.nn.sigmoid(pre_act)).astype(jnp.bfloat16)
        pre_acts[k] = pre_act
        roots[k] = root
        hiddens[k] = hidden
        if not last:
            streams[k + 1] = (wide + dot(hidden, weight_out(k), 1, 0)).astype(jnp.bfloat16)

    def swap_part(unit):
        remote(
            parts.at[unit, :, other],
            from_core.at[unit],
            part_send.at[unit],
            part_recv.at[unit],
            partner,
        )

    def make_in_part(k, grad_act):
        scaled = (grad_act * roots[k][:, :rank]).astype(jnp.bfloat16)
        part = dot(streams[k], scaled, 0, 0).astype(jnp.bfloat16)
        parts[2 * k] = part.reshape(planes, CORES, in_rows, rank)
        swap_part(2 * k)

    def make_out_part(k, grad_rounded):
        part = dot(hiddens[k], grad_rounded, 0, 0).astype(jnp.bfloat16)
        for t in range(tiles):
            parts[2 * k + 1, :, :, out_rows * t : out_rows * (t + 1), :] = part[
                :, 128 * t : 128 * (t + 1)
            ].reshape(planes, CORES, out_rows, 128)
        swap_part(2 * k + 1)

    def send_chip_sums(unit):
        landed(from_core.at[unit], part_recv.at[unit])
        chip_sums[unit] = (
            parts[unit, :, core].astype(jnp.float32) + from_core[unit].astype(jnp.float32)
        ).astype(jnp.bfloat16)
        for offset in range(1, planes):
            remote(
                chip_sums.at[unit, lax.rem(plane + offset, planes)],
                from_planes.at[unit, offset - 1],
                sum_send.at[unit, offset - 1],
                sum_recv.at[unit, offset - 1],
                plane_peer(offset),
            )

    def send_total(unit):
        k, kind = unit // 2, unit % 2
        total = chip_sums[unit, plane].astype(jnp.float32)
        for offset in range(1, planes):
            landed(from_planes.at[unit, offset - 1], sum_recv.at[unit, offset - 1])
            total = total + from_planes[unit, offset - 1].astype(jnp.float32)
        totals[unit] = total.astype(jnp.bfloat16)
        own = owned.at[kind, me_s]

        @pl.when(me_s != k)
        def _():
            send(
                totals.at[unit], own, total_send.at[unit], total_recv.at[kind, me_s], (k, me_d)
            )

        @pl.when(me_s == k)
        def _():
            pltpu.make_async_copy(totals.at[unit], own, total_recv.at[kind, me_s]).start()

    def units_of(k):
        units = [2 * k] + ([2 * k - 1] if k > 0 else [])
        return [2 * k + 1] + units if k == sections - 1 else units

    grad = cotangent_ref[...].astype(jnp.float32)
    for k in reversed(range(sections)):
        slot = 2 * sections - 1 - k
        pre_act = pre_acts[k]
        root = roots[k]
        squash = jax.nn.sigmoid(pre_act)
        grad_act = grad_partial * squash * (1.0 + pre_act * (1.0 - squash))
        act = grad_act.astype(jnp.bfloat16)
        copies = []
        if k > 0:
            column = root[:, :1]
            inner_mean = jnp.sum(grad_act * pre_act, axis=1, keepdims=True) / channels
            grad_normed = dot(act, weight_in(k), 1, 1)
            grad = grad + column * (
                grad_normed - streams[k].astype(jnp.float32) * (column * inner_mean)
            )
            grad_rounded = grad.astype(jnp.bfloat16)
            grad_partial = dot(grad_rounded, weight_out(k - 1), 1, 1)
            sent[slot, :tokens] = grad_partial.astype(jnp.bfloat16)
            copies = swap(slot, tokens)
        if k == sections - 1:
            make_out_part(k, cotangent_ref[...])
        make_in_part(k, grad_act)
        if k > 0:
            make_out_part(k - 1, grad_rounded)
        if k == 0 and sections > 2:
            for unit in units_of(k + 2):
                send_total(unit)
        for unit in units_of(k):
            send_chip_sums(unit)
        if 0 < k < sections - 2:
            for unit in units_of(k + 2):
                send_total(unit)
        for offset, copy in enumerate(copies):
            copy.wait_recv()
            grad_partial = grad_partial + received[slot, offset, :tokens].astype(jnp.float32)
    for k in (1, 0):
        for unit in units_of(k):
            send_total(unit)

    square = jnp.zeros((8, 128), jnp.float32)
    out_parts = []
    for s in range(sections):
        landed(owned.at[1, s], total_recv.at[1, s])
        landed(owned.at[0, s], total_recv.at[0, s])
        own = slice(in_rows * s, in_rows * (s + 1))
        in_part = owned[0, s].astype(jnp.float32) * gain_rows[own]
        out_part = owned[1, s].astype(jnp.float32)
        grad_in_ref[own] = in_part
        out_parts.append(
            jnp.concatenate(
                [out_part[out_rows * t : out_rows * (t + 1)] for t in range(tiles)], axis=1
            )
        )
        square = square + jnp.sum((in_part * in_part).reshape(-1, 8, 128), axis=0)
        square = square + jnp.sum((out_part * out_part).reshape(-1, 8, 128), axis=0)
    squares[0] = square
    copies = [
        remote(
            squares.at[0],
            squares_dp.at[offset - 1],
            dp_send.at[offset - 1],
            dp_recv.at[offset - 1],
            dp_peer(offset),
        )
        for offset in range(1, dp_count)
    ]
    grad_out_ref[...] = jnp.concatenate(
        [
            out_parts[s][:, in_rows * d : in_rows * (d + 1)]
            for d in range(dp_count)
            for s in range(sections)
        ],
        axis=1,
    )
    for offset, copy in enumerate(copies):
        copy.wait_recv()
        square = square + squares_dp[offset]
    squares[1] = square
    copies = [
        remote(
            squares.at[1],
            squares_section.at[offset - 1],
            section_send.at[offset - 1],
            section_recv.at[offset - 1],
            section_peer(offset),
        )
        for offset in range(1, sections)
    ]
    for offset, copy in enumerate(copies):
        copy.wait_recv()
        square = square + squares_section[offset]
    count_all = 2.0 * channels * rank * sections
    norm_total = jnp.sum(square, keepdims=True)
    factor = jnp.minimum(1.0, lax.rsqrt(norm_total / count_all + CLIP_EPS))
    factor_ref[...] = jnp.broadcast_to(factor, factor_ref.shape)

    for copy in started:
        copy.wait_send()
    for k in range(sections):
        for offset in range(1, planes):
            target = lax.rem(plane + offset, planes)

            @pl.when((target - plane != far) & (plane - target != far))
            def _():
                landed(weights.at[k, plane, core], rail_send.at[k, offset - 1])

        @pl.when(plane == far - 1)
        def _():
            landed(weights.at[k, 0, core], relay_send.at[k, 0])

        @pl.when(plane == 1)
        def _():
            landed(weights.at[k, far, core], relay_send.at[k, 1])

        @pl.when(me_s != k)
        def _():
            landed(totals.at[2 * k], total_send.at[2 * k])
            landed(totals.at[2 * k + 1], total_send.at[2 * k + 1])


def adam_kernel(factor_any, grad_in_any, grad_out_any, *refs):
    inputs, outputs, loaded, sems = refs[:6], refs[6:12], refs[12:15], refs[15]
    loads = [
        pltpu.make_async_copy(source, target, sems.at[i])
        for i, (source, target) in enumerate(
            zip((factor_any, grad_in_any, grad_out_any), loaded)
        )
    ]
    for copy in loads:
        copy.start()
    for copy in loads:
        copy.wait()
    factor = loaded[0][:1, :1]
    for place in (0, 1):
        weight, moment, variance = inputs[3 * place : 3 * place + 3]
        grad = loaded[place + 1][...]
        results = update(weight[0], grad, moment[0], variance[0], factor)
        for ref, result in zip(outputs[3 * place : 3 * place + 3], results):
            ref[...] = result


def fast_shards(
    stream_in,
    cotangent,
    norm_gain,
    weight_in,
    weight_out,
    moment_in,
    variance_in,
    moment_out,
    variance_out,
):
    sections = lax.axis_size("section")
    dp_count = lax.axis_size("dp")
    planes = dp_count // CORES
    channels = stream_in.shape[-1]
    tokens = stream_in.shape[0] * stream_in.shape[1]
    shard_rows, rank = weight_in.shape[1:]
    if tokens != rank:
        return shards(
            stream_in,
            cotangent,
            norm_gain,
            weight_in,
            weight_out,
            moment_in,
            variance_in,
            moment_out,
            variance_out,
        )
    out_rows = weight_out.shape[1]
    in_rows = shard_rows // sections
    width = channels // sections
    tiles = width // 128
    piece_rows = in_rows + out_rows * tiles

    narrow, full = jnp.bfloat16, jnp.float32
    slots = 2 * sections - 1
    units = 2 * sections
    dma = pltpu.SemaphoreType.DMA
    vmem = pl.BlockSpec(memory_space=pltpu.VMEM)
    grad_w_in, grad_w_out, factor = pl.pallas_call(
        functools.partial(step_kernel, sections, planes),
        out_shape=(
            jax.ShapeDtypeStruct((shard_rows, rank), full),
            jax.ShapeDtypeStruct((out_rows, channels), full),
            jax.ShapeDtypeStruct((8, 128), full),
        ),
        in_specs=[pl.BlockSpec(memory_space=pl.ANY)] * 5,
        out_specs=(vmem, vmem, vmem),
        scratch_shapes=[
            pltpu.VMEM((2, tokens, channels), narrow),
            pltpu.VMEM((1, channels), narrow),
            pltpu.VMEM((shard_rows, rank), narrow),
            pltpu.VMEM((out_rows, channels), narrow),
            pltpu.VMEM((tokens, width), narrow),
            pltpu.VMEM((sections, piece_rows, 128), narrow),
            pltpu.VMEM((shard_rows, 128), full),
            pltpu.VMEM((sections, planes, CORES, piece_rows, 128), narrow),
            pltpu.VMEM((units, planes, CORES, in_rows, 128), narrow),
            pltpu.VMEM((units, planes, in_rows, 128), narrow),
            pltpu.VMEM((units, planes, in_rows, 128), narrow),
            pltpu.VMEM((units, planes - 1, in_rows, 128), narrow),
            pltpu.VMEM((units, in_rows, 128), narrow),
            pltpu.VMEM((2, sections, in_rows, 128), narrow),
            pltpu.VMEM((sections, tokens, width), narrow),
            pltpu.VMEM((sections, tokens, rank), full),
            pltpu.VMEM((sections, tokens, tokens), full),
            pltpu.VMEM((sections, tokens, rank), narrow),
            pltpu.VMEM((slots, 2 * tokens + 16, rank), narrow),
            pltpu.VMEM((slots, sections - 1, 2 * tokens + 16, rank), narrow),
            pltpu.VMEM((2, 8, 128), full),
            pltpu.VMEM((dp_count - 1, 8, 128), full),
            pltpu.VMEM((sections - 1, 8, 128), full),
            dma((5,)),
            dma((sections - 1,)),
            dma((sections,)),
            dma((sections, planes - 1)),
            dma((sections, 2)),
            dma((sections, planes)),
            dma((sections, planes, CORES)),
            dma((slots, sections - 1)),
            dma((slots, sections - 1)),
            dma((units,)),
            dma((units,)),
            dma((units, planes - 1)),
            dma((units, planes - 1)),
            dma((units,)),
            dma((2, sections)),
            dma((dp_count - 1,)),
            dma((dp_count - 1,)),
            dma((sections - 1,)),
            dma((sections - 1,)),
        ],
        compiler_params=pltpu.CompilerParams(
            collective_id=0, has_side_effects=True, vmem_limit_bytes=60 * 1024 * 1024
        ),
    )(
        stream_in.reshape(tokens, channels),
        cotangent.reshape(tokens, channels),
        norm_gain,
        weight_in[0],
        weight_out[0],
    )
    in_shape = jax.ShapeDtypeStruct(moment_in.shape, full)
    out_shape = jax.ShapeDtypeStruct(moment_out.shape, full)
    return pl.pallas_call(
        adam_kernel,
        out_shape=(in_shape,) * 3 + (out_shape,) * 3,
        in_specs=[pl.BlockSpec(memory_space=pl.ANY)] * 3 + [vmem] * 6,
        out_specs=(vmem,) * 6,
        scratch_shapes=[
            pltpu.VMEM((8, 128), full),
            pltpu.VMEM((shard_rows, rank), full),
            pltpu.VMEM((out_rows, channels), full),
            dma((3,)),
        ],
        compiler_params=pltpu.CompilerParams(vmem_limit_bytes=16 * 1024 * 1024),
    )(
        factor,
        grad_w_in,
        grad_w_out,
        weight_in,
        moment_in,
        variance_in,
        weight_out,
        moment_out,
        variance_out,
    )


def aligned(sections, dp_count):
    width, in_rows, out_rows = E // sections, E // (sections * dp_count), R // dp_count
    return (
        sections > 1
        and dp_count % CORES == 0
        and dp_count > 2 * CORES
        and width % 128 == 0
        and in_rows % 16 == 0
        and out_rows % 16 == 0
        and R == 128
        and E <= 128 * 128
        and E % (64 * dp_count) == 0
    )


def solution(mesh):
    fast = aligned(mesh.shape["section"], mesh.shape["dp"])
    return jax.shard_map(
        fast_shards if fast else shards,
        mesh=mesh,
        in_specs=(
            P(None, "dp", None),
            P(None, "dp", None),
            P("section", None),
            P("section", "dp", None),
            P("section", "dp", None),
            P("section", "dp", None),
            P("section", "dp", None),
            P("section", "dp", None),
            P("section", "dp", None),
        ),
        out_specs=(
            P("section", "dp", None),
            P("section", "dp", None),
            P("section", "dp", None),
            P("section", "dp", None),
            P("section", "dp", None),
            P("section", "dp", None),
        ),
        check_vma=False,
    )
```

```python
import functools

import jax
import jax.numpy as jnp
from jax import lax
from jax.experimental import pallas as pl
from jax.experimental.pallas import tpu as pltpu
from jax.sharding import PartitionSpec as P

E = 3584
R = 128


NORM_EPS = 1e-06
BETA_ONE = 0.9
BETA_TWO = 0.95
STEP_RATE = 0.01
ADAM_EPS = 1e-08
CLIP_EPS = 1e-06


def from_behind(x, axis, by):
    count = lax.axis_size(axis)
    pairs = [(i, i + by) for i in range(count) if 0 <= i + by < count]
    return lax.ppermute(x, axis, pairs)


def normalize(stream, gain):
    values = stream.astype(jnp.float32)
    inv_root = lax.rsqrt(jnp.mean(values * values, axis=-1, keepdims=True) + NORM_EPS)
    unit_rows = values * inv_root
    normed = (unit_rows * gain.astype(jnp.float32)).astype(jnp.bfloat16)
    return (values, inv_root, unit_rows, normed)


def section_forward(stream, gain, in_weight, out_weight):
    values, inv_root, unit_rows, normed = normalize(stream, gain)
    pre_act = jnp.dot(normed, in_weight, preferred_element_type=jnp.float32)
    hidden = (pre_act * jax.nn.sigmoid(pre_act)).astype(jnp.bfloat16)
    return (values + jnp.dot(hidden, out_weight, preferred_element_type=jnp.float32)).astype(
        jnp.bfloat16
    )


def section_backward(stream, grad_rows, gain, in_weight, out_weight):
    values, inv_root, unit_rows, normed = normalize(stream, gain)
    pre_act = jnp.dot(normed, in_weight, preferred_element_type=jnp.float32)
    squash = jax.nn.sigmoid(pre_act)
    hidden = (pre_act * squash).astype(jnp.bfloat16)
    grad_hidden = lax.dot_general(
        grad_rows, out_weight, (((1,), (1,)), ((), ())), preferred_element_type=jnp.float32
    )
    grad_act = (grad_hidden * squash * (1.0 + pre_act * (1.0 - squash))).astype(jnp.bfloat16)
    grad_normed = lax.dot_general(
        grad_act, in_weight, (((1,), (1,)), ((), ())), preferred_element_type=jnp.float32
    ) * gain.astype(jnp.float32)
    inner_mean = jnp.mean(grad_normed * unit_rows, axis=-1, keepdims=True)
    grad_in = (
        grad_rows.astype(jnp.float32) + inv_root * (grad_normed - unit_rows * inner_mean)
    ).astype(jnp.bfloat16)
    return (grad_in, normed, grad_act, hidden)


def contract_rows(left, right):
    return lax.dot_general(
        left, right, (((0,), (0,)), ((), ())), preferred_element_type=jnp.float32
    )


def forward_tick(step_tick, position, is_first, incoming, saved_rows, inputs, weights):
    batch_count = inputs.shape[0]
    chain_index = step_tick - position
    active = jnp.logical_and(chain_index >= 0, chain_index < batch_count)
    batch_slot = jnp.clip(chain_index, 0, batch_count - 1)
    stream = jnp.where(is_first, lax.dynamic_index_in_dim(inputs, batch_slot, 0, False), incoming)
    kept_row = jnp.where(active, stream, lax.dynamic_index_in_dim(saved_rows, batch_slot, 0, False))
    saved_rows = lax.dynamic_update_index_in_dim(saved_rows, kept_row, batch_slot, 0)
    section_out = lax.cond(
        active, lambda rows_in: section_forward(rows_in, *weights), jnp.zeros_like, stream
    )
    return (section_out, saved_rows)


def backward_tick(
    step_tick, position, is_last, incoming, saved_rows, targets, weights, grad_sums, groups
):
    batch_count = targets.shape[0]
    chain_index = step_tick - position
    active = jnp.logical_and(chain_index >= 0, chain_index < batch_count)
    batch_slot = jnp.clip(chain_index, 0, batch_count - 1)
    grad_rows = jnp.where(
        is_last, lax.dynamic_index_in_dim(targets, batch_slot, 0, False), incoming
    )
    stream = lax.dynamic_index_in_dim(saved_rows, batch_slot, 0, False)
    half_group = batch_slot * groups // batch_count

    def run_section(operands):
        rows_in, grad_now, sums_now = operands
        grad_in, normed, grad_act, hidden = section_backward(rows_in, grad_now, *weights)
        sum_in, sum_out = sums_now
        sum_in = lax.dynamic_update_index_in_dim(
            sum_in,
            lax.dynamic_index_in_dim(sum_in, half_group, 0, False)
            + contract_rows(normed, grad_act),
            half_group,
            0,
        )
        sum_out = lax.dynamic_update_index_in_dim(
            sum_out,
            lax.dynamic_index_in_dim(sum_out, half_group, 0, False)
            + contract_rows(hidden, grad_now),
            half_group,
            0,
        )
        return (grad_in, (sum_in, sum_out))

    def skip_section(operands):
        return (jnp.zeros_like(operands[1]), operands[2])

    return lax.cond(active, run_section, skip_section, (stream, grad_rows, grad_sums))


def update(weight, grad, moment, variance, factor):
    scaled = factor * grad
    moment = BETA_ONE * moment + (1.0 - BETA_ONE) * scaled
    variance = BETA_TWO * variance + (1.0 - BETA_TWO) * scaled * scaled
    weight = weight.astype(jnp.float32) - STEP_RATE * moment / (jnp.sqrt(variance) + ADAM_EPS)
    return (weight[None], moment[None], variance[None])


def shards(
    stream_in,
    cotangent,
    norm_gain,
    weight_in,
    weight_out,
    moment_in,
    variance_in,
    moment_out,
    variance_out,
):
    section_count = lax.axis_size("section")
    section_place = lax.axis_index("section")
    micro_count = stream_in.shape[0]
    in_slice = weight_in[0]
    out_slice = weight_out[0]
    full_in_shape = (in_slice.shape[0] * lax.axis_size("dp"), in_slice.shape[1])
    full_out_shape = (out_slice.shape[0] * lax.axis_size("dp"), out_slice.shape[1])
    empty_stream = jnp.zeros(stream_in.shape[1:], jnp.bfloat16)
    is_first = section_place == 0
    is_last = section_place == section_count - 1
    whole_in, whole_out = (
        lax.all_gather(in_slice, "dp", axis=0, tiled=True),
        lax.all_gather(out_slice, "dp", axis=0, tiled=True),
    )
    own_layer = (norm_gain[0], whole_in, whole_out)
    tick_count = micro_count + section_count - 1

    def run_forward(step_tick, loop_state):
        incoming, saved_rows = loop_state
        section_out, saved_rows = forward_tick(
            step_tick, section_place, is_first, incoming, saved_rows, stream_in, own_layer
        )
        return (from_behind(section_out, "section", 1), saved_rows)

    _, saved_rows = lax.fori_loop(
        0, tick_count, run_forward, (empty_stream, jnp.zeros_like(stream_in))
    )
    start_sums = (
        jnp.zeros((2,) + full_in_shape, jnp.float32),
        jnp.zeros((2,) + full_out_shape, jnp.float32),
    )

    def run_backward(step_tick, loop_state):
        incoming, grad_sums = loop_state
        grad_in, grad_sums = backward_tick(
            step_tick,
            section_count - 1 - section_place,
            is_last,
            incoming,
            saved_rows,
            cotangent,
            own_layer,
            grad_sums,
            2,
        )
        return (from_behind(grad_in, "section", -1), grad_sums)

    _, (stacked_in, stacked_out) = lax.fori_loop(
        0, tick_count, run_backward, (empty_stream, start_sums)
    )
    reduced_in, reduced_out = (
        lax.psum_scatter(
            stacked_in.astype(jnp.bfloat16), "dp", scatter_dimension=1, tiled=True
        ).astype(jnp.float32),
        lax.psum_scatter(
            stacked_out.astype(jnp.bfloat16), "dp", scatter_dimension=1, tiled=True
        ).astype(jnp.float32),
    )
    grad_w_in = reduced_in[0] + reduced_in[1]
    grad_w_out = reduced_out[0] + reduced_out[1]
    local_sum = jnp.sum(grad_w_in * grad_w_in) + jnp.sum(grad_w_out * grad_w_out)
    norm_total = lax.psum(local_sum, ("section", "dp"))
    count_all = 2.0 * E * R * section_count
    factor = jnp.minimum(1.0, lax.rsqrt(norm_total / count_all + CLIP_EPS))
    new_in, new_moment_in, new_variance_in = update(
        in_slice, grad_w_in, moment_in[0], variance_in[0], factor
    )
    new_out, new_moment_out, new_variance_out = update(
        out_slice, grad_w_out, moment_out[0], variance_out[0], factor
    )
    return (new_in, new_moment_in, new_variance_in, new_out, new_moment_out, new_variance_out)


MESH = pl.DeviceIdType.MESH
CORES = 2


def dot(left, right, left_dim, right_dim):
    return lax.dot_general(
        left, right, (((left_dim,), (right_dim,)), ((), ())), preferred_element_type=jnp.float32
    )


def step_kernel(
    sections,
    planes,
    stream_any,
    cotangent_any,
    gain_any,
    weight_in_any,
    weight_out_any,
    grad_in_ref,
    grad_out_ref,
    factor_ref,
    rows_ref,
    gain_ref,
    weight_in_ref,
    weight_out_ref,
    cotangent_ref,
    piece_ref,
    gain_rows,
    gain_sent,
    gain_of,
    weights,
    parts,
    from_core,
    chip_sums,
    from_planes,
    totals,
    owned,
    streams,
    pre_acts,
    roots,
    hiddens,
    sent,
    received,
    squares,
    squares_dp,
    squares_section,
    load_sems,
    gain_send,
    gain_recv,
    piece_send,
    piece_recv,
    rail_send,
    relay_send,
    core_send,
    weight_recv,
    swap_send,
    swap_recv,
    part_send,
    part_recv,
    sum_send,
    sum_recv,
    total_send,
    total_recv,
    dp_send,
    dp_recv,
    section_send,
    section_recv,
):
    me_s = lax.axis_index("section")
    me_d = lax.axis_index("dp")
    plane = me_d // CORES
    core = lax.rem(me_d, CORES)
    other = 1 - core
    dp_count = planes * CORES
    tokens, width = cotangent_ref.shape
    channels = width * sections
    shard_rows, rank = weight_in_ref.shape
    tiles = width // 128
    in_rows = shard_rows // sections
    out_rows = weight_out_ref.shape[0]

    def section_peer(offset):
        return (lax.rem(me_s + offset, sections), me_d)

    def dp_peer(offset):
        return (me_s, lax.rem(me_d + offset, dp_count))

    def plane_peer(offset):
        return (me_s, lax.rem(plane + offset, planes) * CORES + core)

    partner = (me_s, plane * CORES + other)

    def send(source, target, send_sem, recv_sem, device):
        copy = pltpu.make_async_remote_copy(
            src_ref=source,
            dst_ref=target,
            send_sem=send_sem,
            recv_sem=recv_sem,
            device_id=device,
            device_id_type=MESH,
        )
        copy.start()
        return copy

    def remote(*copy):
        started.append(send(*copy))
        return started[-1]

    def landed(target, sem):
        pltpu.make_async_copy(target, target, sem).wait()

    started = []
    loads = [
        pltpu.make_async_copy(source, target, load_sems.at[i])
        for i, (source, target) in enumerate(
            (
                (gain_any, gain_ref),
                (weight_out_any, weight_out_ref),
                (weight_in_any, weight_in_ref),
                (stream_any, rows_ref.at[0]),
                (cotangent_any, rows_ref.at[1]),
            )
        )
    ]
    for copy in loads:
        copy.start()
    barrier = pltpu.get_barrier_semaphore()
    for offset in range(1, sections):
        pl.semaphore_signal(barrier, inc=1, device_id=section_peer(offset), device_id_type=MESH)
    for offset in range(1, dp_count):
        pl.semaphore_signal(barrier, inc=1, device_id=dp_peer(offset), device_id_type=MESH)

    loads[0].wait()
    gain_row = gain_ref[...].astype(jnp.float32)
    gain_tiles = channels // 128
    gains = [gain_row[:, 128 * t : 128 * (t + 1)] for t in range(gain_tiles)]
    gains = jnp.concatenate(gains + [jnp.zeros((128 - gain_tiles, 128), jnp.float32)], axis=0)
    gains = jnp.transpose(gains)
    lanes = lax.broadcasted_iota(jnp.int32, (128, 128), 1)
    for b in range(shard_rows // 64):
        half = me_d * (shard_rows // 64) + b
        column = jnp.sum(jnp.where(lanes == half // 2, gains, 0.0), axis=1, keepdims=True)
        odd = jnp.full((64, 1), lax.rem(half, 2), jnp.int32) == 1
        gain_rows[64 * b : 64 * (b + 1)] = jnp.broadcast_to(
            jnp.where(odd, column[64:], column[:64]), (64, 128)
        )

    def own_channels(rows, s):
        cuts = [
            rows[:, shard_rows * d + in_rows * s : shard_rows * d + in_rows * (s + 1)]
            for d in range(dp_count)
        ]
        return jnp.concatenate(cuts, axis=1)

    loads[1].wait()
    loads[2].wait()
    shard_out = weight_out_ref[...].astype(jnp.float32)
    for s in range(sections):
        own = slice(in_rows * s, in_rows * (s + 1))
        piece_ref[s, :in_rows] = (
            weight_in_ref[own].astype(jnp.float32) * gain_rows[own]
        ).astype(jnp.bfloat16)
        cut = own_channels(shard_out, s).astype(jnp.bfloat16)
        for t in range(tiles):
            piece_ref[s, in_rows + out_rows * t : in_rows + out_rows * (t + 1)] = cut[
                :, 128 * t : 128 * (t + 1)
            ]
    pl.semaphore_wait(barrier, sections + dp_count - 2)

    for offset in range(1, sections):
        target = section_peer(offset)
        remote(
            piece_ref.at[target[0]],
            weights.at[me_s, plane, core],
            piece_send.at[offset - 1],
            piece_recv.at[me_s],
            target,
        )
    pltpu.make_async_copy(
        piece_ref.at[me_s], weights.at[me_s, plane, core], piece_recv.at[me_s]
    ).start()
    far = planes - 1
    for place in range(sections):
        k = me_s if place == 0 else jnp.where(place - 1 < me_s, place - 1, place)
        landed(weights.at[k, plane, core], piece_recv.at[k])
        piece = weights.at[k, plane, core]
        for offset in range(1, planes):
            target = lax.rem(plane + offset, planes)

            @pl.when((target - plane != far) & (plane - target != far))
            def _():
                send(
                    piece,
                    piece,
                    rail_send.at[k, offset - 1],
                    weight_recv.at[k, plane, core],
                    (me_s, target * CORES + core),
                )

        remote(piece, piece, core_send.at[k, 0], weight_recv.at[k, plane, core], partner)

    for s in range(sections):
        gain_sent[s] = gain_rows[in_rows * s : in_rows * (s + 1)].astype(jnp.bfloat16)
    for offset in range(1, sections):
        target = section_peer(offset)
        remote(
            gain_sent.at[target[0]],
            gain_of.at[me_s],
            gain_send.at[offset - 1],
            gain_recv.at[me_s],
            target,
        )
    pltpu.make_async_copy(gain_sent.at[me_s], gain_of.at[me_s], gain_recv.at[me_s]).start()

    def pass_on(k):
        for offset in range(1, planes):
            source = lax.rem(plane + offset, planes)
            piece = weights.at[k, source, core]
            landed(piece, weight_recv.at[k, source, core])

            @pl.when((source == 0) & (plane == far - 1))
            def _():
                send(
                    piece,
                    piece,
                    relay_send.at[k, 0],
                    weight_recv.at[k, source, core],
                    (me_s, far * CORES + core),
                )

            @pl.when((source == far) & (plane == 1))
            def _():
                send(
                    piece, piece, relay_send.at[k, 1], weight_recv.at[k, source, core], (me_s, core)
                )

            remote(
                piece, piece, core_send.at[k, offset], weight_recv.at[k, source, core], partner
            )

    def arrive(k):
        for source in range(planes):
            landed(weights.at[k, source, other], weight_recv.at[k, source, other])

    def weight_in(k):
        return weights[k, :, :, :in_rows, :].reshape(width, rank)

    def weight_out(k):
        columns = [
            weights[k, :, :, in_rows + out_rows * t : in_rows + out_rows * (t + 1), :].reshape(
                rank, 128
            )
            for t in range(tiles)
        ]
        return jnp.concatenate(columns, axis=1)

    def swap(slot, rows):
        return [
            remote(
                sent.at[slot, pl.ds(0, rows)],
                received.at[slot, offset - 1, pl.ds(0, rows)],
                swap_send.at[slot, offset - 1],
                swap_recv.at[slot, offset - 1],
                section_peer(offset),
            )
            for offset in range(1, sections)
        ]

    def spread(column):
        return jnp.transpose(jnp.broadcast_to(column, (tokens, tokens)))[:8]

    loads[3].wait()
    loads[4].wait()
    for s in range(sections):

        @pl.when(me_s == s)
        def _():
            streams[0] = own_channels(rows_ref[0].astype(jnp.float32), s).astype(jnp.bfloat16)
            cotangent_ref[...] = own_channels(rows_ref[1].astype(jnp.float32), s).astype(
                jnp.bfloat16
            )

    pass_on(0)
    grad_partial = None
    for k in range(sections):
        last = k == sections - 1
        arrive(k)
        values = streams[k]
        wide = values.astype(jnp.float32)
        partial = dot(values, weight_in(k), 1, 0)
        square = spread(jnp.sum(wide * wide, axis=1, keepdims=True))
        square_hi = square.astype(jnp.bfloat16).astype(jnp.float32)
        sent[k, :tokens] = partial.astype(jnp.bfloat16)
        sent[k, tokens : tokens + 16] = jnp.concatenate(
            [square_hi, square - square_hi], axis=0
        ).astype(jnp.bfloat16)
        rows = tokens + 16
        if last:
            grad_partial = dot(cotangent_ref[...], weight_out(k), 1, 1)
            sent[k, rows : rows + tokens] = grad_partial.astype(jnp.bfloat16)
            rows = rows + tokens
        copies = swap(k, rows)
        if not last:
            pass_on(k + 1)
        for offset, copy in enumerate(copies):
            copy.wait_recv()
            arrived = received[k, offset, : tokens + 16].astype(jnp.float32)
            partial = partial + arrived[:tokens]
            square = square + arrived[tokens : tokens + 8] + arrived[tokens + 8 : tokens + 16]
            if last:
                grad_partial = grad_partial + received[
                    k, offset, tokens + 16 : rows
                ].astype(jnp.float32)
        mean = jnp.transpose(jnp.broadcast_to(square[:1], (tokens, tokens))) / channels
        root = lax.rsqrt(mean + NORM_EPS)
        pre_act = partial * root[:, :rank]
        hidden = (pre_act * jax.nn.sigmoid(pre_act)).astype(jnp.bfloat16)
        pre_acts[k] = pre_act
        roots[k] = root
        hiddens[k] = hidden
        if not last:
            streams[k + 1] = (wide + dot(hidden, weight_out(k), 1, 0)).astype(jnp.bfloat16)

    def swap_part(unit):
        remote(
            parts.at[unit, :, other],
            from_core.at[unit],
            part_send.at[unit],
            part_recv.at[unit],
            partner,
        )

    def make_in_part(k, grad_act):
        scaled = (grad_act * roots[k][:, :rank]).astype(jnp.bfloat16)
        part = dot(streams[k], scaled, 0, 0).astype(jnp.bfloat16)
        parts[2 * k] = part.reshape(planes, CORES, in_rows, rank)
        swap_part(2 * k)

    def make_out_part(k, grad_rounded):
        part = dot(hiddens[k], grad_rounded, 0, 0).astype(jnp.bfloat16)
        for t in range(tiles):
            parts[2 * k + 1, :, :, out_rows * t : out_rows * (t + 1), :] = part[
                :, 128 * t : 128 * (t + 1)
            ].reshape(planes, CORES, out_rows, 128)
        swap_part(2 * k + 1)

    def send_chip_sums(unit):
        landed(from_core.at[unit], part_recv.at[unit])
        chip_sums[unit] = (
            parts[unit, :, core].astype(jnp.float32) + from_core[unit].astype(jnp.float32)
        ).astype(jnp.bfloat16)
        for offset in range(1, planes):
            remote(
                chip_sums.at[unit, lax.rem(plane + offset, planes)],
                from_planes.at[unit, offset - 1],
                sum_send.at[unit, offset - 1],
                sum_recv.at[unit, offset - 1],
                plane_peer(offset),
            )

    def send_total(unit):
        k, kind = unit // 2, unit % 2
        total = chip_sums[unit, plane].astype(jnp.float32)
        for offset in range(1, planes):
            landed(from_planes.at[unit, offset - 1], sum_recv.at[unit, offset - 1])
            total = total + from_planes[unit, offset - 1].astype(jnp.float32)
        total = total.astype(jnp.bfloat16)
        totals[unit] = total
        own = owned.at[kind, me_s]

        @pl.when(me_s != k)
        def _():
            send(
                totals.at[unit], own, total_send.at[unit], total_recv.at[kind, me_s], (k, me_d)
            )

        @pl.when(me_s == k)
        def _():
            pltpu.make_async_copy(totals.at[unit], own, total_recv.at[kind, me_s]).start()

        grad_total = total.astype(jnp.float32)
        if kind == 0:
            grad_total = grad_total * gain_of[k].astype(jnp.float32)
        return jnp.sum((grad_total * grad_total).reshape(-1, 8, 128), axis=0)

    def units_of(k):
        units = [2 * k] + ([2 * k - 1] if k > 0 else [])
        return [2 * k + 1] + units if k == sections - 1 else units

    for k in range(sections):
        landed(gain_of.at[k], gain_recv.at[k])
    square = jnp.zeros((8, 128), jnp.float32)
    grad = cotangent_ref[...].astype(jnp.float32)
    for k in reversed(range(sections)):
        slot = 2 * sections - 1 - k
        pre_act = pre_acts[k]
        root = roots[k]
        squash = jax.nn.sigmoid(pre_act)
        grad_act = grad_partial * squash * (1.0 + pre_act * (1.0 - squash))
        act = grad_act.astype(jnp.bfloat16)
        copies = []
        if k > 0:
            column = root[:, :1]
            inner_mean = jnp.sum(grad_act * pre_act, axis=1, keepdims=True) / channels
            grad_normed = dot(act, weight_in(k), 1, 1)
            grad = grad + column * (
                grad_normed - streams[k].astype(jnp.float32) * (column * inner_mean)
            )
            grad_rounded = grad.astype(jnp.bfloat16)
            grad_partial = dot(grad_rounded, weight_out(k - 1), 1, 1)
            sent[slot, :tokens] = grad_partial.astype(jnp.bfloat16)
            copies = swap(slot, tokens)
        if k == sections - 1:
            make_out_part(k, cotangent_ref[...])
        make_in_part(k, grad_act)
        if k > 0:
            make_out_part(k - 1, grad_rounded)
        if k == 0 and sections > 2:
            for unit in units_of(k + 2):
                square = square + send_total(unit)
        for unit in units_of(k):
            send_chip_sums(unit)
        if 0 < k < sections - 2:
            for unit in units_of(k + 2):
                square = square + send_total(unit)
        for offset, copy in enumerate(copies):
            copy.wait_recv()
            grad_partial = grad_partial + received[slot, offset, :tokens].astype(jnp.float32)
    for k in (1, 0):
        for unit in units_of(k):
            square = square + send_total(unit)

    squares[0] = square
    copies = [
        remote(
            squares.at[0],
            squares_dp.at[offset - 1],
            dp_send.at[offset - 1],
            dp_recv.at[offset - 1],
            dp_peer(offset),
        )
        for offset in range(1, dp_count)
    ]
    out_parts = []
    for s in range(sections):
        landed(owned.at[1, s], total_recv.at[1, s])
        landed(owned.at[0, s], total_recv.at[0, s])
        own = slice(in_rows * s, in_rows * (s + 1))
        in_part = owned[0, s].astype(jnp.float32) * gain_rows[own]
        out_part = owned[1, s].astype(jnp.float32)
        grad_in_ref[own] = in_part
        out_parts.append(
            jnp.concatenate(
                [out_part[out_rows * t : out_rows * (t + 1)] for t in range(tiles)], axis=1
            )
        )
    grad_out_ref[...] = jnp.concatenate(
        [
            out_parts[s][:, in_rows * d : in_rows * (d + 1)]
            for d in range(dp_count)
            for s in range(sections)
        ],
        axis=1,
    )
    for offset, copy in enumerate(copies):
        copy.wait_recv()
        square = square + squares_dp[offset]
    squares[1] = square
    copies = [
        remote(
            squares.at[1],
            squares_section.at[offset - 1],
            section_send.at[offset - 1],
            section_recv.at[offset - 1],
            section_peer(offset),
        )
        for offset in range(1, sections)
    ]
    for offset, copy in enumerate(copies):
        copy.wait_recv()
        square = square + squares_section[offset]
    count_all = 2.0 * channels * rank * sections
    norm_total = jnp.sum(square, keepdims=True)
    factor = jnp.minimum(1.0, lax.rsqrt(norm_total / count_all + CLIP_EPS))
    factor_ref[...] = jnp.broadcast_to(factor, factor_ref.shape)

    for copy in started:
        copy.wait_send()
    for k in range(sections):
        for offset in range(1, planes):
            target = lax.rem(plane + offset, planes)

            @pl.when((target - plane != far) & (plane - target != far))
            def _():
                landed(weights.at[k, plane, core], rail_send.at[k, offset - 1])

        @pl.when(plane == far - 1)
        def _():
            landed(weights.at[k, 0, core], relay_send.at[k, 0])

        @pl.when(plane == 1)
        def _():
            landed(weights.at[k, far, core], relay_send.at[k, 1])

        @pl.when(me_s != k)
        def _():
            landed(totals.at[2 * k], total_send.at[2 * k])
            landed(totals.at[2 * k + 1], total_send.at[2 * k + 1])


def adam_kernel(*refs):
    inputs, outputs, loaded, results = refs[:9], refs[9:15], refs[15:24], refs[24:30]
    load_sems, store_sems = refs[30:]
    loads = [
        pltpu.make_async_copy(inputs[i], loaded[i], load_sems.at[i]) for i in range(len(inputs))
    ]
    for copy in loads:
        copy.start()
    stores = []
    loads[0].wait()
    factor = loaded[0][:1, :1]
    for place in (0, 1):
        for copy in loads[4 * place + 1 : 4 * place + 5]:
            copy.wait()
        grad, weight, moment, variance = loaded[4 * place + 1 : 4 * place + 5]
        updated = update(weight[0], grad[...], moment[0], variance[0], factor)
        for i, result in enumerate(updated, start=3 * place):
            results[i][...] = result
            copy = pltpu.make_async_copy(results[i], outputs[i], store_sems.at[i])
            copy.start()
            stores.append(copy)
    for copy in stores:
        copy.wait()


def fast_shards(
    stream_in,
    cotangent,
    norm_gain,
    weight_in,
    weight_out,
    moment_in,
    variance_in,
    moment_out,
    variance_out,
):
    sections = lax.axis_size("section")
    dp_count = lax.axis_size("dp")
    planes = dp_count // CORES
    channels = stream_in.shape[-1]
    tokens = stream_in.shape[0] * stream_in.shape[1]
    shard_rows, rank = weight_in.shape[1:]
    if tokens != rank:
        return shards(
            stream_in,
            cotangent,
            norm_gain,
            weight_in,
            weight_out,
            moment_in,
            variance_in,
            moment_out,
            variance_out,
        )
    out_rows = weight_out.shape[1]
    in_rows = shard_rows // sections
    width = channels // sections
    tiles = width // 128
    piece_rows = in_rows + out_rows * tiles

    narrow, full = jnp.bfloat16, jnp.float32
    slots = 2 * sections - 1
    units = 2 * sections
    dma = pltpu.SemaphoreType.DMA
    vmem = pl.BlockSpec(memory_space=pltpu.VMEM)
    grad_w_in, grad_w_out, factor = pl.pallas_call(
        functools.partial(step_kernel, sections, planes),
        out_shape=(
            jax.ShapeDtypeStruct((shard_rows, rank), full),
            jax.ShapeDtypeStruct((out_rows, channels), full),
            jax.ShapeDtypeStruct((8, 128), full),
        ),
        in_specs=[pl.BlockSpec(memory_space=pl.ANY)] * 5,
        out_specs=(vmem, vmem, vmem),
        scratch_shapes=[
            pltpu.VMEM((2, tokens, channels), narrow),
            pltpu.VMEM((1, channels), narrow),
            pltpu.VMEM((shard_rows, rank), narrow),
            pltpu.VMEM((out_rows, channels), narrow),
            pltpu.VMEM((tokens, width), narrow),
            pltpu.VMEM((sections, piece_rows, 128), narrow),
            pltpu.VMEM((shard_rows, 128), full),
            pltpu.VMEM((sections, in_rows, 128), narrow),
            pltpu.VMEM((sections, in_rows, 128), narrow),
            pltpu.VMEM((sections, planes, CORES, piece_rows, 128), narrow),
            pltpu.VMEM((units, planes, CORES, in_rows, 128), narrow),
            pltpu.VMEM((units, planes, in_rows, 128), narrow),
            pltpu.VMEM((units, planes, in_rows, 128), narrow),
            pltpu.VMEM((units, planes - 1, in_rows, 128), narrow),
            pltpu.VMEM((units, in_rows, 128), narrow),
            pltpu.VMEM((2, sections, in_rows, 128), narrow),
            pltpu.VMEM((sections, tokens, width), narrow),
            pltpu.VMEM((sections, tokens, rank), full),
            pltpu.VMEM((sections, tokens, tokens), full),
            pltpu.VMEM((sections, tokens, rank), narrow),
            pltpu.VMEM((slots, 2 * tokens + 16, rank), narrow),
            pltpu.VMEM((slots, sections - 1, 2 * tokens + 16, rank), narrow),
            pltpu.VMEM((2, 8, 128), full),
            pltpu.VMEM((dp_count - 1, 8, 128), full),
            pltpu.VMEM((sections - 1, 8, 128), full),
            dma((5,)),
            dma((sections - 1,)),
            dma((sections,)),
            dma((sections - 1,)),
            dma((sections,)),
            dma((sections, planes - 1)),
            dma((sections, 2)),
            dma((sections, planes)),
            dma((sections, planes, CORES)),
            dma((slots, sections - 1)),
            dma((slots, sections - 1)),
            dma((units,)),
            dma((units,)),
            dma((units, planes - 1)),
            dma((units, planes - 1)),
            dma((units,)),
            dma((2, sections)),
            dma((dp_count - 1,)),
            dma((dp_count - 1,)),
            dma((sections - 1,)),
            dma((sections - 1,)),
        ],
        compiler_params=pltpu.CompilerParams(
            collective_id=0, has_side_effects=True, vmem_limit_bytes=60 * 1024 * 1024
        ),
    )(
        stream_in.reshape(tokens, channels),
        cotangent.reshape(tokens, channels),
        norm_gain,
        weight_in[0],
        weight_out[0],
    )
    in_shape = jax.ShapeDtypeStruct(moment_in.shape, full)
    out_shape = jax.ShapeDtypeStruct(moment_out.shape, full)
    arrays = (
        factor,
        grad_w_in,
        weight_in,
        moment_in,
        variance_in,
        grad_w_out,
        weight_out,
        moment_out,
        variance_out,
    )
    anywhere = pl.BlockSpec(memory_space=pl.ANY)
    return pl.pallas_call(
        adam_kernel,
        out_shape=(in_shape,) * 3 + (out_shape,) * 3,
        in_specs=[anywhere] * len(arrays),
        out_specs=(anywhere,) * 6,
        scratch_shapes=[
            *(pltpu.VMEM(array.shape, array.dtype) for array in arrays),
            *(pltpu.VMEM(shape.shape, full) for shape in (in_shape,) * 3 + (out_shape,) * 3),
            dma((len(arrays),)),
            dma((6,)),
        ],
        compiler_params=pltpu.CompilerParams(vmem_limit_bytes=60 * 1024 * 1024),
    )(*arrays)


def aligned(sections, dp_count):
    width, in_rows, out_rows = E // sections, E // (sections * dp_count), R // dp_count
    return (
        sections > 1
        and dp_count % CORES == 0
        and dp_count > 2 * CORES
        and width % 128 == 0
        and in_rows % 16 == 0
        and out_rows % 16 == 0
        and R == 128
        and E <= 128 * 128
        and E % (64 * dp_count) == 0
    )


def solution(mesh):
    fast = aligned(mesh.shape["section"], mesh.shape["dp"])
    return jax.shard_map(
        fast_shards if fast else shards,
        mesh=mesh,
        in_specs=(
            P(None, "dp", None),
            P(None, "dp", None),
            P("section", None),
            P("section", "dp", None),
            P("section", "dp", None),
            P("section", "dp", None),
            P("section", "dp", None),
            P("section", "dp", None),
            P("section", "dp", None),
        ),
        out_specs=(
            P("section", "dp", None),
            P("section", "dp", None),
            P("section", "dp", None),
            P("section", "dp", None),
            P("section", "dp", None),
            P("section", "dp", None),
        ),
        check_vma=False,
    )
```

```python
import functools

import jax
import jax.numpy as jnp
from jax import lax
from jax.experimental import pallas as pl
from jax.experimental.pallas import tpu as pltpu
from jax.sharding import PartitionSpec as P

E = 3584
R = 128


NORM_EPS = 1e-06
BETA_ONE = 0.9
BETA_TWO = 0.95
STEP_RATE = 0.01
ADAM_EPS = 1e-08
CLIP_EPS = 1e-06


def from_behind(x, axis, by):
    count = lax.axis_size(axis)
    pairs = [(i, i + by) for i in range(count) if 0 <= i + by < count]
    return lax.ppermute(x, axis, pairs)


def normalize(stream, gain):
    values = stream.astype(jnp.float32)
    inv_root = lax.rsqrt(jnp.mean(values * values, axis=-1, keepdims=True) + NORM_EPS)
    unit_rows = values * inv_root
    normed = (unit_rows * gain.astype(jnp.float32)).astype(jnp.bfloat16)
    return (values, inv_root, unit_rows, normed)


def section_forward(stream, gain, in_weight, out_weight):
    values, inv_root, unit_rows, normed = normalize(stream, gain)
    pre_act = jnp.dot(normed, in_weight, preferred_element_type=jnp.float32)
    hidden = (pre_act * jax.nn.sigmoid(pre_act)).astype(jnp.bfloat16)
    return (values + jnp.dot(hidden, out_weight, preferred_element_type=jnp.float32)).astype(
        jnp.bfloat16
    )


def section_backward(stream, grad_rows, gain, in_weight, out_weight):
    values, inv_root, unit_rows, normed = normalize(stream, gain)
    pre_act = jnp.dot(normed, in_weight, preferred_element_type=jnp.float32)
    squash = jax.nn.sigmoid(pre_act)
    hidden = (pre_act * squash).astype(jnp.bfloat16)
    grad_hidden = lax.dot_general(
        grad_rows, out_weight, (((1,), (1,)), ((), ())), preferred_element_type=jnp.float32
    )
    grad_act = (grad_hidden * squash * (1.0 + pre_act * (1.0 - squash))).astype(jnp.bfloat16)
    grad_normed = lax.dot_general(
        grad_act, in_weight, (((1,), (1,)), ((), ())), preferred_element_type=jnp.float32
    ) * gain.astype(jnp.float32)
    inner_mean = jnp.mean(grad_normed * unit_rows, axis=-1, keepdims=True)
    grad_in = (
        grad_rows.astype(jnp.float32) + inv_root * (grad_normed - unit_rows * inner_mean)
    ).astype(jnp.bfloat16)
    return (grad_in, normed, grad_act, hidden)


def contract_rows(left, right):
    return lax.dot_general(
        left, right, (((0,), (0,)), ((), ())), preferred_element_type=jnp.float32
    )


def forward_tick(step_tick, position, is_first, incoming, saved_rows, inputs, weights):
    batch_count = inputs.shape[0]
    chain_index = step_tick - position
    active = jnp.logical_and(chain_index >= 0, chain_index < batch_count)
    batch_slot = jnp.clip(chain_index, 0, batch_count - 1)
    stream = jnp.where(is_first, lax.dynamic_index_in_dim(inputs, batch_slot, 0, False), incoming)
    kept_row = jnp.where(active, stream, lax.dynamic_index_in_dim(saved_rows, batch_slot, 0, False))
    saved_rows = lax.dynamic_update_index_in_dim(saved_rows, kept_row, batch_slot, 0)
    section_out = lax.cond(
        active, lambda rows_in: section_forward(rows_in, *weights), jnp.zeros_like, stream
    )
    return (section_out, saved_rows)


def backward_tick(
    step_tick, position, is_last, incoming, saved_rows, targets, weights, grad_sums, groups
):
    batch_count = targets.shape[0]
    chain_index = step_tick - position
    active = jnp.logical_and(chain_index >= 0, chain_index < batch_count)
    batch_slot = jnp.clip(chain_index, 0, batch_count - 1)
    grad_rows = jnp.where(
        is_last, lax.dynamic_index_in_dim(targets, batch_slot, 0, False), incoming
    )
    stream = lax.dynamic_index_in_dim(saved_rows, batch_slot, 0, False)
    half_group = batch_slot * groups // batch_count

    def run_section(operands):
        rows_in, grad_now, sums_now = operands
        grad_in, normed, grad_act, hidden = section_backward(rows_in, grad_now, *weights)
        sum_in, sum_out = sums_now
        sum_in = lax.dynamic_update_index_in_dim(
            sum_in,
            lax.dynamic_index_in_dim(sum_in, half_group, 0, False)
            + contract_rows(normed, grad_act),
            half_group,
            0,
        )
        sum_out = lax.dynamic_update_index_in_dim(
            sum_out,
            lax.dynamic_index_in_dim(sum_out, half_group, 0, False)
            + contract_rows(hidden, grad_now),
            half_group,
            0,
        )
        return (grad_in, (sum_in, sum_out))

    def skip_section(operands):
        return (jnp.zeros_like(operands[1]), operands[2])

    return lax.cond(active, run_section, skip_section, (stream, grad_rows, grad_sums))


def update(weight, grad, moment, variance, factor):
    scaled = factor * grad
    moment = BETA_ONE * moment + (1.0 - BETA_ONE) * scaled
    variance = BETA_TWO * variance + (1.0 - BETA_TWO) * scaled * scaled
    weight = weight.astype(jnp.float32) - STEP_RATE * moment / (jnp.sqrt(variance) + ADAM_EPS)
    return (weight[None], moment[None], variance[None])


def shards(
    stream_in,
    cotangent,
    norm_gain,
    weight_in,
    weight_out,
    moment_in,
    variance_in,
    moment_out,
    variance_out,
):
    section_count = lax.axis_size("section")
    section_place = lax.axis_index("section")
    micro_count = stream_in.shape[0]
    in_slice = weight_in[0]
    out_slice = weight_out[0]
    full_in_shape = (in_slice.shape[0] * lax.axis_size("dp"), in_slice.shape[1])
    full_out_shape = (out_slice.shape[0] * lax.axis_size("dp"), out_slice.shape[1])
    empty_stream = jnp.zeros(stream_in.shape[1:], jnp.bfloat16)
    is_first = section_place == 0
    is_last = section_place == section_count - 1
    whole_in, whole_out = (
        lax.all_gather(in_slice, "dp", axis=0, tiled=True),
        lax.all_gather(out_slice, "dp", axis=0, tiled=True),
    )
    own_layer = (norm_gain[0], whole_in, whole_out)
    tick_count = micro_count + section_count - 1

    def run_forward(step_tick, loop_state):
        incoming, saved_rows = loop_state
        section_out, saved_rows = forward_tick(
            step_tick, section_place, is_first, incoming, saved_rows, stream_in, own_layer
        )
        return (from_behind(section_out, "section", 1), saved_rows)

    _, saved_rows = lax.fori_loop(
        0, tick_count, run_forward, (empty_stream, jnp.zeros_like(stream_in))
    )
    start_sums = (
        jnp.zeros((2,) + full_in_shape, jnp.float32),
        jnp.zeros((2,) + full_out_shape, jnp.float32),
    )

    def run_backward(step_tick, loop_state):
        incoming, grad_sums = loop_state
        grad_in, grad_sums = backward_tick(
            step_tick,
            section_count - 1 - section_place,
            is_last,
            incoming,
            saved_rows,
            cotangent,
            own_layer,
            grad_sums,
            2,
        )
        return (from_behind(grad_in, "section", -1), grad_sums)

    _, (stacked_in, stacked_out) = lax.fori_loop(
        0, tick_count, run_backward, (empty_stream, start_sums)
    )
    reduced_in, reduced_out = (
        lax.psum_scatter(
            stacked_in.astype(jnp.bfloat16), "dp", scatter_dimension=1, tiled=True
        ).astype(jnp.float32),
        lax.psum_scatter(
            stacked_out.astype(jnp.bfloat16), "dp", scatter_dimension=1, tiled=True
        ).astype(jnp.float32),
    )
    grad_w_in = reduced_in[0] + reduced_in[1]
    grad_w_out = reduced_out[0] + reduced_out[1]
    local_sum = jnp.sum(grad_w_in * grad_w_in) + jnp.sum(grad_w_out * grad_w_out)
    norm_total = lax.psum(local_sum, ("section", "dp"))
    count_all = 2.0 * E * R * section_count
    factor = jnp.minimum(1.0, lax.rsqrt(norm_total / count_all + CLIP_EPS))
    new_in, new_moment_in, new_variance_in = update(
        in_slice, grad_w_in, moment_in[0], variance_in[0], factor
    )
    new_out, new_moment_out, new_variance_out = update(
        out_slice, grad_w_out, moment_out[0], variance_out[0], factor
    )
    return (new_in, new_moment_in, new_variance_in, new_out, new_moment_out, new_variance_out)


MESH = pl.DeviceIdType.MESH
CORES = 2
HALVES = 2


def dot(left, right, left_dim, right_dim):
    return lax.dot_general(
        left, right, (((left_dim,), (right_dim,)), ((), ())), preferred_element_type=jnp.float32
    )


def step_kernel(
    sections,
    planes,
    stream_any,
    cotangent_any,
    gain_any,
    weight_in_any,
    weight_out_any,
    grad_in_ref,
    grad_out_ref,
    factor_ref,
    rows_ref,
    gain_ref,
    weight_in_ref,
    weight_out_ref,
    cotangent_ref,
    piece_ref,
    gain_rows,
    gain_sent,
    gain_of,
    weights,
    parts,
    from_core,
    chip_sums,
    from_planes,
    totals,
    owned,
    streams,
    pre_acts,
    roots,
    hiddens,
    sent,
    received,
    sent_halves,
    received_halves,
    squares,
    squares_dp,
    squares_section,
    load_sems,
    gain_send,
    gain_recv,
    piece_send,
    piece_recv,
    rail_send,
    relay_send,
    core_send,
    weight_recv,
    swap_send,
    swap_recv,
    half_send,
    half_recv,
    part_send,
    part_recv,
    sum_send,
    sum_recv,
    total_send,
    total_recv,
    dp_send,
    dp_recv,
    section_send,
    section_recv,
):
    me_s = lax.axis_index("section")
    me_d = lax.axis_index("dp")
    plane = me_d // CORES
    core = lax.rem(me_d, CORES)
    other = 1 - core
    dp_count = planes * CORES
    tokens, width = cotangent_ref.shape
    channels = width * sections
    shard_rows, rank = weight_in_ref.shape
    tiles = width // 128
    in_rows = shard_rows // sections
    out_rows = weight_out_ref.shape[0]

    def section_peer(offset):
        return (lax.rem(me_s + offset, sections), me_d)

    def dp_peer(offset):
        return (me_s, lax.rem(me_d + offset, dp_count))

    def plane_peer(offset):
        return (me_s, lax.rem(plane + offset, planes) * CORES + core)

    partner = (me_s, plane * CORES + other)

    def send(source, target, send_sem, recv_sem, device):
        copy = pltpu.make_async_remote_copy(
            src_ref=source,
            dst_ref=target,
            send_sem=send_sem,
            recv_sem=recv_sem,
            device_id=device,
            device_id_type=MESH,
        )
        copy.start()
        return copy

    def remote(*copy):
        started.append(send(*copy))
        return started[-1]

    def landed(target, sem):
        pltpu.make_async_copy(target, target, sem).wait()

    started = []
    loads = [
        pltpu.make_async_copy(source, target, load_sems.at[i])
        for i, (source, target) in enumerate(
            (
                (gain_any, gain_ref),
                (weight_out_any, weight_out_ref),
                (weight_in_any, weight_in_ref),
                (stream_any, rows_ref.at[0]),
                (cotangent_any, rows_ref.at[1]),
            )
        )
    ]
    for copy in loads:
        copy.start()
    barrier = pltpu.get_barrier_semaphore()
    for offset in range(1, sections):
        pl.semaphore_signal(barrier, inc=1, device_id=section_peer(offset), device_id_type=MESH)
    for offset in range(1, dp_count):
        pl.semaphore_signal(barrier, inc=1, device_id=dp_peer(offset), device_id_type=MESH)

    loads[0].wait()
    gain_row = gain_ref[...].astype(jnp.float32)
    gain_tiles = channels // 128
    gains = [gain_row[:, 128 * t : 128 * (t + 1)] for t in range(gain_tiles)]
    gains = jnp.concatenate(gains + [jnp.zeros((128 - gain_tiles, 128), jnp.float32)], axis=0)
    gains = jnp.transpose(gains)
    lanes = lax.broadcasted_iota(jnp.int32, (128, 128), 1)
    for b in range(shard_rows // 64):
        half = me_d * (shard_rows // 64) + b
        column = jnp.sum(jnp.where(lanes == half // 2, gains, 0.0), axis=1, keepdims=True)
        odd = jnp.full((64, 1), lax.rem(half, 2), jnp.int32) == 1
        gain_rows[64 * b : 64 * (b + 1)] = jnp.broadcast_to(
            jnp.where(odd, column[64:], column[:64]), (64, 128)
        )

    def own_channels(rows, s):
        cuts = [
            rows[:, shard_rows * d + in_rows * s : shard_rows * d + in_rows * (s + 1)]
            for d in range(dp_count)
        ]
        return jnp.concatenate(cuts, axis=1)

    loads[1].wait()
    loads[2].wait()
    shard_out = weight_out_ref[...].astype(jnp.float32)
    for s in range(sections):
        own = slice(in_rows * s, in_rows * (s + 1))
        piece_ref[s, :in_rows] = (
            weight_in_ref[own].astype(jnp.float32) * gain_rows[own]
        ).astype(jnp.bfloat16)
        cut = own_channels(shard_out, s).astype(jnp.bfloat16)
        for t in range(tiles):
            piece_ref[s, in_rows + out_rows * t : in_rows + out_rows * (t + 1)] = cut[
                :, 128 * t : 128 * (t + 1)
            ]
    pl.semaphore_wait(barrier, sections + dp_count - 2)

    for offset in range(1, sections):
        target = section_peer(offset)
        remote(
            piece_ref.at[target[0]],
            weights.at[me_s, plane, core],
            piece_send.at[offset - 1],
            piece_recv.at[me_s],
            target,
        )
    pltpu.make_async_copy(
        piece_ref.at[me_s], weights.at[me_s, plane, core], piece_recv.at[me_s]
    ).start()
    far = planes - 1
    for place in range(sections):
        k = me_s if place == 0 else jnp.where(place - 1 < me_s, place - 1, place)
        landed(weights.at[k, plane, core], piece_recv.at[k])
        piece = weights.at[k, plane, core]
        for offset in range(1, planes):
            target = lax.rem(plane + offset, planes)

            @pl.when((target - plane != far) & (plane - target != far))
            def _():
                send(
                    piece,
                    piece,
                    rail_send.at[k, offset - 1],
                    weight_recv.at[k, plane, core],
                    (me_s, target * CORES + core),
                )

        remote(piece, piece, core_send.at[k, 0], weight_recv.at[k, plane, core], partner)

    for s in range(sections):
        gain_sent[s] = gain_rows[in_rows * s : in_rows * (s + 1)].astype(jnp.bfloat16)
    for offset in range(1, sections):
        target = section_peer(offset)
        remote(
            gain_sent.at[target[0]],
            gain_of.at[me_s],
            gain_send.at[offset - 1],
            gain_recv.at[me_s],
            target,
        )
    pltpu.make_async_copy(gain_sent.at[me_s], gain_of.at[me_s], gain_recv.at[me_s]).start()

    def pass_on(k):
        for offset in range(1, planes):
            source = lax.rem(plane + offset, planes)
            piece = weights.at[k, source, core]
            landed(piece, weight_recv.at[k, source, core])

            @pl.when((source == 0) & (plane == far - 1))
            def _():
                send(
                    piece,
                    piece,
                    relay_send.at[k, 0],
                    weight_recv.at[k, source, core],
                    (me_s, far * CORES + core),
                )

            @pl.when((source == far) & (plane == 1))
            def _():
                send(
                    piece, piece, relay_send.at[k, 1], weight_recv.at[k, source, core], (me_s, core)
                )

            remote(
                piece, piece, core_send.at[k, offset], weight_recv.at[k, source, core], partner
            )

    def arrive(k):
        for source in range(planes):
            landed(weights.at[k, source, other], weight_recv.at[k, source, other])

    def weight_in(k):
        return weights[k, :, :, :in_rows, :].reshape(width, rank)

    def weight_out(k):
        columns = [
            weights[k, :, :, in_rows + out_rows * t : in_rows + out_rows * (t + 1), :].reshape(
                rank, 128
            )
            for t in range(tiles)
        ]
        return jnp.concatenate(columns, axis=1)

    def swap(slot, rows):
        return [
            remote(
                sent.at[slot, pl.ds(0, rows)],
                received.at[slot, offset - 1, pl.ds(0, rows)],
                swap_send.at[slot, offset - 1],
                swap_recv.at[slot, offset - 1],
                section_peer(offset),
            )
            for offset in range(1, sections)
        ]

    def spread(column):
        return jnp.transpose(jnp.broadcast_to(column, (tokens, tokens)))[:8]

    loads[3].wait()
    loads[4].wait()
    for s in range(sections):

        @pl.when(me_s == s)
        def _():
            streams[0] = own_channels(rows_ref[0].astype(jnp.float32), s).astype(jnp.bfloat16)
            cotangent_ref[...] = own_channels(rows_ref[1].astype(jnp.float32), s).astype(
                jnp.bfloat16
            )

    half = tokens // HALVES

    def forward_send(k, h):
        rows = slice(half * h, half * (h + 1))
        values = streams[k, rows]
        wide = values.astype(jnp.float32)
        partial = dot(values, weight_in(k), 1, 0)
        square = jnp.sum(wide * wide, axis=1, keepdims=True)
        square = spread(jnp.concatenate([square, jnp.zeros((tokens - half, 1), jnp.float32)], axis=0))
        square_hi = square.astype(jnp.bfloat16).astype(jnp.float32)
        sent_half = sent_halves.at[HALVES * k + h]
        sent_half[:half] = partial.astype(jnp.bfloat16)
        sent_half[half : half + 16] = jnp.concatenate(
            [square_hi, square - square_hi], axis=0
        ).astype(jnp.bfloat16)
        count = half + 16
        grad_part = None
        if k == sections - 1:
            grad_part = dot(cotangent_ref[rows], weight_out(k), 1, 1)
            sent_half[count : count + half] = grad_part.astype(jnp.bfloat16)
            count = count + half
        copies = [
            remote(
                sent_half.at[pl.ds(0, count)],
                received_halves.at[HALVES * k + h, offset - 1, pl.ds(0, count)],
                half_send.at[HALVES * k + h, offset - 1],
                half_recv.at[HALVES * k + h, offset - 1],
                section_peer(offset),
            )
            for offset in range(1, sections)
        ]
        return copies, partial, square, grad_part

    def forward_receive(k, h, state):
        rows = slice(half * h, half * (h + 1))
        copies, partial, square, grad_part = state
        for offset, copy in enumerate(copies):
            copy.wait_recv()
            count = half + 16 + (0 if grad_part is None else half)
            arrived = received_halves[HALVES * k + h, offset, :count].astype(jnp.float32)
            partial = partial + arrived[:half]
            square = square + arrived[half : half + 8] + arrived[half + 8 : half + 16]
            if grad_part is not None:
                grad_part = grad_part + arrived[half + 16 : half + 16 + half]
        mean = jnp.transpose(jnp.broadcast_to(square[:1], (tokens, tokens)))[:half] / channels
        root = lax.rsqrt(mean + NORM_EPS)
        pre_act = partial * root[:, :rank]
        hidden = (pre_act * jax.nn.sigmoid(pre_act)).astype(jnp.bfloat16)
        pre_acts[k, rows] = pre_act
        roots[k, rows] = root
        hiddens[k, rows] = hidden
        if k < sections - 1:
            streams[k + 1, rows] = (
                streams[k, rows].astype(jnp.float32) + dot(hidden, weight_out(k), 1, 0)
            ).astype(jnp.bfloat16)
        return grad_part

    pass_on(0)
    arrive(0)
    states = [forward_send(0, h) for h in range(HALVES)]
    for k in range(1, sections):
        pass_on(k)
        for h in range(HALVES):
            forward_receive(k - 1, h, states[h])
            if h == 0:
                arrive(k)
            states[h] = forward_send(k, h)
    grad_partial = jnp.concatenate(
        [forward_receive(sections - 1, h, states[h]) for h in range(HALVES)], axis=0
    )

    def swap_part(unit):
        remote(
            parts.at[unit, :, other],
            from_core.at[unit],
            part_send.at[unit],
            part_recv.at[unit],
            partner,
        )

    def make_in_part(k, grad_act):
        scaled = (grad_act * roots[k][:, :rank]).astype(jnp.bfloat16)
        part = dot(streams[k], scaled, 0, 0).astype(jnp.bfloat16)
        parts[2 * k] = part.reshape(planes, CORES, in_rows, rank)
        swap_part(2 * k)

    def make_out_part(k, grad_rounded):
        part = dot(hiddens[k], grad_rounded, 0, 0).astype(jnp.bfloat16)
        for t in range(tiles):
            parts[2 * k + 1, :, :, out_rows * t : out_rows * (t + 1), :] = part[
                :, 128 * t : 128 * (t + 1)
            ].reshape(planes, CORES, out_rows, 128)
        swap_part(2 * k + 1)

    def send_chip_sums(unit):
        landed(from_core.at[unit], part_recv.at[unit])
        chip_sums[unit] = (
            parts[unit, :, core].astype(jnp.float32) + from_core[unit].astype(jnp.float32)
        ).astype(jnp.bfloat16)
        for offset in range(1, planes):
            remote(
                chip_sums.at[unit, lax.rem(plane + offset, planes)],
                from_planes.at[unit, offset - 1],
                sum_send.at[unit, offset - 1],
                sum_recv.at[unit, offset - 1],
                plane_peer(offset),
            )

    def send_total(unit):
        k, kind = unit // 2, unit % 2
        total = chip_sums[unit, plane].astype(jnp.float32)
        for offset in range(1, planes):
            landed(from_planes.at[unit, offset - 1], sum_recv.at[unit, offset - 1])
            total = total + from_planes[unit, offset - 1].astype(jnp.float32)
        total = total.astype(jnp.bfloat16)
        totals[unit] = total
        own = owned.at[kind, me_s]

        @pl.when(me_s != k)
        def _():
            send(
                totals.at[unit], own, total_send.at[unit], total_recv.at[kind, me_s], (k, me_d)
            )

        @pl.when(me_s == k)
        def _():
            pltpu.make_async_copy(totals.at[unit], own, total_recv.at[kind, me_s]).start()

        grad_total = total.astype(jnp.float32)
        if kind == 0:
            grad_total = grad_total * gain_of[k].astype(jnp.float32)
        return jnp.sum((grad_total * grad_total).reshape(-1, 8, 128), axis=0)

    def units_of(k):
        units = [2 * k] + ([2 * k - 1] if k > 0 else [])
        return [2 * k + 1] + units if k == sections - 1 else units

    for k in range(sections):
        landed(gain_of.at[k], gain_recv.at[k])
    square = jnp.zeros((8, 128), jnp.float32)
    grad = cotangent_ref[...].astype(jnp.float32)
    for k in reversed(range(sections)):
        slot = sections - 1 - k
        pre_act = pre_acts[k]
        root = roots[k]
        squash = jax.nn.sigmoid(pre_act)
        grad_act = grad_partial * squash * (1.0 + pre_act * (1.0 - squash))
        act = grad_act.astype(jnp.bfloat16)
        copies = []
        if k > 0:
            column = root[:, :1]
            inner_mean = jnp.sum(grad_act * pre_act, axis=1, keepdims=True) / channels
            grad_normed = dot(act, weight_in(k), 1, 1)
            grad = grad + column * (
                grad_normed - streams[k].astype(jnp.float32) * (column * inner_mean)
            )
            grad_rounded = grad.astype(jnp.bfloat16)
            grad_partial = dot(grad_rounded, weight_out(k - 1), 1, 1)
            sent[slot, :tokens] = grad_partial.astype(jnp.bfloat16)
            copies = swap(slot, tokens)
        if k == sections - 1:
            make_out_part(k, cotangent_ref[...])
        make_in_part(k, grad_act)
        if k > 0:
            make_out_part(k - 1, grad_rounded)
        if k == 0 and sections > 2:
            for unit in units_of(k + 2):
                square = square + send_total(unit)
        for unit in units_of(k):
            send_chip_sums(unit)
        if 0 < k < sections - 2:
            for unit in units_of(k + 2):
                square = square + send_total(unit)
        for offset, copy in enumerate(copies):
            copy.wait_recv()
            grad_partial = grad_partial + received[slot, offset, :tokens].astype(jnp.float32)
    for k in (1, 0):
        for unit in units_of(k):
            square = square + send_total(unit)

    squares[0] = square
    copies = [
        remote(
            squares.at[0],
            squares_dp.at[offset - 1],
            dp_send.at[offset - 1],
            dp_recv.at[offset - 1],
            dp_peer(offset),
        )
        for offset in range(1, dp_count)
    ]
    out_parts = []
    for s in range(sections):
        landed(owned.at[1, s], total_recv.at[1, s])
        landed(owned.at[0, s], total_recv.at[0, s])
        own = slice(in_rows * s, in_rows * (s + 1))
        in_part = owned[0, s].astype(jnp.float32) * gain_rows[own]
        out_part = owned[1, s].astype(jnp.float32)
        grad_in_ref[own] = in_part
        out_parts.append(
            jnp.concatenate(
                [out_part[out_rows * t : out_rows * (t + 1)] for t in range(tiles)], axis=1
            )
        )
    grad_out_ref[...] = jnp.concatenate(
        [
            out_parts[s][:, in_rows * d : in_rows * (d + 1)]
            for d in range(dp_count)
            for s in range(sections)
        ],
        axis=1,
    )
    for offset, copy in enumerate(copies):
        copy.wait_recv()
        square = square + squares_dp[offset]
    squares[1] = square
    copies = [
        remote(
            squares.at[1],
            squares_section.at[offset - 1],
            section_send.at[offset - 1],
            section_recv.at[offset - 1],
            section_peer(offset),
        )
        for offset in range(1, sections)
    ]
    for offset, copy in enumerate(copies):
        copy.wait_recv()
        square = square + squares_section[offset]
    count_all = 2.0 * channels * rank * sections
    norm_total = jnp.sum(square, keepdims=True)
    factor = jnp.minimum(1.0, lax.rsqrt(norm_total / count_all + CLIP_EPS))
    factor_ref[...] = jnp.broadcast_to(factor, factor_ref.shape)

    for copy in started:
        copy.wait_send()
    for k in range(sections):
        for offset in range(1, planes):
            target = lax.rem(plane + offset, planes)

            @pl.when((target - plane != far) & (plane - target != far))
            def _():
                landed(weights.at[k, plane, core], rail_send.at[k, offset - 1])

        @pl.when(plane == far - 1)
        def _():
            landed(weights.at[k, 0, core], relay_send.at[k, 0])

        @pl.when(plane == 1)
        def _():
            landed(weights.at[k, far, core], relay_send.at[k, 1])

        @pl.when(me_s != k)
        def _():
            landed(totals.at[2 * k], total_send.at[2 * k])
            landed(totals.at[2 * k + 1], total_send.at[2 * k + 1])


def adam_kernel(*refs):
    inputs, outputs, loaded, results = refs[:9], refs[9:15], refs[15:24], refs[24:30]
    load_sems, store_sems = refs[30:]
    loads = [
        pltpu.make_async_copy(inputs[i], loaded[i], load_sems.at[i]) for i in range(len(inputs))
    ]
    for copy in loads:
        copy.start()
    stores = []
    loads[0].wait()
    factor = loaded[0][:1, :1]
    for place in (0, 1):
        for copy in loads[4 * place + 1 : 4 * place + 5]:
            copy.wait()
        grad, weight, moment, variance = loaded[4 * place + 1 : 4 * place + 5]
        updated = update(weight[0], grad[...], moment[0], variance[0], factor)
        for i, result in enumerate(updated, start=3 * place):
            results[i][...] = result
            copy = pltpu.make_async_copy(results[i], outputs[i], store_sems.at[i])
            copy.start()
            stores.append(copy)
    for copy in stores:
        copy.wait()


def fast_shards(
    stream_in,
    cotangent,
    norm_gain,
    weight_in,
    weight_out,
    moment_in,
    variance_in,
    moment_out,
    variance_out,
):
    sections = lax.axis_size("section")
    dp_count = lax.axis_size("dp")
    planes = dp_count // CORES
    channels = stream_in.shape[-1]
    tokens = stream_in.shape[0] * stream_in.shape[1]
    shard_rows, rank = weight_in.shape[1:]
    if tokens != rank:
        return shards(
            stream_in,
            cotangent,
            norm_gain,
            weight_in,
            weight_out,
            moment_in,
            variance_in,
            moment_out,
            variance_out,
        )
    out_rows = weight_out.shape[1]
    in_rows = shard_rows // sections
    width = channels // sections
    tiles = width // 128
    piece_rows = in_rows + out_rows * tiles

    narrow, full = jnp.bfloat16, jnp.float32
    slots = sections - 1
    chunks = HALVES * sections
    half = tokens // HALVES
    units = 2 * sections
    dma = pltpu.SemaphoreType.DMA
    vmem = pl.BlockSpec(memory_space=pltpu.VMEM)
    grad_w_in, grad_w_out, factor = pl.pallas_call(
        functools.partial(step_kernel, sections, planes),
        out_shape=(
            jax.ShapeDtypeStruct((shard_rows, rank), full),
            jax.ShapeDtypeStruct((out_rows, channels), full),
            jax.ShapeDtypeStruct((8, 128), full),
        ),
        in_specs=[pl.BlockSpec(memory_space=pl.ANY)] * 5,
        out_specs=(vmem, vmem, vmem),
        scratch_shapes=[
            pltpu.VMEM((2, tokens, channels), narrow),
            pltpu.VMEM((1, channels), narrow),
            pltpu.VMEM((shard_rows, rank), narrow),
            pltpu.VMEM((out_rows, channels), narrow),
            pltpu.VMEM((tokens, width), narrow),
            pltpu.VMEM((sections, piece_rows, 128), narrow),
            pltpu.VMEM((shard_rows, 128), full),
            pltpu.VMEM((sections, in_rows, 128), narrow),
            pltpu.VMEM((sections, in_rows, 128), narrow),
            pltpu.VMEM((sections, planes, CORES, piece_rows, 128), narrow),
            pltpu.VMEM((units, planes, CORES, in_rows, 128), narrow),
            pltpu.VMEM((units, planes, in_rows, 128), narrow),
            pltpu.VMEM((units, planes, in_rows, 128), narrow),
            pltpu.VMEM((units, planes - 1, in_rows, 128), narrow),
            pltpu.VMEM((units, in_rows, 128), narrow),
            pltpu.VMEM((2, sections, in_rows, 128), narrow),
            pltpu.VMEM((sections, tokens, width), narrow),
            pltpu.VMEM((sections, tokens, rank), full),
            pltpu.VMEM((sections, tokens, tokens), full),
            pltpu.VMEM((sections, tokens, rank), narrow),
            pltpu.VMEM((slots, tokens, rank), narrow),
            pltpu.VMEM((slots, sections - 1, tokens, rank), narrow),
            pltpu.VMEM((chunks, 2 * half + 16, rank), narrow),
            pltpu.VMEM((chunks, sections - 1, 2 * half + 16, rank), narrow),
            pltpu.VMEM((2, 8, 128), full),
            pltpu.VMEM((dp_count - 1, 8, 128), full),
            pltpu.VMEM((sections - 1, 8, 128), full),
            dma((5,)),
            dma((sections - 1,)),
            dma((sections,)),
            dma((sections - 1,)),
            dma((sections,)),
            dma((sections, planes - 1)),
            dma((sections, 2)),
            dma((sections, planes)),
            dma((sections, planes, CORES)),
            dma((slots, sections - 1)),
            dma((slots, sections - 1)),
            dma((chunks, sections - 1)),
            dma((chunks, sections - 1)),
            dma((units,)),
            dma((units,)),
            dma((units, planes - 1)),
            dma((units, planes - 1)),
            dma((units,)),
            dma((2, sections)),
            dma((dp_count - 1,)),
            dma((dp_count - 1,)),
            dma((sections - 1,)),
            dma((sections - 1,)),
        ],
        compiler_params=pltpu.CompilerParams(
            collective_id=0, has_side_effects=True, vmem_limit_bytes=60 * 1024 * 1024
        ),
    )(
        stream_in.reshape(tokens, channels),
        cotangent.reshape(tokens, channels),
        norm_gain,
        weight_in[0],
        weight_out[0],
    )
    in_shape = jax.ShapeDtypeStruct(moment_in.shape, full)
    out_shape = jax.ShapeDtypeStruct(moment_out.shape, full)
    arrays = (
        factor,
        grad_w_in,
        weight_in,
        moment_in,
        variance_in,
        grad_w_out,
        weight_out,
        moment_out,
        variance_out,
    )
    anywhere = pl.BlockSpec(memory_space=pl.ANY)
    return pl.pallas_call(
        adam_kernel,
        out_shape=(in_shape,) * 3 + (out_shape,) * 3,
        in_specs=[anywhere] * len(arrays),
        out_specs=(anywhere,) * 6,
        scratch_shapes=[
            *(pltpu.VMEM(array.shape, array.dtype) for array in arrays),
            *(pltpu.VMEM(shape.shape, full) for shape in (in_shape,) * 3 + (out_shape,) * 3),
            dma((len(arrays),)),
            dma((6,)),
        ],
        compiler_params=pltpu.CompilerParams(vmem_limit_bytes=60 * 1024 * 1024),
    )(*arrays)


def aligned(sections, dp_count):
    width, in_rows, out_rows = E // sections, E // (sections * dp_count), R // dp_count
    return (
        sections > 1
        and dp_count % CORES == 0
        and dp_count > 2 * CORES
        and width % 128 == 0
        and in_rows % 16 == 0
        and out_rows % 16 == 0
        and R == 128
        and E <= 128 * 128
        and E % (64 * dp_count) == 0
    )


def solution(mesh):
    fast = aligned(mesh.shape["section"], mesh.shape["dp"])
    return jax.shard_map(
        fast_shards if fast else shards,
        mesh=mesh,
        in_specs=(
            P(None, "dp", None),
            P(None, "dp", None),
            P("section", None),
            P("section", "dp", None),
            P("section", "dp", None),
            P("section", "dp", None),
            P("section", "dp", None),
            P("section", "dp", None),
            P("section", "dp", None),
        ),
        out_specs=(
            P("section", "dp", None),
            P("section", "dp", None),
            P("section", "dp", None),
            P("section", "dp", None),
            P("section", "dp", None),
            P("section", "dp", None),
        ),
        check_vma=False,
    )
```

```python
import functools

import jax
import jax.numpy as jnp
from jax import lax
from jax.experimental import pallas as pl
from jax.experimental.pallas import tpu as pltpu
from jax.sharding import PartitionSpec as P

E = 3584
R = 128


NORM_EPS = 1e-06
BETA_ONE = 0.9
BETA_TWO = 0.95
STEP_RATE = 0.01
ADAM_EPS = 1e-08
CLIP_EPS = 1e-06


def from_behind(x, axis, by):
    count = lax.axis_size(axis)
    pairs = [(i, i + by) for i in range(count) if 0 <= i + by < count]
    return lax.ppermute(x, axis, pairs)


def normalize(stream, gain):
    values = stream.astype(jnp.float32)
    inv_root = lax.rsqrt(jnp.mean(values * values, axis=-1, keepdims=True) + NORM_EPS)
    unit_rows = values * inv_root
    normed = (unit_rows * gain.astype(jnp.float32)).astype(jnp.bfloat16)
    return (values, inv_root, unit_rows, normed)


def section_forward(stream, gain, in_weight, out_weight):
    values, inv_root, unit_rows, normed = normalize(stream, gain)
    pre_act = jnp.dot(normed, in_weight, preferred_element_type=jnp.float32)
    hidden = (pre_act * jax.nn.sigmoid(pre_act)).astype(jnp.bfloat16)
    return (values + jnp.dot(hidden, out_weight, preferred_element_type=jnp.float32)).astype(
        jnp.bfloat16
    )


def section_backward(stream, grad_rows, gain, in_weight, out_weight):
    values, inv_root, unit_rows, normed = normalize(stream, gain)
    pre_act = jnp.dot(normed, in_weight, preferred_element_type=jnp.float32)
    squash = jax.nn.sigmoid(pre_act)
    hidden = (pre_act * squash).astype(jnp.bfloat16)
    grad_hidden = lax.dot_general(
        grad_rows, out_weight, (((1,), (1,)), ((), ())), preferred_element_type=jnp.float32
    )
    grad_act = (grad_hidden * squash * (1.0 + pre_act * (1.0 - squash))).astype(jnp.bfloat16)
    grad_normed = lax.dot_general(
        grad_act, in_weight, (((1,), (1,)), ((), ())), preferred_element_type=jnp.float32
    ) * gain.astype(jnp.float32)
    inner_mean = jnp.mean(grad_normed * unit_rows, axis=-1, keepdims=True)
    grad_in = (
        grad_rows.astype(jnp.float32) + inv_root * (grad_normed - unit_rows * inner_mean)
    ).astype(jnp.bfloat16)
    return (grad_in, normed, grad_act, hidden)


def contract_rows(left, right):
    return lax.dot_general(
        left, right, (((0,), (0,)), ((), ())), preferred_element_type=jnp.float32
    )


def forward_tick(step_tick, position, is_first, incoming, saved_rows, inputs, weights):
    batch_count = inputs.shape[0]
    chain_index = step_tick - position
    active = jnp.logical_and(chain_index >= 0, chain_index < batch_count)
    batch_slot = jnp.clip(chain_index, 0, batch_count - 1)
    stream = jnp.where(is_first, lax.dynamic_index_in_dim(inputs, batch_slot, 0, False), incoming)
    kept_row = jnp.where(active, stream, lax.dynamic_index_in_dim(saved_rows, batch_slot, 0, False))
    saved_rows = lax.dynamic_update_index_in_dim(saved_rows, kept_row, batch_slot, 0)
    section_out = lax.cond(
        active, lambda rows_in: section_forward(rows_in, *weights), jnp.zeros_like, stream
    )
    return (section_out, saved_rows)


def backward_tick(
    step_tick, position, is_last, incoming, saved_rows, targets, weights, grad_sums, groups
):
    batch_count = targets.shape[0]
    chain_index = step_tick - position
    active = jnp.logical_and(chain_index >= 0, chain_index < batch_count)
    batch_slot = jnp.clip(chain_index, 0, batch_count - 1)
    grad_rows = jnp.where(
        is_last, lax.dynamic_index_in_dim(targets, batch_slot, 0, False), incoming
    )
    stream = lax.dynamic_index_in_dim(saved_rows, batch_slot, 0, False)
    half_group = batch_slot * groups // batch_count

    def run_section(operands):
        rows_in, grad_now, sums_now = operands
        grad_in, normed, grad_act, hidden = section_backward(rows_in, grad_now, *weights)
        sum_in, sum_out = sums_now
        sum_in = lax.dynamic_update_index_in_dim(
            sum_in,
            lax.dynamic_index_in_dim(sum_in, half_group, 0, False)
            + contract_rows(normed, grad_act),
            half_group,
            0,
        )
        sum_out = lax.dynamic_update_index_in_dim(
            sum_out,
            lax.dynamic_index_in_dim(sum_out, half_group, 0, False)
            + contract_rows(hidden, grad_now),
            half_group,
            0,
        )
        return (grad_in, (sum_in, sum_out))

    def skip_section(operands):
        return (jnp.zeros_like(operands[1]), operands[2])

    return lax.cond(active, run_section, skip_section, (stream, grad_rows, grad_sums))


def update(weight, grad, moment, variance, factor):
    scaled = factor * grad
    moment = BETA_ONE * moment + (1.0 - BETA_ONE) * scaled
    variance = BETA_TWO * variance + (1.0 - BETA_TWO) * scaled * scaled
    weight = weight.astype(jnp.float32) - STEP_RATE * moment / (jnp.sqrt(variance) + ADAM_EPS)
    return (weight[None], moment[None], variance[None])


def shards(
    stream_in,
    cotangent,
    norm_gain,
    weight_in,
    weight_out,
    moment_in,
    variance_in,
    moment_out,
    variance_out,
):
    section_count = lax.axis_size("section")
    section_place = lax.axis_index("section")
    micro_count = stream_in.shape[0]
    in_slice = weight_in[0]
    out_slice = weight_out[0]
    full_in_shape = (in_slice.shape[0] * lax.axis_size("dp"), in_slice.shape[1])
    full_out_shape = (out_slice.shape[0] * lax.axis_size("dp"), out_slice.shape[1])
    empty_stream = jnp.zeros(stream_in.shape[1:], jnp.bfloat16)
    is_first = section_place == 0
    is_last = section_place == section_count - 1
    whole_in, whole_out = (
        lax.all_gather(in_slice, "dp", axis=0, tiled=True),
        lax.all_gather(out_slice, "dp", axis=0, tiled=True),
    )
    own_layer = (norm_gain[0], whole_in, whole_out)
    tick_count = micro_count + section_count - 1

    def run_forward(step_tick, loop_state):
        incoming, saved_rows = loop_state
        section_out, saved_rows = forward_tick(
            step_tick, section_place, is_first, incoming, saved_rows, stream_in, own_layer
        )
        return (from_behind(section_out, "section", 1), saved_rows)

    _, saved_rows = lax.fori_loop(
        0, tick_count, run_forward, (empty_stream, jnp.zeros_like(stream_in))
    )
    start_sums = (
        jnp.zeros((2,) + full_in_shape, jnp.float32),
        jnp.zeros((2,) + full_out_shape, jnp.float32),
    )

    def run_backward(step_tick, loop_state):
        incoming, grad_sums = loop_state
        grad_in, grad_sums = backward_tick(
            step_tick,
            section_count - 1 - section_place,
            is_last,
            incoming,
            saved_rows,
            cotangent,
            own_layer,
            grad_sums,
            2,
        )
        return (from_behind(grad_in, "section", -1), grad_sums)

    _, (stacked_in, stacked_out) = lax.fori_loop(
        0, tick_count, run_backward, (empty_stream, start_sums)
    )
    reduced_in, reduced_out = (
        lax.psum_scatter(
            stacked_in.astype(jnp.bfloat16), "dp", scatter_dimension=1, tiled=True
        ).astype(jnp.float32),
        lax.psum_scatter(
            stacked_out.astype(jnp.bfloat16), "dp", scatter_dimension=1, tiled=True
        ).astype(jnp.float32),
    )
    grad_w_in = reduced_in[0] + reduced_in[1]
    grad_w_out = reduced_out[0] + reduced_out[1]
    local_sum = jnp.sum(grad_w_in * grad_w_in) + jnp.sum(grad_w_out * grad_w_out)
    norm_total = lax.psum(local_sum, ("section", "dp"))
    count_all = 2.0 * E * R * section_count
    factor = jnp.minimum(1.0, lax.rsqrt(norm_total / count_all + CLIP_EPS))
    new_in, new_moment_in, new_variance_in = update(
        in_slice, grad_w_in, moment_in[0], variance_in[0], factor
    )
    new_out, new_moment_out, new_variance_out = update(
        out_slice, grad_w_out, moment_out[0], variance_out[0], factor
    )
    return (new_in, new_moment_in, new_variance_in, new_out, new_moment_out, new_variance_out)


MESH = pl.DeviceIdType.MESH
CORES = 2
HALVES = 2


def dot(left, right, left_dim, right_dim):
    return lax.dot_general(
        left, right, (((left_dim,), (right_dim,)), ((), ())), preferred_element_type=jnp.float32
    )


def step_kernel(
    sections,
    planes,
    stream_any,
    cotangent_any,
    gain_any,
    weight_in_any,
    weight_out_any,
    grad_in_ref,
    grad_out_ref,
    factor_ref,
    rows_ref,
    gain_ref,
    weight_in_ref,
    weight_out_ref,
    cotangent_ref,
    piece_ref,
    gain_rows,
    gain_sent,
    gain_of,
    weights,
    parts,
    from_core,
    chip_sums,
    from_planes,
    relayed,
    totals,
    owned,
    streams,
    pre_acts,
    roots,
    hiddens,
    sent,
    received,
    sent_halves,
    received_halves,
    squares,
    squares_dp,
    squares_section,
    load_sems,
    gain_send,
    gain_recv,
    piece_send,
    piece_recv,
    rail_send,
    relay_send,
    core_send,
    weight_recv,
    swap_send,
    swap_recv,
    half_send,
    half_recv,
    part_send,
    part_recv,
    sum_send,
    sum_recv,
    relay_recv,
    total_send,
    total_recv,
    dp_send,
    dp_recv,
    section_send,
    section_recv,
):
    me_s = lax.axis_index("section")
    me_d = lax.axis_index("dp")
    plane = me_d // CORES
    core = lax.rem(me_d, CORES)
    other = 1 - core
    dp_count = planes * CORES
    tokens, width = cotangent_ref.shape
    channels = width * sections
    shard_rows, rank = weight_in_ref.shape
    tiles = width // 128
    in_rows = shard_rows // sections
    out_rows = weight_out_ref.shape[0]

    def section_peer(offset):
        return (lax.rem(me_s + offset, sections), me_d)

    def dp_peer(offset):
        return (me_s, lax.rem(me_d + offset, dp_count))

    def plane_peer(offset):
        return (me_s, lax.rem(plane + offset, planes) * CORES + core)

    partner = (me_s, plane * CORES + other)

    def send(source, target, send_sem, recv_sem, device):
        copy = pltpu.make_async_remote_copy(
            src_ref=source,
            dst_ref=target,
            send_sem=send_sem,
            recv_sem=recv_sem,
            device_id=device,
            device_id_type=MESH,
        )
        copy.start()
        return copy

    def remote(*copy):
        started.append(send(*copy))
        return started[-1]

    def landed(target, sem):
        pltpu.make_async_copy(target, target, sem).wait()

    started = []
    loads = [
        pltpu.make_async_copy(source, target, load_sems.at[i])
        for i, (source, target) in enumerate(
            (
                (gain_any, gain_ref),
                (weight_out_any, weight_out_ref),
                (weight_in_any, weight_in_ref),
                (stream_any, rows_ref.at[0]),
                (cotangent_any, rows_ref.at[1]),
            )
        )
    ]
    for copy in loads:
        copy.start()
    barrier = pltpu.get_barrier_semaphore()
    for offset in range(1, sections):
        pl.semaphore_signal(barrier, inc=1, device_id=section_peer(offset), device_id_type=MESH)
    for offset in range(1, dp_count):
        pl.semaphore_signal(barrier, inc=1, device_id=dp_peer(offset), device_id_type=MESH)

    loads[0].wait()
    gain_row = gain_ref[...].astype(jnp.float32)
    gain_tiles = channels // 128
    gains = [gain_row[:, 128 * t : 128 * (t + 1)] for t in range(gain_tiles)]
    gains = jnp.concatenate(gains + [jnp.zeros((128 - gain_tiles, 128), jnp.float32)], axis=0)
    gains = jnp.transpose(gains)
    lanes = lax.broadcasted_iota(jnp.int32, (128, 128), 1)
    for b in range(shard_rows // 64):
        half = me_d * (shard_rows // 64) + b
        column = jnp.sum(jnp.where(lanes == half // 2, gains, 0.0), axis=1, keepdims=True)
        odd = jnp.full((64, 1), lax.rem(half, 2), jnp.int32) == 1
        gain_rows[64 * b : 64 * (b + 1)] = jnp.broadcast_to(
            jnp.where(odd, column[64:], column[:64]), (64, 128)
        )

    def own_channels(rows, s):
        cuts = [
            rows[:, shard_rows * d + in_rows * s : shard_rows * d + in_rows * (s + 1)]
            for d in range(dp_count)
        ]
        return jnp.concatenate(cuts, axis=1)

    loads[1].wait()
    loads[2].wait()
    shard_out = weight_out_ref[...].astype(jnp.float32)
    for s in range(sections):
        own = slice(in_rows * s, in_rows * (s + 1))
        piece_ref[s, :in_rows] = (
            weight_in_ref[own].astype(jnp.float32) * gain_rows[own]
        ).astype(jnp.bfloat16)
        cut = own_channels(shard_out, s).astype(jnp.bfloat16)
        for t in range(tiles):
            piece_ref[s, in_rows + out_rows * t : in_rows + out_rows * (t + 1)] = cut[
                :, 128 * t : 128 * (t + 1)
            ]
    pl.semaphore_wait(barrier, sections + dp_count - 2)

    for offset in range(1, sections):
        target = section_peer(offset)
        remote(
            piece_ref.at[target[0]],
            weights.at[me_s, plane, core],
            piece_send.at[offset - 1],
            piece_recv.at[me_s],
            target,
        )
    pltpu.make_async_copy(
        piece_ref.at[me_s], weights.at[me_s, plane, core], piece_recv.at[me_s]
    ).start()
    far = planes - 1
    for place in range(sections):
        k = me_s if place == 0 else jnp.where(place - 1 < me_s, place - 1, place)
        landed(weights.at[k, plane, core], piece_recv.at[k])
        piece = weights.at[k, plane, core]
        for offset in range(1, planes):
            target = lax.rem(plane + offset, planes)

            @pl.when((target - plane != far) & (plane - target != far))
            def _():
                send(
                    piece,
                    piece,
                    rail_send.at[k, offset - 1],
                    weight_recv.at[k, plane, core],
                    (me_s, target * CORES + core),
                )

        remote(piece, piece, core_send.at[k, 0], weight_recv.at[k, plane, core], partner)

    for s in range(sections):
        gain_sent[s] = gain_rows[in_rows * s : in_rows * (s + 1)].astype(jnp.bfloat16)
    for offset in range(1, sections):
        target = section_peer(offset)
        remote(
            gain_sent.at[target[0]],
            gain_of.at[me_s],
            gain_send.at[offset - 1],
            gain_recv.at[me_s],
            target,
        )
    pltpu.make_async_copy(gain_sent.at[me_s], gain_of.at[me_s], gain_recv.at[me_s]).start()

    def pass_on(k):
        for offset in range(1, planes):
            source = lax.rem(plane + offset, planes)
            piece = weights.at[k, source, core]
            landed(piece, weight_recv.at[k, source, core])

            @pl.when((source == 0) & (plane == far - 1))
            def _():
                send(
                    piece,
                    piece,
                    relay_send.at[k, 0],
                    weight_recv.at[k, source, core],
                    (me_s, far * CORES + core),
                )

            @pl.when((source == far) & (plane == 1))
            def _():
                send(
                    piece, piece, relay_send.at[k, 1], weight_recv.at[k, source, core], (me_s, core)
                )

            remote(
                piece, piece, core_send.at[k, offset], weight_recv.at[k, source, core], partner
            )

    def arrive(k):
        for source in range(planes):
            landed(weights.at[k, source, other], weight_recv.at[k, source, other])

    def weight_in(k):
        return weights[k, :, :, :in_rows, :].reshape(width, rank)

    def weight_out(k):
        columns = [
            weights[k, :, :, in_rows + out_rows * t : in_rows + out_rows * (t + 1), :].reshape(
                rank, 128
            )
            for t in range(tiles)
        ]
        return jnp.concatenate(columns, axis=1)

    def swap(slot, rows):
        return [
            remote(
                sent.at[slot, pl.ds(0, rows)],
                received.at[slot, offset - 1, pl.ds(0, rows)],
                swap_send.at[slot, offset - 1],
                swap_recv.at[slot, offset - 1],
                section_peer(offset),
            )
            for offset in range(1, sections)
        ]

    def spread(column):
        return jnp.transpose(jnp.broadcast_to(column, (tokens, tokens)))[:8]

    loads[3].wait()
    loads[4].wait()
    for s in range(sections):

        @pl.when(me_s == s)
        def _():
            streams[0] = own_channels(rows_ref[0].astype(jnp.float32), s).astype(jnp.bfloat16)
            cotangent_ref[...] = own_channels(rows_ref[1].astype(jnp.float32), s).astype(
                jnp.bfloat16
            )

    half = tokens // HALVES

    def forward_send(k, h):
        rows = slice(half * h, half * (h + 1))
        values = streams[k, rows]
        wide = values.astype(jnp.float32)
        partial = dot(values, weight_in(k), 1, 0)
        square = jnp.sum(wide * wide, axis=1, keepdims=True)
        square = spread(jnp.concatenate([square, jnp.zeros((tokens - half, 1), jnp.float32)], axis=0))
        square_hi = square.astype(jnp.bfloat16).astype(jnp.float32)
        sent_half = sent_halves.at[HALVES * k + h]
        sent_half[:half] = partial.astype(jnp.bfloat16)
        sent_half[half : half + 16] = jnp.concatenate(
            [square_hi, square - square_hi], axis=0
        ).astype(jnp.bfloat16)
        count = half + 16
        grad_part = None
        if k == sections - 1:
            grad_part = dot(cotangent_ref[rows], weight_out(k), 1, 1)
            sent_half[count : count + half] = grad_part.astype(jnp.bfloat16)
            count = count + half
        copies = [
            remote(
                sent_half.at[pl.ds(0, count)],
                received_halves.at[HALVES * k + h, offset - 1, pl.ds(0, count)],
                half_send.at[HALVES * k + h, offset - 1],
                half_recv.at[HALVES * k + h, offset - 1],
                section_peer(offset),
            )
            for offset in range(1, sections)
        ]
        return copies, partial, square, grad_part

    def forward_receive(k, h, state):
        rows = slice(half * h, half * (h + 1))
        copies, partial, square, grad_part = state
        for offset, copy in enumerate(copies):
            copy.wait_recv()
            count = half + 16 + (0 if grad_part is None else half)
            arrived = received_halves[HALVES * k + h, offset, :count].astype(jnp.float32)
            partial = partial + arrived[:half]
            square = square + arrived[half : half + 8] + arrived[half + 8 : half + 16]
            if grad_part is not None:
                grad_part = grad_part + arrived[half + 16 : half + 16 + half]
        mean = jnp.transpose(jnp.broadcast_to(square[:1], (tokens, tokens)))[:half] / channels
        root = lax.rsqrt(mean + NORM_EPS)
        pre_act = partial * root[:, :rank]
        hidden = (pre_act * jax.nn.sigmoid(pre_act)).astype(jnp.bfloat16)
        pre_acts[k, rows] = pre_act
        roots[k, rows] = root
        hiddens[k, rows] = hidden
        if k < sections - 1:
            streams[k + 1, rows] = (
                streams[k, rows].astype(jnp.float32) + dot(hidden, weight_out(k), 1, 0)
            ).astype(jnp.bfloat16)
        return grad_part

    pass_on(0)
    arrive(0)
    states = [forward_send(0, h) for h in range(HALVES)]
    for k in range(1, sections):
        pass_on(k)
        for h in range(HALVES):
            forward_receive(k - 1, h, states[h])
            if h == 0:
                arrive(k)
            states[h] = forward_send(k, h)
    grad_partial = jnp.concatenate(
        [forward_receive(sections - 1, h, states[h]) for h in range(HALVES)], axis=0
    )

    def swap_part(unit):
        remote(
            parts.at[unit, :, other],
            from_core.at[unit],
            part_send.at[unit],
            part_recv.at[unit],
            partner,
        )

    def make_in_part(k, grad_act):
        scaled = (grad_act * roots[k][:, :rank]).astype(jnp.bfloat16)
        part = dot(streams[k], scaled, 0, 0).astype(jnp.bfloat16)
        parts[2 * k] = part.reshape(planes, CORES, in_rows, rank)
        swap_part(2 * k)

    def make_out_part(k, grad_rounded):
        part = dot(hiddens[k], grad_rounded, 0, 0).astype(jnp.bfloat16)
        for t in range(tiles):
            parts[2 * k + 1, :, :, out_rows * t : out_rows * (t + 1), :] = part[
                :, 128 * t : 128 * (t + 1)
            ].reshape(planes, CORES, out_rows, 128)
        swap_part(2 * k + 1)

    def send_chip_sums(unit):
        landed(from_core.at[unit], part_recv.at[unit])
        chip_sums[unit] = (
            parts[unit, :, core].astype(jnp.float32) + from_core[unit].astype(jnp.float32)
        ).astype(jnp.bfloat16)
        for offset in range(1, planes):
            target = lax.rem(plane + offset, planes)
            if unit == 0:
                send_sum(unit, offset, target)
                continue
            ends = ((plane == 0) & (target == far)) | ((plane == far) & (target == 0))
            later = ((plane == 1) & (target == far)) | ((plane == far - 1) & (target == 0))

            @pl.when(jnp.logical_not(ends | later))
            def _():
                send_sum(unit, offset, target)

            @pl.when(ends)
            def _():
                side = jnp.where(plane == 0, 0, 1)
                relay = jnp.where(plane == 0, 1, far - 1)
                send(
                    chip_sums.at[unit, target],
                    relayed.at[unit, side],
                    sum_send.at[unit, offset - 1],
                    relay_recv.at[unit, side],
                    (me_s, relay * CORES + core),
                )

    def send_sum(unit, offset, target):
        send(
            chip_sums.at[unit, target],
            from_planes.at[unit, offset - 1],
            sum_send.at[unit, offset - 1],
            sum_recv.at[unit, offset - 1],
            (me_s, target * CORES + core),
        )

    def relay_sum(unit):
        for side, relay, target in ((0, 1, far), (1, far - 1, 0)):

            @pl.when(plane == relay)
            def _():
                landed(relayed.at[unit, side], relay_recv.at[unit, side])
                chip_sums[unit, target] = (
                    chip_sums[unit, target].astype(jnp.float32)
                    + relayed[unit, side].astype(jnp.float32)
                ).astype(jnp.bfloat16)
                send_sum(unit, (target - relay) % planes, target)

    def send_total(unit):
        k, kind = unit // 2, unit % 2
        total = chip_sums[unit, plane].astype(jnp.float32)
        for offset in range(1, planes):
            source = lax.rem(plane + planes - offset, planes)
            ends = ((plane == 0) & (source == far)) | ((plane == far) & (source == 0))
            direct = jnp.logical_not(ends) if unit > 0 else plane >= 0

            @pl.when(direct)
            def _():
                landed(from_planes.at[unit, offset - 1], sum_recv.at[unit, offset - 1])

            total = total + from_planes[unit, offset - 1].astype(jnp.float32)
        total = total.astype(jnp.bfloat16)
        totals[unit] = total
        own = owned.at[kind, me_s]

        @pl.when(me_s != k)
        def _():
            send(
                totals.at[unit], own, total_send.at[unit], total_recv.at[kind, me_s], (k, me_d)
            )

        @pl.when(me_s == k)
        def _():
            pltpu.make_async_copy(totals.at[unit], own, total_recv.at[kind, me_s]).start()

        grad_total = total.astype(jnp.float32)
        if kind == 0:
            grad_total = grad_total * gain_of[k].astype(jnp.float32)
        return jnp.sum((grad_total * grad_total).reshape(-1, 8, 128), axis=0)

    def units_of(k):
        units = [2 * k] + ([2 * k - 1] if k > 0 else [])
        return [2 * k + 1] + units if k == sections - 1 else units

    for k in range(sections):
        landed(gain_of.at[k], gain_recv.at[k])
    square = jnp.zeros((8, 128), jnp.float32)
    nothing = jnp.zeros((2 * sections - 1, in_rows, 128), jnp.bfloat16)

    @pl.when(plane == 0)
    def _():
        from_planes[1:, 0] = nothing

    @pl.when(plane == far)
    def _():
        from_planes[1:, far - 1] = nothing

    grad = cotangent_ref[...].astype(jnp.float32)
    for k in reversed(range(sections)):
        slot = sections - 1 - k
        pre_act = pre_acts[k]
        root = roots[k]
        squash = jax.nn.sigmoid(pre_act)
        grad_act = grad_partial * squash * (1.0 + pre_act * (1.0 - squash))
        act = grad_act.astype(jnp.bfloat16)
        copies = []
        if k > 0:
            column = root[:, :1]
            inner_mean = jnp.sum(grad_act * pre_act, axis=1, keepdims=True) / channels
            grad_normed = dot(act, weight_in(k), 1, 1)
            grad = grad + column * (
                grad_normed - streams[k].astype(jnp.float32) * (column * inner_mean)
            )
            grad_rounded = grad.astype(jnp.bfloat16)
            grad_partial = dot(grad_rounded, weight_out(k - 1), 1, 1)
            sent[slot, :tokens] = grad_partial.astype(jnp.bfloat16)
            copies = swap(slot, tokens)
        if k < sections - 1:
            for unit in units_of(k + 1):
                relay_sum(unit)
        else:
            make_out_part(k, cotangent_ref[...])
        make_in_part(k, grad_act)
        if k > 0:
            make_out_part(k - 1, grad_rounded)
        if k == 0 and sections > 2:
            for unit in units_of(k + 2):
                square = square + send_total(unit)
        for unit in units_of(k):
            send_chip_sums(unit)
        if 0 < k < sections - 2:
            for unit in units_of(k + 2):
                square = square + send_total(unit)
        for offset, copy in enumerate(copies):
            copy.wait_recv()
            grad_partial = grad_partial + received[slot, offset, :tokens].astype(jnp.float32)
    for k in (1, 0):
        for unit in units_of(k):
            square = square + send_total(unit)

    squares[0] = square
    copies = [
        remote(
            squares.at[0],
            squares_dp.at[offset - 1],
            dp_send.at[offset - 1],
            dp_recv.at[offset - 1],
            dp_peer(offset),
        )
        for offset in range(1, dp_count)
    ]
    out_parts = []
    for s in range(sections):
        landed(owned.at[1, s], total_recv.at[1, s])
        landed(owned.at[0, s], total_recv.at[0, s])
        own = slice(in_rows * s, in_rows * (s + 1))
        in_part = owned[0, s].astype(jnp.float32) * gain_rows[own]
        out_part = owned[1, s].astype(jnp.float32)
        grad_in_ref[own] = in_part
        out_parts.append(
            jnp.concatenate(
                [out_part[out_rows * t : out_rows * (t + 1)] for t in range(tiles)], axis=1
            )
        )
    grad_out_ref[...] = jnp.concatenate(
        [
            out_parts[s][:, in_rows * d : in_rows * (d + 1)]
            for d in range(dp_count)
            for s in range(sections)
        ],
        axis=1,
    )
    for offset, copy in enumerate(copies):
        copy.wait_recv()
        square = square + squares_dp[offset]
    squares[1] = square
    copies = [
        remote(
            squares.at[1],
            squares_section.at[offset - 1],
            section_send.at[offset - 1],
            section_recv.at[offset - 1],
            section_peer(offset),
        )
        for offset in range(1, sections)
    ]
    for offset, copy in enumerate(copies):
        copy.wait_recv()
        square = square + squares_section[offset]
    count_all = 2.0 * channels * rank * sections
    norm_total = jnp.sum(square, keepdims=True)
    factor = jnp.minimum(1.0, lax.rsqrt(norm_total / count_all + CLIP_EPS))
    factor_ref[...] = jnp.broadcast_to(factor, factor_ref.shape)

    for copy in started:
        copy.wait_send()
    for unit in range(2 * sections):
        for offset in range(1, planes):
            landed(chip_sums.at[unit, 0], sum_send.at[unit, offset - 1])
    for k in range(sections):
        for offset in range(1, planes):
            target = lax.rem(plane + offset, planes)

            @pl.when((target - plane != far) & (plane - target != far))
            def _():
                landed(weights.at[k, plane, core], rail_send.at[k, offset - 1])

        @pl.when(plane == far - 1)
        def _():
            landed(weights.at[k, 0, core], relay_send.at[k, 0])

        @pl.when(plane == 1)
        def _():
            landed(weights.at[k, far, core], relay_send.at[k, 1])

        @pl.when(me_s != k)
        def _():
            landed(totals.at[2 * k], total_send.at[2 * k])
            landed(totals.at[2 * k + 1], total_send.at[2 * k + 1])


def adam_kernel(*refs):
    inputs, outputs, loaded, results = refs[:9], refs[9:15], refs[15:24], refs[24:30]
    load_sems, store_sems = refs[30:]
    loads = [
        pltpu.make_async_copy(inputs[i], loaded[i], load_sems.at[i]) for i in range(len(inputs))
    ]
    for copy in loads:
        copy.start()
    stores = []
    loads[0].wait()
    factor = loaded[0][:1, :1]
    for place in (0, 1):
        for copy in loads[4 * place + 1 : 4 * place + 5]:
            copy.wait()
        grad, weight, moment, variance = loaded[4 * place + 1 : 4 * place + 5]
        updated = update(weight[0], grad[...], moment[0], variance[0], factor)
        for i, result in enumerate(updated, start=3 * place):
            results[i][...] = result
            copy = pltpu.make_async_copy(results[i], outputs[i], store_sems.at[i])
            copy.start()
            stores.append(copy)
    for copy in stores:
        copy.wait()


def fast_shards(
    stream_in,
    cotangent,
    norm_gain,
    weight_in,
    weight_out,
    moment_in,
    variance_in,
    moment_out,
    variance_out,
):
    sections = lax.axis_size("section")
    dp_count = lax.axis_size("dp")
    planes = dp_count // CORES
    channels = stream_in.shape[-1]
    tokens = stream_in.shape[0] * stream_in.shape[1]
    shard_rows, rank = weight_in.shape[1:]
    if tokens != rank:
        return shards(
            stream_in,
            cotangent,
            norm_gain,
            weight_in,
            weight_out,
            moment_in,
            variance_in,
            moment_out,
            variance_out,
        )
    out_rows = weight_out.shape[1]
    in_rows = shard_rows // sections
    width = channels // sections
    tiles = width // 128
    piece_rows = in_rows + out_rows * tiles

    narrow, full = jnp.bfloat16, jnp.float32
    slots = sections - 1
    chunks = HALVES * sections
    half = tokens // HALVES
    units = 2 * sections
    dma = pltpu.SemaphoreType.DMA
    vmem = pl.BlockSpec(memory_space=pltpu.VMEM)
    grad_w_in, grad_w_out, factor = pl.pallas_call(
        functools.partial(step_kernel, sections, planes),
        out_shape=(
            jax.ShapeDtypeStruct((shard_rows, rank), full),
            jax.ShapeDtypeStruct((out_rows, channels), full),
            jax.ShapeDtypeStruct((8, 128), full),
        ),
        in_specs=[pl.BlockSpec(memory_space=pl.ANY)] * 5,
        out_specs=(vmem, vmem, vmem),
        scratch_shapes=[
            pltpu.VMEM((2, tokens, channels), narrow),
            pltpu.VMEM((1, channels), narrow),
            pltpu.VMEM((shard_rows, rank), narrow),
            pltpu.VMEM((out_rows, channels), narrow),
            pltpu.VMEM((tokens, width), narrow),
            pltpu.VMEM((sections, piece_rows, 128), narrow),
            pltpu.VMEM((shard_rows, 128), full),
            pltpu.VMEM((sections, in_rows, 128), narrow),
            pltpu.VMEM((sections, in_rows, 128), narrow),
            pltpu.VMEM((sections, planes, CORES, piece_rows, 128), narrow),
            pltpu.VMEM((units, planes, CORES, in_rows, 128), narrow),
            pltpu.VMEM((units, planes, in_rows, 128), narrow),
            pltpu.VMEM((units, planes, in_rows, 128), narrow),
            pltpu.VMEM((units, planes - 1, in_rows, 128), narrow),
            pltpu.VMEM((units, 2, in_rows, 128), narrow),
            pltpu.VMEM((units, in_rows, 128), narrow),
            pltpu.VMEM((2, sections, in_rows, 128), narrow),
            pltpu.VMEM((sections, tokens, width), narrow),
            pltpu.VMEM((sections, tokens, rank), full),
            pltpu.VMEM((sections, tokens, tokens), full),
            pltpu.VMEM((sections, tokens, rank), narrow),
            pltpu.VMEM((slots, tokens, rank), narrow),
            pltpu.VMEM((slots, sections - 1, tokens, rank), narrow),
            pltpu.VMEM((chunks, 2 * half + 16, rank), narrow),
            pltpu.VMEM((chunks, sections - 1, 2 * half + 16, rank), narrow),
            pltpu.VMEM((2, 8, 128), full),
            pltpu.VMEM((dp_count - 1, 8, 128), full),
            pltpu.VMEM((sections - 1, 8, 128), full),
            dma((5,)),
            dma((sections - 1,)),
            dma((sections,)),
            dma((sections - 1,)),
            dma((sections,)),
            dma((sections, planes - 1)),
            dma((sections, 2)),
            dma((sections, planes)),
            dma((sections, planes, CORES)),
            dma((slots, sections - 1)),
            dma((slots, sections - 1)),
            dma((chunks, sections - 1)),
            dma((chunks, sections - 1)),
            dma((units,)),
            dma((units,)),
            dma((units, planes - 1)),
            dma((units, planes - 1)),
            dma((units, 2)),
            dma((units,)),
            dma((2, sections)),
            dma((dp_count - 1,)),
            dma((dp_count - 1,)),
            dma((sections - 1,)),
            dma((sections - 1,)),
        ],
        compiler_params=pltpu.CompilerParams(
            collective_id=0, has_side_effects=True, vmem_limit_bytes=60 * 1024 * 1024
        ),
    )(
        stream_in.reshape(tokens, channels),
        cotangent.reshape(tokens, channels),
        norm_gain,
        weight_in[0],
        weight_out[0],
    )
    in_shape = jax.ShapeDtypeStruct(moment_in.shape, full)
    out_shape = jax.ShapeDtypeStruct(moment_out.shape, full)
    arrays = (
        factor,
        grad_w_in,
        weight_in,
        moment_in,
        variance_in,
        grad_w_out,
        weight_out,
        moment_out,
        variance_out,
    )
    anywhere = pl.BlockSpec(memory_space=pl.ANY)
    return pl.pallas_call(
        adam_kernel,
        out_shape=(in_shape,) * 3 + (out_shape,) * 3,
        in_specs=[anywhere] * len(arrays),
        out_specs=(anywhere,) * 6,
        scratch_shapes=[
            *(pltpu.VMEM(array.shape, array.dtype) for array in arrays),
            *(pltpu.VMEM(shape.shape, full) for shape in (in_shape,) * 3 + (out_shape,) * 3),
            dma((len(arrays),)),
            dma((6,)),
        ],
        compiler_params=pltpu.CompilerParams(vmem_limit_bytes=60 * 1024 * 1024),
    )(*arrays)


def aligned(sections, dp_count):
    width, in_rows, out_rows = E // sections, E // (sections * dp_count), R // dp_count
    return (
        sections > 1
        and dp_count % CORES == 0
        and dp_count > 2 * CORES
        and width % 128 == 0
        and in_rows % 16 == 0
        and out_rows % 16 == 0
        and R == 128
        and E <= 128 * 128
        and E % (64 * dp_count) == 0
    )


def solution(mesh):
    fast = aligned(mesh.shape["section"], mesh.shape["dp"])
    return jax.shard_map(
        fast_shards if fast else shards,
        mesh=mesh,
        in_specs=(
            P(None, "dp", None),
            P(None, "dp", None),
            P("section", None),
            P("section", "dp", None),
            P("section", "dp", None),
            P("section", "dp", None),
            P("section", "dp", None),
            P("section", "dp", None),
            P("section", "dp", None),
        ),
        out_specs=(
            P("section", "dp", None),
            P("section", "dp", None),
            P("section", "dp", None),
            P("section", "dp", None),
            P("section", "dp", None),
            P("section", "dp", None),
        ),
        check_vma=False,
    )
```

```python
import functools

import jax
import jax.numpy as jnp
from jax import lax
from jax.experimental import pallas as pl
from jax.experimental.pallas import tpu as pltpu
from jax.sharding import PartitionSpec as P

E = 3584
R = 128


NORM_EPS = 1e-06
BETA_ONE = 0.9
BETA_TWO = 0.95
STEP_RATE = 0.01
ADAM_EPS = 1e-08
CLIP_EPS = 1e-06


def from_behind(x, axis, by):
    count = lax.axis_size(axis)
    pairs = [(i, i + by) for i in range(count) if 0 <= i + by < count]
    return lax.ppermute(x, axis, pairs)


def normalize(stream, gain):
    values = stream.astype(jnp.float32)
    inv_root = lax.rsqrt(jnp.mean(values * values, axis=-1, keepdims=True) + NORM_EPS)
    unit_rows = values * inv_root
    normed = (unit_rows * gain.astype(jnp.float32)).astype(jnp.bfloat16)
    return (values, inv_root, unit_rows, normed)


def section_forward(stream, gain, in_weight, out_weight):
    values, inv_root, unit_rows, normed = normalize(stream, gain)
    pre_act = jnp.dot(normed, in_weight, preferred_element_type=jnp.float32)
    hidden = (pre_act * jax.nn.sigmoid(pre_act)).astype(jnp.bfloat16)
    return (values + jnp.dot(hidden, out_weight, preferred_element_type=jnp.float32)).astype(
        jnp.bfloat16
    )


def section_backward(stream, grad_rows, gain, in_weight, out_weight):
    values, inv_root, unit_rows, normed = normalize(stream, gain)
    pre_act = jnp.dot(normed, in_weight, preferred_element_type=jnp.float32)
    squash = jax.nn.sigmoid(pre_act)
    hidden = (pre_act * squash).astype(jnp.bfloat16)
    grad_hidden = lax.dot_general(
        grad_rows, out_weight, (((1,), (1,)), ((), ())), preferred_element_type=jnp.float32
    )
    grad_act = (grad_hidden * squash * (1.0 + pre_act * (1.0 - squash))).astype(jnp.bfloat16)
    grad_normed = lax.dot_general(
        grad_act, in_weight, (((1,), (1,)), ((), ())), preferred_element_type=jnp.float32
    ) * gain.astype(jnp.float32)
    inner_mean = jnp.mean(grad_normed * unit_rows, axis=-1, keepdims=True)
    grad_in = (
        grad_rows.astype(jnp.float32) + inv_root * (grad_normed - unit_rows * inner_mean)
    ).astype(jnp.bfloat16)
    return (grad_in, normed, grad_act, hidden)


def contract_rows(left, right):
    return lax.dot_general(
        left, right, (((0,), (0,)), ((), ())), preferred_element_type=jnp.float32
    )


def forward_tick(step_tick, position, is_first, incoming, saved_rows, inputs, weights):
    batch_count = inputs.shape[0]
    chain_index = step_tick - position
    active = jnp.logical_and(chain_index >= 0, chain_index < batch_count)
    batch_slot = jnp.clip(chain_index, 0, batch_count - 1)
    stream = jnp.where(is_first, lax.dynamic_index_in_dim(inputs, batch_slot, 0, False), incoming)
    kept_row = jnp.where(active, stream, lax.dynamic_index_in_dim(saved_rows, batch_slot, 0, False))
    saved_rows = lax.dynamic_update_index_in_dim(saved_rows, kept_row, batch_slot, 0)
    section_out = lax.cond(
        active, lambda rows_in: section_forward(rows_in, *weights), jnp.zeros_like, stream
    )
    return (section_out, saved_rows)


def backward_tick(
    step_tick, position, is_last, incoming, saved_rows, targets, weights, grad_sums, groups
):
    batch_count = targets.shape[0]
    chain_index = step_tick - position
    active = jnp.logical_and(chain_index >= 0, chain_index < batch_count)
    batch_slot = jnp.clip(chain_index, 0, batch_count - 1)
    grad_rows = jnp.where(
        is_last, lax.dynamic_index_in_dim(targets, batch_slot, 0, False), incoming
    )
    stream = lax.dynamic_index_in_dim(saved_rows, batch_slot, 0, False)
    half_group = batch_slot * groups // batch_count

    def run_section(operands):
        rows_in, grad_now, sums_now = operands
        grad_in, normed, grad_act, hidden = section_backward(rows_in, grad_now, *weights)
        sum_in, sum_out = sums_now
        sum_in = lax.dynamic_update_index_in_dim(
            sum_in,
            lax.dynamic_index_in_dim(sum_in, half_group, 0, False)
            + contract_rows(normed, grad_act),
            half_group,
            0,
        )
        sum_out = lax.dynamic_update_index_in_dim(
            sum_out,
            lax.dynamic_index_in_dim(sum_out, half_group, 0, False)
            + contract_rows(hidden, grad_now),
            half_group,
            0,
        )
        return (grad_in, (sum_in, sum_out))

    def skip_section(operands):
        return (jnp.zeros_like(operands[1]), operands[2])

    return lax.cond(active, run_section, skip_section, (stream, grad_rows, grad_sums))


def update(weight, grad, moment, variance, factor):
    scaled = factor * grad
    moment = BETA_ONE * moment + (1.0 - BETA_ONE) * scaled
    variance = BETA_TWO * variance + (1.0 - BETA_TWO) * scaled * scaled
    weight = weight.astype(jnp.float32) - STEP_RATE * moment / (jnp.sqrt(variance) + ADAM_EPS)
    return (weight[None], moment[None], variance[None])


def shards(
    stream_in,
    cotangent,
    norm_gain,
    weight_in,
    weight_out,
    moment_in,
    variance_in,
    moment_out,
    variance_out,
):
    section_count = lax.axis_size("section")
    section_place = lax.axis_index("section")
    micro_count = stream_in.shape[0]
    in_slice = weight_in[0]
    out_slice = weight_out[0]
    full_in_shape = (in_slice.shape[0] * lax.axis_size("dp"), in_slice.shape[1])
    full_out_shape = (out_slice.shape[0] * lax.axis_size("dp"), out_slice.shape[1])
    empty_stream = jnp.zeros(stream_in.shape[1:], jnp.bfloat16)
    is_first = section_place == 0
    is_last = section_place == section_count - 1
    whole_in, whole_out = (
        lax.all_gather(in_slice, "dp", axis=0, tiled=True),
        lax.all_gather(out_slice, "dp", axis=0, tiled=True),
    )
    own_layer = (norm_gain[0], whole_in, whole_out)
    tick_count = micro_count + section_count - 1

    def run_forward(step_tick, loop_state):
        incoming, saved_rows = loop_state
        section_out, saved_rows = forward_tick(
            step_tick, section_place, is_first, incoming, saved_rows, stream_in, own_layer
        )
        return (from_behind(section_out, "section", 1), saved_rows)

    _, saved_rows = lax.fori_loop(
        0, tick_count, run_forward, (empty_stream, jnp.zeros_like(stream_in))
    )
    start_sums = (
        jnp.zeros((2,) + full_in_shape, jnp.float32),
        jnp.zeros((2,) + full_out_shape, jnp.float32),
    )

    def run_backward(step_tick, loop_state):
        incoming, grad_sums = loop_state
        grad_in, grad_sums = backward_tick(
            step_tick,
            section_count - 1 - section_place,
            is_last,
            incoming,
            saved_rows,
            cotangent,
            own_layer,
            grad_sums,
            2,
        )
        return (from_behind(grad_in, "section", -1), grad_sums)

    _, (stacked_in, stacked_out) = lax.fori_loop(
        0, tick_count, run_backward, (empty_stream, start_sums)
    )
    reduced_in, reduced_out = (
        lax.psum_scatter(
            stacked_in.astype(jnp.bfloat16), "dp", scatter_dimension=1, tiled=True
        ).astype(jnp.float32),
        lax.psum_scatter(
            stacked_out.astype(jnp.bfloat16), "dp", scatter_dimension=1, tiled=True
        ).astype(jnp.float32),
    )
    grad_w_in = reduced_in[0] + reduced_in[1]
    grad_w_out = reduced_out[0] + reduced_out[1]
    local_sum = jnp.sum(grad_w_in * grad_w_in) + jnp.sum(grad_w_out * grad_w_out)
    norm_total = lax.psum(local_sum, ("section", "dp"))
    count_all = 2.0 * E * R * section_count
    factor = jnp.minimum(1.0, lax.rsqrt(norm_total / count_all + CLIP_EPS))
    new_in, new_moment_in, new_variance_in = update(
        in_slice, grad_w_in, moment_in[0], variance_in[0], factor
    )
    new_out, new_moment_out, new_variance_out = update(
        out_slice, grad_w_out, moment_out[0], variance_out[0], factor
    )
    return (new_in, new_moment_in, new_variance_in, new_out, new_moment_out, new_variance_out)


MESH = pl.DeviceIdType.MESH
CORES = 2
HALVES = 2


def dot(left, right, left_dim, right_dim):
    return lax.dot_general(
        left, right, (((left_dim,), (right_dim,)), ((), ())), preferred_element_type=jnp.float32
    )


def step_kernel(
    sections,
    planes,
    stream_any,
    cotangent_any,
    gain_any,
    weight_in_any,
    weight_out_any,
    grad_in_ref,
    grad_out_ref,
    factor_ref,
    rows_ref,
    gain_ref,
    weight_in_ref,
    weight_out_ref,
    cotangent_ref,
    piece_ref,
    gain_rows,
    gain_sent,
    gain_of,
    weights,
    parts,
    from_core,
    chip_sums,
    from_planes,
    totals,
    owned,
    streams,
    pre_acts,
    roots,
    hiddens,
    sent,
    received,
    sent_halves,
    received_halves,
    squares,
    squares_dp,
    squares_section,
    load_sems,
    gain_send,
    gain_recv,
    piece_send,
    piece_recv,
    rail_send,
    relay_send,
    core_send,
    weight_recv,
    swap_send,
    swap_recv,
    half_send,
    half_recv,
    part_send,
    part_recv,
    sum_send,
    sum_recv,
    total_send,
    total_recv,
    dp_send,
    dp_recv,
    section_send,
    section_recv,
):
    me_s = lax.axis_index("section")
    me_d = lax.axis_index("dp")
    plane = me_d // CORES
    core = lax.rem(me_d, CORES)
    other = 1 - core
    dp_count = planes * CORES
    tokens, width = cotangent_ref.shape
    channels = width * sections
    shard_rows, rank = weight_in_ref.shape
    tiles = width // 128
    in_rows = shard_rows // sections
    out_rows = weight_out_ref.shape[0]

    def section_peer(offset):
        return (lax.rem(me_s + offset, sections), me_d)

    def dp_peer(offset):
        return (me_s, lax.rem(me_d + offset, dp_count))

    def plane_peer(offset):
        return (me_s, lax.rem(plane + offset, planes) * CORES + core)

    partner = (me_s, plane * CORES + other)

    def send(source, target, send_sem, recv_sem, device):
        copy = pltpu.make_async_remote_copy(
            src_ref=source,
            dst_ref=target,
            send_sem=send_sem,
            recv_sem=recv_sem,
            device_id=device,
            device_id_type=MESH,
        )
        copy.start()
        return copy

    def remote(*copy):
        started.append(send(*copy))
        return started[-1]

    def landed(target, sem):
        pltpu.make_async_copy(target, target, sem).wait()

    started = []
    loads = [
        pltpu.make_async_copy(source, target, load_sems.at[i])
        for i, (source, target) in enumerate(
            (
                (gain_any, gain_ref),
                (weight_out_any, weight_out_ref),
                (weight_in_any, weight_in_ref),
                (stream_any, rows_ref.at[0]),
                (cotangent_any, rows_ref.at[1]),
            )
        )
    ]
    for copy in loads:
        copy.start()
    barrier = pltpu.get_barrier_semaphore()
    for offset in range(1, sections):
        pl.semaphore_signal(barrier, inc=1, device_id=section_peer(offset), device_id_type=MESH)
    for offset in range(1, dp_count):
        pl.semaphore_signal(barrier, inc=1, device_id=dp_peer(offset), device_id_type=MESH)

    loads[0].wait()
    gain_row = gain_ref[...].astype(jnp.float32)
    gain_tiles = channels // 128
    gains = [gain_row[:, 128 * t : 128 * (t + 1)] for t in range(gain_tiles)]
    gains = jnp.concatenate(gains + [jnp.zeros((128 - gain_tiles, 128), jnp.float32)], axis=0)
    gains = jnp.transpose(gains)
    lanes = lax.broadcasted_iota(jnp.int32, (128, 128), 1)
    for b in range(shard_rows // 64):
        half = me_d * (shard_rows // 64) + b
        column = jnp.sum(jnp.where(lanes == half // 2, gains, 0.0), axis=1, keepdims=True)
        odd = jnp.full((64, 1), lax.rem(half, 2), jnp.int32) == 1
        gain_rows[64 * b : 64 * (b + 1)] = jnp.broadcast_to(
            jnp.where(odd, column[64:], column[:64]), (64, 128)
        )

    def own_channels(rows, s):
        cuts = [
            rows[:, shard_rows * d + in_rows * s : shard_rows * d + in_rows * (s + 1)]
            for d in range(dp_count)
        ]
        return jnp.concatenate(cuts, axis=1)

    loads[1].wait()
    loads[2].wait()
    shard_out = weight_out_ref[...].astype(jnp.float32)
    for s in range(sections):
        own = slice(in_rows * s, in_rows * (s + 1))
        piece_ref[s, :in_rows] = (
            weight_in_ref[own].astype(jnp.float32) * gain_rows[own]
        ).astype(jnp.bfloat16)
        cut = own_channels(shard_out, s).astype(jnp.bfloat16)
        for t in range(tiles):
            piece_ref[s, in_rows + out_rows * t : in_rows + out_rows * (t + 1)] = cut[
                :, 128 * t : 128 * (t + 1)
            ]
    pl.semaphore_wait(barrier, sections + dp_count - 2)

    for offset in range(1, sections):
        target = section_peer(offset)
        remote(
            piece_ref.at[target[0]],
            weights.at[me_s, plane, core],
            piece_send.at[offset - 1],
            piece_recv.at[me_s],
            target,
        )
    pltpu.make_async_copy(
        piece_ref.at[me_s], weights.at[me_s, plane, core], piece_recv.at[me_s]
    ).start()
    far = planes - 1
    for place in range(sections):
        k = me_s if place == 0 else jnp.where(place - 1 < me_s, place - 1, place)
        landed(weights.at[k, plane, core], piece_recv.at[k])
        piece = weights.at[k, plane, core]
        for offset in range(1, planes):
            target = lax.rem(plane + offset, planes)

            @pl.when((target - plane != far) & (plane - target != far))
            def _():
                send(
                    piece,
                    piece,
                    rail_send.at[k, offset - 1],
                    weight_recv.at[k, plane, core],
                    (me_s, target * CORES + core),
                )

        remote(piece, piece, core_send.at[k, 0], weight_recv.at[k, plane, core], partner)

    for s in range(sections):
        gain_sent[s] = gain_rows[in_rows * s : in_rows * (s + 1)].astype(jnp.bfloat16)
    for offset in range(1, sections):
        target = section_peer(offset)
        remote(
            gain_sent.at[target[0]],
            gain_of.at[me_s],
            gain_send.at[offset - 1],
            gain_recv.at[me_s],
            target,
        )
    pltpu.make_async_copy(gain_sent.at[me_s], gain_of.at[me_s], gain_recv.at[me_s]).start()

    def pass_on(k):
        for offset in range(1, planes):
            source = lax.rem(plane + offset, planes)
            piece = weights.at[k, source, core]
            landed(piece, weight_recv.at[k, source, core])

            @pl.when((source == 0) & (plane == far - 1))
            def _():
                send(
                    piece,
                    piece,
                    relay_send.at[k, 0],
                    weight_recv.at[k, source, core],
                    (me_s, far * CORES + core),
                )

            @pl.when((source == far) & (plane == 1))
            def _():
                send(
                    piece, piece, relay_send.at[k, 1], weight_recv.at[k, source, core], (me_s, core)
                )

            remote(
                piece, piece, core_send.at[k, offset], weight_recv.at[k, source, core], partner
            )

    def arrive(k):
        for source in range(planes):
            landed(weights.at[k, source, other], weight_recv.at[k, source, other])

    def weight_in(k):
        return weights[k, :, :, :in_rows, :].reshape(width, rank)

    def weight_out(k):
        columns = [
            weights[k, :, :, in_rows + out_rows * t : in_rows + out_rows * (t + 1), :].reshape(
                rank, 128
            )
            for t in range(tiles)
        ]
        return jnp.concatenate(columns, axis=1)

    def swap(slot, rows):
        return [
            remote(
                sent.at[slot, pl.ds(0, rows)],
                received.at[slot, offset - 1, pl.ds(0, rows)],
                swap_send.at[slot, offset - 1],
                swap_recv.at[slot, offset - 1],
                section_peer(offset),
            )
            for offset in range(1, sections)
        ]

    def spread(column):
        return jnp.transpose(jnp.broadcast_to(column, (tokens, tokens)))[:8]

    loads[3].wait()
    loads[4].wait()
    for s in range(sections):

        @pl.when(me_s == s)
        def _():
            streams[0] = own_channels(rows_ref[0].astype(jnp.float32), s).astype(jnp.bfloat16)
            cotangent_ref[...] = own_channels(rows_ref[1].astype(jnp.float32), s).astype(
                jnp.bfloat16
            )

    half = tokens // HALVES

    def forward_send(k, h):
        rows = slice(half * h, half * (h + 1))
        values = streams[k, rows]
        wide = values.astype(jnp.float32)
        partial = dot(values, weight_in(k), 1, 0)
        square = jnp.sum(wide * wide, axis=1, keepdims=True)
        square = spread(jnp.concatenate([square, jnp.zeros((tokens - half, 1), jnp.float32)], axis=0))
        square_hi = square.astype(jnp.bfloat16).astype(jnp.float32)
        sent_half = sent_halves.at[HALVES * k + h]
        sent_half[:half] = partial.astype(jnp.bfloat16)
        sent_half[half : half + 16] = jnp.concatenate(
            [square_hi, square - square_hi], axis=0
        ).astype(jnp.bfloat16)
        count = half + 16
        grad_part = None
        if k == sections - 1:
            grad_part = dot(cotangent_ref[rows], weight_out(k), 1, 1)
            sent_half[count : count + half] = grad_part.astype(jnp.bfloat16)
            count = count + half
        copies = [
            remote(
                sent_half.at[pl.ds(0, count)],
                received_halves.at[HALVES * k + h, offset - 1, pl.ds(0, count)],
                half_send.at[HALVES * k + h, offset - 1],
                half_recv.at[HALVES * k + h, offset - 1],
                section_peer(offset),
            )
            for offset in range(1, sections)
        ]
        return copies, partial, square, grad_part

    def forward_receive(k, h, state):
        rows = slice(half * h, half * (h + 1))
        copies, partial, square, grad_part = state
        for offset, copy in enumerate(copies):
            copy.wait_recv()
            count = half + 16 + (0 if grad_part is None else half)
            arrived = received_halves[HALVES * k + h, offset, :count].astype(jnp.float32)
            partial = partial + arrived[:half]
            square = square + arrived[half : half + 8] + arrived[half + 8 : half + 16]
            if grad_part is not None:
                grad_part = grad_part + arrived[half + 16 : half + 16 + half]
        mean = jnp.transpose(jnp.broadcast_to(square[:1], (tokens, tokens)))[:half] / channels
        root = lax.rsqrt(mean + NORM_EPS)
        pre_act = partial * root[:, :rank]
        hidden = (pre_act * jax.nn.sigmoid(pre_act)).astype(jnp.bfloat16)
        pre_acts[k, rows] = pre_act
        roots[k, rows] = root
        hiddens[k, rows] = hidden
        if k < sections - 1:
            streams[k + 1, rows] = (
                streams[k, rows].astype(jnp.float32) + dot(hidden, weight_out(k), 1, 0)
            ).astype(jnp.bfloat16)
        return grad_part

    pass_on(0)
    arrive(0)
    states = [forward_send(0, h) for h in range(HALVES)]
    for k in range(1, sections):
        pass_on(k)
        for h in range(HALVES):
            forward_receive(k - 1, h, states[h])
            if h == 0:
                arrive(k)
            states[h] = forward_send(k, h)
    grad_partial = jnp.concatenate(
        [forward_receive(sections - 1, h, states[h]) for h in range(HALVES)], axis=0
    )

    def swap_part(unit):
        remote(
            parts.at[unit, :, other],
            from_core.at[unit],
            part_send.at[unit],
            part_recv.at[unit],
            partner,
        )

    def make_in_part(k, grad_act):
        scaled = (grad_act * roots[k][:, :rank]).astype(jnp.bfloat16)
        part = dot(streams[k], scaled, 0, 0).astype(jnp.bfloat16)
        parts[2 * k] = part.reshape(planes, CORES, in_rows, rank)
        swap_part(2 * k)

    def make_out_part(k, grad_rounded):
        part = dot(hiddens[k], grad_rounded, 0, 0).astype(jnp.bfloat16)
        for t in range(tiles):
            parts[2 * k + 1, :, :, out_rows * t : out_rows * (t + 1), :] = part[
                :, 128 * t : 128 * (t + 1)
            ].reshape(planes, CORES, out_rows, 128)
        swap_part(2 * k + 1)

    def send_chip_sums(unit):
        landed(from_core.at[unit], part_recv.at[unit])
        chip_sums[unit] = (
            parts[unit, :, core].astype(jnp.float32) + from_core[unit].astype(jnp.float32)
        ).astype(jnp.bfloat16)
        for offset in range(1, planes):
            remote(
                chip_sums.at[unit, lax.rem(plane + offset, planes)],
                from_planes.at[unit, offset - 1],
                sum_send.at[unit, offset - 1],
                sum_recv.at[unit, offset - 1],
                plane_peer(offset),
            )

    def send_total(unit):
        k, kind = unit // 2, unit % 2
        total = chip_sums[unit, plane].astype(jnp.float32)
        for offset in range(1, planes):
            landed(from_planes.at[unit, offset - 1], sum_recv.at[unit, offset - 1])
            total = total + from_planes[unit, offset - 1].astype(jnp.float32)
        total = total.astype(jnp.bfloat16)
        totals[unit] = total
        own = owned.at[kind, me_s]

        @pl.when(me_s != k)
        def _():
            send(
                totals.at[unit], own, total_send.at[unit], total_recv.at[kind, me_s], (k, me_d)
            )

        @pl.when(me_s == k)
        def _():
            pltpu.make_async_copy(totals.at[unit], own, total_recv.at[kind, me_s]).start()

        grad_total = total.astype(jnp.float32)
        if kind == 0:
            grad_total = grad_total * gain_of[k].astype(jnp.float32)
        return jnp.sum((grad_total * grad_total).reshape(-1, 8, 128), axis=0)

    def units_of(k):
        units = [2 * k] + ([2 * k - 1] if k > 0 else [])
        return [2 * k + 1] + units if k == sections - 1 else units

    for k in range(sections):
        landed(gain_of.at[k], gain_recv.at[k])
    square = jnp.zeros((8, 128), jnp.float32)
    grad = cotangent_ref[...].astype(jnp.float32)
    for k in reversed(range(sections)):
        slot = sections - 1 - k
        pre_act = pre_acts[k]
        root = roots[k]
        squash = jax.nn.sigmoid(pre_act)
        grad_act = grad_partial * squash * (1.0 + pre_act * (1.0 - squash))
        act = grad_act.astype(jnp.bfloat16)
        copies = []
        if k > 0:
            column = root[:, :1]
            inner_mean = jnp.sum(grad_act * pre_act, axis=1, keepdims=True) / channels
            grad_normed = dot(act, weight_in(k), 1, 1)
            grad = grad + column * (
                grad_normed - streams[k].astype(jnp.float32) * (column * inner_mean)
            )
            grad_rounded = grad.astype(jnp.bfloat16)
            grad_partial = dot(grad_rounded, weight_out(k - 1), 1, 1)
            sent[slot, :tokens] = grad_partial.astype(jnp.bfloat16)
            copies = swap(slot, tokens)
        if 0 < k < sections - 1:
            for unit in units_of(k + 1):
                send_chip_sums(unit)
        if k == sections - 1:
            make_out_part(k, cotangent_ref[...])
        make_in_part(k, grad_act)
        if k > 0:
            make_out_part(k - 1, grad_rounded)
        else:
            for unit in units_of(1):
                send_chip_sums(unit)
            if sections > 2:
                for unit in units_of(2):
                    square = square + send_total(unit)
            send_chip_sums(0)
        if 0 < k < sections - 2:
            for unit in units_of(k + 2):
                square = square + send_total(unit)
        for offset, copy in enumerate(copies):
            copy.wait_recv()
            grad_partial = grad_partial + received[slot, offset, :tokens].astype(jnp.float32)
    for k in (1, 0):
        for unit in units_of(k):
            square = square + send_total(unit)

    squares[0] = square
    copies = [
        remote(
            squares.at[0],
            squares_dp.at[offset - 1],
            dp_send.at[offset - 1],
            dp_recv.at[offset - 1],
            dp_peer(offset),
        )
        for offset in range(1, dp_count)
    ]
    out_parts = []
    for s in range(sections):
        landed(owned.at[1, s], total_recv.at[1, s])
        landed(owned.at[0, s], total_recv.at[0, s])
        own = slice(in_rows * s, in_rows * (s + 1))
        in_part = owned[0, s].astype(jnp.float32) * gain_rows[own]
        out_part = owned[1, s].astype(jnp.float32)
        grad_in_ref[own] = in_part
        out_parts.append(
            jnp.concatenate(
                [out_part[out_rows * t : out_rows * (t + 1)] for t in range(tiles)], axis=1
            )
        )
    grad_out_ref[...] = jnp.concatenate(
        [
            out_parts[s][:, in_rows * d : in_rows * (d + 1)]
            for d in range(dp_count)
            for s in range(sections)
        ],
        axis=1,
    )
    for offset, copy in enumerate(copies):
        copy.wait_recv()
        square = square + squares_dp[offset]
    squares[1] = square
    copies = [
        remote(
            squares.at[1],
            squares_section.at[offset - 1],
            section_send.at[offset - 1],
            section_recv.at[offset - 1],
            section_peer(offset),
        )
        for offset in range(1, sections)
    ]
    for offset, copy in enumerate(copies):
        copy.wait_recv()
        square = square + squares_section[offset]
    count_all = 2.0 * channels * rank * sections
    norm_total = jnp.sum(square, keepdims=True)
    factor = jnp.minimum(1.0, lax.rsqrt(norm_total / count_all + CLIP_EPS))
    factor_ref[...] = jnp.broadcast_to(factor, factor_ref.shape)

    for copy in started:
        copy.wait_send()
    for k in range(sections):
        for offset in range(1, planes):
            target = lax.rem(plane + offset, planes)

            @pl.when((target - plane != far) & (plane - target != far))
            def _():
                landed(weights.at[k, plane, core], rail_send.at[k, offset - 1])

        @pl.when(plane == far - 1)
        def _():
            landed(weights.at[k, 0, core], relay_send.at[k, 0])

        @pl.when(plane == 1)
        def _():
            landed(weights.at[k, far, core], relay_send.at[k, 1])

        @pl.when(me_s != k)
        def _():
            landed(totals.at[2 * k], total_send.at[2 * k])
            landed(totals.at[2 * k + 1], total_send.at[2 * k + 1])


def adam_kernel(*refs):
    inputs, outputs, loaded, results = refs[:9], refs[9:15], refs[15:24], refs[24:30]
    load_sems, store_sems = refs[30:]
    loads = [
        pltpu.make_async_copy(inputs[i], loaded[i], load_sems.at[i]) for i in range(len(inputs))
    ]
    for copy in loads:
        copy.start()
    stores = []
    loads[0].wait()
    factor = loaded[0][:1, :1]
    for place in (0, 1):
        for copy in loads[4 * place + 1 : 4 * place + 5]:
            copy.wait()
        grad, weight, moment, variance = loaded[4 * place + 1 : 4 * place + 5]
        updated = update(weight[0], grad[...], moment[0], variance[0], factor)
        for i, result in enumerate(updated, start=3 * place):
            results[i][...] = result
            copy = pltpu.make_async_copy(results[i], outputs[i], store_sems.at[i])
            copy.start()
            stores.append(copy)
    for copy in stores:
        copy.wait()


def fast_shards(
    stream_in,
    cotangent,
    norm_gain,
    weight_in,
    weight_out,
    moment_in,
    variance_in,
    moment_out,
    variance_out,
):
    sections = lax.axis_size("section")
    dp_count = lax.axis_size("dp")
    planes = dp_count // CORES
    channels = stream_in.shape[-1]
    tokens = stream_in.shape[0] * stream_in.shape[1]
    shard_rows, rank = weight_in.shape[1:]
    if tokens != rank:
        return shards(
            stream_in,
            cotangent,
            norm_gain,
            weight_in,
            weight_out,
            moment_in,
            variance_in,
            moment_out,
            variance_out,
        )
    out_rows = weight_out.shape[1]
    in_rows = shard_rows // sections
    width = channels // sections
    tiles = width // 128
    piece_rows = in_rows + out_rows * tiles

    narrow, full = jnp.bfloat16, jnp.float32
    slots = sections - 1
    chunks = HALVES * sections
    half = tokens // HALVES
    units = 2 * sections
    dma = pltpu.SemaphoreType.DMA
    vmem = pl.BlockSpec(memory_space=pltpu.VMEM)
    grad_w_in, grad_w_out, factor = pl.pallas_call(
        functools.partial(step_kernel, sections, planes),
        out_shape=(
            jax.ShapeDtypeStruct((shard_rows, rank), full),
            jax.ShapeDtypeStruct((out_rows, channels), full),
            jax.ShapeDtypeStruct((8, 128), full),
        ),
        in_specs=[pl.BlockSpec(memory_space=pl.ANY)] * 5,
        out_specs=(vmem, vmem, vmem),
        scratch_shapes=[
            pltpu.VMEM((2, tokens, channels), narrow),
            pltpu.VMEM((1, channels), narrow),
            pltpu.VMEM((shard_rows, rank), narrow),
            pltpu.VMEM((out_rows, channels), narrow),
            pltpu.VMEM((tokens, width), narrow),
            pltpu.VMEM((sections, piece_rows, 128), narrow),
            pltpu.VMEM((shard_rows, 128), full),
            pltpu.VMEM((sections, in_rows, 128), narrow),
            pltpu.VMEM((sections, in_rows, 128), narrow),
            pltpu.VMEM((sections, planes, CORES, piece_rows, 128), narrow),
            pltpu.VMEM((units, planes, CORES, in_rows, 128), narrow),
            pltpu.VMEM((units, planes, in_rows, 128), narrow),
            pltpu.VMEM((units, planes, in_rows, 128), narrow),
            pltpu.VMEM((units, planes - 1, in_rows, 128), narrow),
            pltpu.VMEM((units, in_rows, 128), narrow),
            pltpu.VMEM((2, sections, in_rows, 128), narrow),
            pltpu.VMEM((sections, tokens, width), narrow),
            pltpu.VMEM((sections, tokens, rank), full),
            pltpu.VMEM((sections, tokens, tokens), full),
            pltpu.VMEM((sections, tokens, rank), narrow),
            pltpu.VMEM((slots, tokens, rank), narrow),
            pltpu.VMEM((slots, sections - 1, tokens, rank), narrow),
            pltpu.VMEM((chunks, 2 * half + 16, rank), narrow),
            pltpu.VMEM((chunks, sections - 1, 2 * half + 16, rank), narrow),
            pltpu.VMEM((2, 8, 128), full),
            pltpu.VMEM((dp_count - 1, 8, 128), full),
            pltpu.VMEM((sections - 1, 8, 128), full),
            dma((5,)),
            dma((sections - 1,)),
            dma((sections,)),
            dma((sections - 1,)),
            dma((sections,)),
            dma((sections, planes - 1)),
            dma((sections, 2)),
            dma((sections, planes)),
            dma((sections, planes, CORES)),
            dma((slots, sections - 1)),
            dma((slots, sections - 1)),
            dma((chunks, sections - 1)),
            dma((chunks, sections - 1)),
            dma((units,)),
            dma((units,)),
            dma((units, planes - 1)),
            dma((units, planes - 1)),
            dma((units,)),
            dma((2, sections)),
            dma((dp_count - 1,)),
            dma((dp_count - 1,)),
            dma((sections - 1,)),
            dma((sections - 1,)),
        ],
        compiler_params=pltpu.CompilerParams(
            collective_id=0, has_side_effects=True, vmem_limit_bytes=60 * 1024 * 1024
        ),
    )(
        stream_in.reshape(tokens, channels),
        cotangent.reshape(tokens, channels),
        norm_gain,
        weight_in[0],
        weight_out[0],
    )
    in_shape = jax.ShapeDtypeStruct(moment_in.shape, full)
    out_shape = jax.ShapeDtypeStruct(moment_out.shape, full)
    arrays = (
        factor,
        grad_w_in,
        weight_in,
        moment_in,
        variance_in,
        grad_w_out,
        weight_out,
        moment_out,
        variance_out,
    )
    anywhere = pl.BlockSpec(memory_space=pl.ANY)
    return pl.pallas_call(
        adam_kernel,
        out_shape=(in_shape,) * 3 + (out_shape,) * 3,
        in_specs=[anywhere] * len(arrays),
        out_specs=(anywhere,) * 6,
        scratch_shapes=[
            *(pltpu.VMEM(array.shape, array.dtype) for array in arrays),
            *(pltpu.VMEM(shape.shape, full) for shape in (in_shape,) * 3 + (out_shape,) * 3),
            dma((len(arrays),)),
            dma((6,)),
        ],
        compiler_params=pltpu.CompilerParams(vmem_limit_bytes=60 * 1024 * 1024),
    )(*arrays)


def aligned(sections, dp_count):
    width, in_rows, out_rows = E // sections, E // (sections * dp_count), R // dp_count
    return (
        sections > 1
        and dp_count % CORES == 0
        and dp_count > 2 * CORES
        and width % 128 == 0
        and in_rows % 16 == 0
        and out_rows % 16 == 0
        and R == 128
        and E <= 128 * 128
        and E % (64 * dp_count) == 0
    )


def solution(mesh):
    fast = aligned(mesh.shape["section"], mesh.shape["dp"])
    return jax.shard_map(
        fast_shards if fast else shards,
        mesh=mesh,
        in_specs=(
            P(None, "dp", None),
            P(None, "dp", None),
            P("section", None),
            P("section", "dp", None),
            P("section", "dp", None),
            P("section", "dp", None),
            P("section", "dp", None),
            P("section", "dp", None),
            P("section", "dp", None),
        ),
        out_specs=(
            P("section", "dp", None),
            P("section", "dp", None),
            P("section", "dp", None),
            P("section", "dp", None),
            P("section", "dp", None),
            P("section", "dp", None),
        ),
        check_vma=False,
    )
```
